256 devices in a mesh: blk: 64 (over z, x, core), emit: 4 (over y).
Axes of the slice: x: 4, y: 4, z: 8, core: 2. Of those that a mesh axis runs over, the one named last changes fastest.
Arguments:
- loglike: bfloat16 [8, 32, 4096], P(None, None, 'emit'), may hold values from -74 to -14
- start_weights: float32 [32, 262144], P('emit', 'blk'), may hold values from 0.1 to 36
- self_trans: bfloat16 [512, 512, 512], P('blk'), may hold values from 9.5703125e-05 to 2.5
- entry_trans: bfloat16 [512, 512, 512], P('blk'), may hold values from 9.5703125e-05 to 2.5
- arc_weight: bfloat16 [512, 8], P('blk'), may hold values from 0.049 to 1
- arc_src: int32 [512, 8], P('blk'), may hold values from 0 to 511, as said below
- send_ids: int32 [8, 64, 64, 1], P(None, 'blk'), may hold values from 0 to 8, as said below
- state_senone: int32 [262144], P('blk'), may hold values from 0 to 4095
Outputs:
- forward_out: float32 [32, 262144], P('emit', 'blk')
- log_like: float32 [32], P('emit')
The draws below stay inside these ranges and needn't reach their ends.
Inputs may be any that keep to these rules, and one draw needn't show every extreme that they name: `arc_src`: the 64 arcs into the blocks of one index of blk come 1 from each index of blk, from distinct blocks of it. `send_ids`: each list holds distinct local block numbers below 8 or the pad value 8; a listed block is the source of an arc into the receiving index's blocks.
All inputs are finite; a program needn't handle non-finite values.
Results may differ from the reference program's by a relative error of at most 0.0032.
The reference program's roundings to bfloat16 on the way count: a program that leaves them out, or rounds other values in their place, can miss the bound.
Values may be sent and summed in bfloat16 or wider, within the bound.
No kernel may reach another device: no remote copies, remote signals or barrier semaphores. Data moves between devices by JAX's collectives and lax.ppermute only.
A program may use at most 128 MiB of HBM per device.

```python
import math
import jax
import jax.numpy as jnp
from jax import lax

BS = 512
S = 4096
A_IN = 8
F = 8
BLK_DEV = 8
NB = 512
STATES = 262144
UTTS = 32
CAP = 1
N_BLK = 64


def arc_plan(key):
    arc_count = BLK_DEV * A_IN
    stride = BLK_DEV // CAP
    subkeys = jax.random.split(jax.random.fold_in(key, 11), N_BLK)

    def permute(subkey):
        return jax.random.permutation(subkey, arc_count)
    orders = jax.vmap(permute)(subkeys).astype(jnp.int32)
    offset = jax.random.randint(jax.random.fold_in(key, 12), (N_BLK, arc_count), 0, stride, dtype=jnp.int32)
    sender = orders // CAP
    local_id = orders % CAP * stride + offset
    return (orders, sender, local_id)


def draw_arc_src(key, part):
    orders, sender, local_id = arc_plan(key)
    return (sender * BLK_DEV + local_id).reshape(NB, A_IN).astype(jnp.int32)


def draw_send_ids(key, part):
    orders, sender, local_id = arc_plan(key)
    key = jax.random.fold_in(key, 3)
    row_index = jnp.arange(N_BLK, dtype=jnp.int32)[:, None]
    slot_table = jnp.zeros((N_BLK, N_BLK * CAP), jnp.int32).at[row_index, orders].set(local_id)
    slot_table = slot_table.reshape(N_BLK, N_BLK, CAP).transpose(1, 0, 2)
    living = jax.random.randint(key, (F, NB), 0, 4, dtype=jnp.int32) > 0
    source = jnp.arange(N_BLK, dtype=jnp.int32)[:, None, None] * BLK_DEV + slot_table
    alive_here = living[:, source]
    return jnp.where(alive_here, slot_table[None], BLK_DEV).astype(jnp.int32)


def draw_start_weights(key, part):
    key = jax.random.fold_in(key, 5)
    rising = jnp.arange(STATES, dtype=jnp.float32) / (STATES - 1)
    spread_base = jnp.exp(jax.random.uniform(key, (UTTS, STATES), jnp.float32, math.log(0.1), math.log(3.0)))
    return spread_base * (1.0 + 2.0 * rising)


def draw_loglike(key, part):
    key = jax.random.fold_in(key, 7)
    level_key = jax.random.fold_in(key, 1)
    noise_key = jax.random.fold_in(key, 2)
    level = jax.random.uniform(level_key, (F, UTTS, 1), jnp.float32, -66.0, -22.0)
    noise = jnp.clip(jax.random.normal(noise_key, (F, UTTS, S), jnp.float32), -4.0, 4.0)
    return (level + noise).astype(jnp.bfloat16)


def transition_blocks(key, diag_low, diag_high):
    off_key = jax.random.fold_in(key, 1)
    diag_key = jax.random.fold_in(key, 2)
    spread = jnp.exp(jax.random.uniform(off_key, (NB, BS, BS), jnp.float32, math.log(0.05), math.log(5.0))) / BS
    diagonal_part = jnp.exp(jax.random.uniform(diag_key, (NB, 1, BS), jnp.float32, math.log(diag_low), math.log(diag_high)))
    on_diag = jnp.arange(BS)[:, None] == jnp.arange(BS)[None, :]
    return jnp.where(on_diag[None], diagonal_part, spread)


def draw_self_trans(key, part):
    key = jax.random.fold_in(key, 13)
    return transition_blocks(key, 0.5, 2.5).astype(jnp.bfloat16)


def draw_entry_trans(key, part):
    key = jax.random.fold_in(key, 17)
    return transition_blocks(key, 0.5, 2.5).astype(jnp.bfloat16)


def draw_arc_weight(key, part):
    key = jax.random.fold_in(key, 19)
    return jnp.exp(jax.random.uniform(key, (NB, A_IN), jnp.float32, math.log(0.05), math.log(1.0))).astype(jnp.bfloat16)


def with_ends(values, rng, least, top_value):
    spot = [jax.random.randint(jax.random.fold_in(rng, axis), (), 0, length) for axis, length in enumerate(values.shape)]
    longest = values.shape.index(max(values.shape))
    next_to = spot[:longest] + [(spot[longest] + 1) % values.shape[longest]] + spot[longest + 1:]
    return values.at[tuple(spot)].set(least).at[tuple(next_to)].set(top_value)


def setup_inputs(seed: int = 0) -> dict:
    keys = jax.random.split(jax.random.key(seed), 9)
    return {
        "loglike": draw_loglike(jax.random.fold_in(keys[8], 71), 0),
        "start_weights": draw_start_weights(jax.random.fold_in(keys[8], 71), 0),
        "self_trans": draw_self_trans(jax.random.fold_in(keys[8], 71), 0),
        "entry_trans": draw_entry_trans(jax.random.fold_in(keys[8], 71), 0),
        "arc_weight": draw_arc_weight(jax.random.fold_in(keys[8], 71), 0),
        "arc_src": draw_arc_src(jax.random.fold_in(keys[8], 71), 0),
        "send_ids": draw_send_ids(jax.random.fold_in(keys[8], 71), 0),
        "state_senone": with_ends(jax.random.randint(keys[7], (STATES,), 0, S), jax.random.fold_in(keys[7], 1), 0, S - 1).astype(jnp.int32),
    }


def reference(loglike, start_weights, self_trans, entry_trans, arc_weight, arc_src, send_ids, state_senone):
    src_owner = arc_src // BLK_DEV
    src_local = arc_src % BLK_DEV
    dst_owner = (jnp.arange(NB, dtype=jnp.int32) // BLK_DEV)[:, None]
    forward = start_weights.reshape(UTTS, NB, BS).transpose(1, 0, 2)
    log_like = jnp.zeros((UTTS,), jnp.float32)
    for frame_no in range(F):
        sent_vals = lax.optimization_barrier(forward.astype(jnp.bfloat16))
        lists = send_ids[frame_no][src_owner, dst_owner]
        present = jnp.any(lists == src_local[:, :, None], axis=2)
        weights = jnp.where(present, arc_weight.astype(jnp.float32), jnp.float32(0.0))
        emission = jnp.exp(jnp.take(loglike[frame_no].astype(jnp.float32), state_senone, axis=1))
        emission = emission.reshape(UTTS, NB, BS).transpose(1, 0, 2)

        def one_block(packed):
            sources, arc_wts, self_mat, entry_mat, own_vals, emis_vals = packed
            picked = sent_vals[sources].astype(jnp.float32)
            inflow = jnp.sum(arc_wts[:, None, None] * picked, axis=0).astype(jnp.bfloat16)
            raw_mass = jnp.dot(own_vals, self_mat, preferred_element_type=jnp.float32)
            raw_mass = raw_mass + jnp.dot(inflow, entry_mat, preferred_element_type=jnp.float32)
            return raw_mass * emis_vals

        raw_mass = lax.map(one_block, (arc_src, weights, self_trans, entry_trans, sent_vals, emission))
        mass_sum = jnp.sum(raw_mass, axis=(0, 2))
        forward = raw_mass * (STATES / mass_sum)[None, :, None]
        log_like = log_like + jnp.log(mass_sum / STATES)
    return forward.transpose(1, 0, 2).reshape(UTTS, STATES), log_like
```

```python
import functools

import jax
import jax.numpy as jnp
from jax import lax
from jax.experimental import pallas as pl
from jax.experimental.pallas import tpu as pltpu
from jax.sharding import PartitionSpec as P

LANES = 128
TOP, BIAS, RATIO, TINY = 65535.0, 32768.0, 2.0**-22, 1e-30
META, PEAK_STEPS = 16, 256.0
MEAN_LOW, MEAN_HIGH = 2.0**-4, 4095.0
VMEM_LIMIT = 48 * 2**20


def exchange(outgoing):
    return lax.all_to_all(outgoing, "blk", split_axis=0, concat_axis=0, tiled=True)


def sum_over_blk(part):
    n_blk = lax.axis_size("blk")
    return jnp.sum(exchange(jnp.broadcast_to(part[None], (n_blk,) + part.shape)), axis=0)


def advance(values, matrices):
    return jnp.einsum("juv,jvw->juw", values, matrices, preferred_element_type=jnp.float32)


def normalised_path(start, rows, self_trans, entry_trans, arc_weight, arc_src, slots, state_senone):
    utt_dev, n_blk = start.shape[0], lax.axis_size("blk")
    blk_dev, block_width = self_trans.shape[:2]
    state_count = blk_dev * block_width * n_blk
    senders = lax.broadcasted_iota(jnp.int32, (1, 1, n_blk), 2)
    arc_values = jnp.where(
        (arc_src // blk_dev)[:, :, None] == senders, arc_weight[:, :, None].astype(jnp.float32), 0.0
    )
    mixing = jnp.sum(arc_values, axis=1).astype(jnp.bfloat16)

    def blocks(values):
        return values.reshape(utt_dev, blk_dev, block_width).transpose(1, 0, 2)

    def frame(frame_no, carry):
        forward, log_like = carry
        sent = forward.astype(jnp.bfloat16)
        padded = jnp.concatenate([sent, jnp.zeros_like(sent[:1])], axis=0)
        outgoing = padded.at[slots[frame_no]].get(mode="promise_in_bounds")
        incoming = exchange(outgoing).reshape(n_blk, utt_dev * block_width)
        inflow = jnp.dot(mixing, incoming, preferred_element_type=jnp.float32)
        inflow = inflow.astype(jnp.bfloat16).reshape(blk_dev, utt_dev, block_width)
        raw_mass = advance(sent, self_trans) + advance(inflow, entry_trans)
        scores = rows[frame_no].at[:, state_senone].get(mode="promise_in_bounds")
        raw_mass = raw_mass * jnp.exp(blocks(scores).astype(jnp.float32))
        mass_sum = sum_over_blk(jnp.sum(raw_mass, axis=(0, 2)))
        forward = raw_mass * (state_count / mass_sum)[None, :, None]
        return forward, log_like + jnp.log(mass_sum / state_count)

    log_like = jnp.zeros((utt_dev,), jnp.float32)
    forward, log_like = lax.fori_loop(0, rows.shape[0], frame, (blocks(start), log_like))
    return forward.transpose(1, 0, 2).reshape(start.shape), log_like


def encode(blocks, mean, core, out_ref):
    utts, width = blocks[0].shape
    lane = lax.broadcasted_iota(jnp.int32, (utts, LANES), 1) - core * META
    meta = jnp.zeros((utts, LANES), jnp.float32)
    bad = jnp.where((mean >= MEAN_LOW) & (mean <= MEAN_HIGH), 0.0, 1.0)
    for d, block in enumerate(blocks):
        peak = jnp.max(block, axis=1, keepdims=True)
        least = jnp.min(block, axis=1, keepdims=True)
        bad = jnp.where((least >= peak * RATIO) & (least >= TINY), bad, 1.0)
        steps = jnp.ceil(jnp.log2(peak) * PEAK_STEPS)
        share = block * jnp.exp2(steps * (-1.0 / PEAK_STEPS))
        root = jnp.exp2(jnp.log2(share) * (1.0 / 3.0))
        code = jnp.clip(jnp.round(root * TOP), 0.0, TOP) - BIAS
        out_ref[:, d * width : (d + 1) * width] = code
        meta = jnp.where(lane == d, steps, meta)
    n = len(blocks)
    out_ref[:, n * width : (n + 1) * width] = jnp.full((utts, width), -BIAS, jnp.float32)
    rest = mean * 8.0
    for digit in range(3):
        whole = jnp.floor(rest)
        meta = jnp.where(lane == n + digit, whole, meta)
        rest = (rest - whole) * 2.0**15
    out_ref[:, (n + 1) * width :] = meta
    return jnp.broadcast_to(bad, (utts, LANES))


def encode_kernel(blk_dev, core_ref, start_ref, out_ref):
    width = start_ref.shape[1] // blk_dev
    blocks = [
        start_ref[:, d * width : (d + 1) * width].astype(jnp.bfloat16).astype(jnp.float32)
        for d in range(blk_dev)
    ]
    encode(blocks, jnp.ones((start_ref.shape[0], 1), jnp.float32), core_ref[0], out_ref)


def encode_start(blk_dev, core, start):
    utts, states = start.shape
    return pl.pallas_call(
        functools.partial(encode_kernel, blk_dev),
        out_shape=jax.ShapeDtypeStruct((utts, states + states // blk_dev + LANES), jnp.float32),
        in_specs=[pl.BlockSpec(memory_space=pltpu.SMEM), pl.BlockSpec(memory_space=pltpu.VMEM)],
        out_specs=pl.BlockSpec(memory_space=pltpu.VMEM),
        compiler_params=pltpu.CompilerParams(vmem_limit_bytes=VMEM_LIMIT),
        name="encode",
    )(core, start)


def pack_kernel(width, core_ref, mine_ref, others_ref, own_ref, other_ref, out_ref):
    mine_at = pl.multiple_of(core_ref[0] * width, width)
    others_at = pl.multiple_of((1 - core_ref[0]) * width, width)
    meta = own_ref[:, own_ref.shape[1] - LANES :] + other_ref[:, own_ref.shape[1] - LANES :]
    for chip in range(out_ref.shape[0]):
        mine = pl.multiple_of(mine_ref[chip] * width, width)
        others = pl.multiple_of(others_ref[chip] * width, width)
        out_ref[chip, :, pl.ds(mine_at, width)] = own_ref[:, pl.ds(mine, width)]
        out_ref[chip, :, pl.ds(others_at, width)] = other_ref[:, pl.ds(others, width)]
        out_ref[chip, :, 2 * width :] = meta


def pack(width, n_chip, core, mine, others, own, other):
    smem = pl.BlockSpec(memory_space=pltpu.SMEM)
    vmem = pl.BlockSpec(memory_space=pltpu.VMEM)
    return pl.pallas_call(
        functools.partial(pack_kernel, width),
        out_shape=jax.ShapeDtypeStruct((n_chip, own.shape[0], 2 * width + LANES), jnp.float32),
        in_specs=[smem] * 3 + [vmem] * 2,
        out_specs=vmem,
        compiler_params=pltpu.CompilerParams(vmem_limit_bytes=VMEM_LIMIT),
        name="pack",
    )(core, mine, others, own, other)


def emission_kernel(rows_ref, senone_ref, emission_ref, level_ref):
    rows = rows_ref[...]
    top = jnp.max(rows, axis=1, keepdims=True)
    mean = jnp.sum(jnp.exp(rows - top), axis=1, keepdims=True) * (1.0 / rows.shape[1])
    level = top + jnp.log(mean)
    level_ref[...] = jnp.broadcast_to(level, level_ref.shape)
    utts = rows.shape[0]

    def group(state_group, _):
        senone = jnp.broadcast_to(senone_ref[pl.ds(state_group, 1), :], (utts, LANES))
        lane = senone & (LANES - 1)
        tile = senone >> 7
        score = jnp.zeros((utts, LANES), jnp.float32)
        for n in range(rows.shape[1] // LANES):
            part = rows_ref[:, n * LANES : (n + 1) * LANES]
            picked = jnp.take_along_axis(part, lane, axis=1, mode="promise_in_bounds")
            score = jnp.where(tile == n, picked, score)
        at = pl.multiple_of(state_group * LANES, LANES)
        emission_ref[:, pl.ds(at, LANES)] = jnp.exp(score - level)
        return 0

    lax.fori_loop(0, senone_ref.shape[0], group, 0)


def emissions(rows, senone_tiles):
    utts, senones = rows.shape
    groups = senone_tiles.shape[0]
    return pl.pallas_call(
        emission_kernel,
        out_shape=(
            jax.ShapeDtypeStruct((utts, groups * LANES), jnp.float32),
            jax.ShapeDtypeStruct((utts, LANES), jnp.float32),
        ),
        compiler_params=pltpu.CompilerParams(vmem_limit_bytes=VMEM_LIMIT),
        cost_estimate=pl.CostEstimate(
            flops=8 * groups * senones * utts, bytes_accessed=2**20, transcendentals=groups * utts * LANES
        ),
        name="emissions",
    )(rows, senone_tiles)


def step_kernel(
    first, core_ref, owner_ref, local_ref, weight_ref, recv_ref, prev_ref, emission_ref, self_ref,
    entry_ref, raw_ref, code_ref, scale_ref, bad_ref,
):
    n_chip, utts = recv_ref.shape[:2]
    blk_dev, width = self_ref.shape[:2]
    arcs = owner_ref.shape[0] // blk_dev
    lane = lax.broadcasted_iota(jnp.int32, (utts, LANES), 1)
    if first:
        scale = jnp.ones((utts, 1), jnp.float32)
    else:
        sums = recv_ref[0, :, 2 * width :]
        for chip in range(1, n_chip):
            sums += recv_ref[chip, :, 2 * width :]
        digit = lane % META - blk_dev
        place = jnp.where(
            digit == 0,
            2.0**-3,
            jnp.where(digit == 1, 2.0**-18, jnp.where(digit == 2, 2.0**-33, 0.0)),
        )
        scale = (2.0 * n_chip) / jnp.sum(sums * place, axis=1, keepdims=True)
    scale_ref[...] = jnp.broadcast_to(scale, scale_ref.shape)
    narrow = jnp.broadcast_to(scale, (utts, LANES))
    scale = jnp.broadcast_to(scale, (utts, width))

    blocks = []
    total = jnp.zeros((utts, width), jnp.float32)
    for d in range(blk_dev):
        inflow = jnp.zeros((utts, width), jnp.float32)
        for a in range(arcs):
            owner, block = owner_ref[d * arcs + a], local_ref[d * arcs + a]
            chip, side = owner >> 1, owner & 1
            code = recv_ref[chip, :, pl.ds(pl.multiple_of(side * width, width), width)] + BIAS
            meta = recv_ref[chip, :, 2 * width :]
            at = jnp.full((utts, LANES), side * META + block, jnp.int32)
            steps = jnp.take_along_axis(meta, at, axis=1, mode="promise_in_bounds")
            unit = jnp.exp2(steps * (1.0 / PEAK_STEPS)) * (narrow * TOP**-3)
            unit = jnp.concatenate([unit] * (width // LANES), axis=1)
            sent = (code * unit * code * code).astype(jnp.bfloat16).astype(jnp.float32)
            inflow += sent * weight_ref[d * arcs + a]
        own = (prev_ref[:, d * width : (d + 1) * width] * scale).astype(jnp.bfloat16)
        raw = jnp.dot(own, self_ref[d], preferred_element_type=jnp.float32)
        raw += jnp.dot(
            inflow.astype(jnp.bfloat16), entry_ref[d], preferred_element_type=jnp.float32
        )
        raw = raw * emission_ref[:, d * width : (d + 1) * width]
        raw_ref[:, d * width : (d + 1) * width] = raw
        total += raw
        blocks.append(raw)
    mean = jnp.sum(total, axis=1, keepdims=True) * (1.0 / (blk_dev * width))
    bad_ref[...] = encode(blocks, mean, core_ref[0], code_ref)


def step(first, core, owners, locals_, weights, received, previous, emission, self_trans, entry_trans):
    blk_dev, width = self_trans.shape[:2]
    utts = previous.shape[0]
    states = blk_dev * width
    smem = pl.BlockSpec(memory_space=pltpu.SMEM)
    vmem = pl.BlockSpec(memory_space=pltpu.VMEM)
    return pl.pallas_call(
        functools.partial(step_kernel, first),
        out_shape=(
            jax.ShapeDtypeStruct((utts, states), jnp.float32),
            jax.ShapeDtypeStruct((utts, states + width + LANES), jnp.float32),
            jax.ShapeDtypeStruct((utts, LANES), jnp.float32),
            jax.ShapeDtypeStruct((utts, LANES), jnp.float32),
        ),
        in_specs=[smem] * 4 + [vmem] * 5,
        out_specs=(vmem,) * 4,
        compiler_params=pltpu.CompilerParams(vmem_limit_bytes=VMEM_LIMIT),
        cost_estimate=pl.CostEstimate(
            flops=4 * utts * blk_dev * width**2, bytes_accessed=4 * blk_dev * width**2,
            transcendentals=0,
        ),
        name="step",
    )(core, owners, locals_, weights, received, previous, emission, self_trans, entry_trans)


def local(
    loglike, start_weights, self_trans, entry_trans, arc_weight, arc_src, send_ids, state_senone
):
    n_blk = lax.axis_size("blk")
    n_chip = n_blk // 2
    n_emit = lax.axis_size("emit")
    blk_dev, width = self_trans.shape[:2]
    utts = start_weights.shape[0]
    frames = loglike.shape[0]
    core = lax.axis_index("blk") % 2
    core_no = core.astype(jnp.int32).reshape(1)

    other_core = [(n, n ^ 1) for n in range(n_blk)]
    same_core = [[2 * n + c for n in range(n_chip)] for c in range(2)]

    def swap(x):
        return lax.ppermute(x, "blk", other_core)

    def exchange_chips(x):
        return lax.all_to_all(
            x, "blk", split_axis=0, concat_axis=0, tiled=True, axis_index_groups=same_core
        )

    def to_same_core(ids):
        ids = ids.reshape(-1, n_chip, 2)
        return jnp.where(core == 0, ids[:, :, 0], ids[:, :, 1])

    slots = send_ids[:, 0, :, 0]
    mine = to_same_core(slots)
    others = to_same_core(swap(slots))

    owners = (arc_src // blk_dev).reshape(-1)
    locals_ = (arc_src % blk_dev).reshape(-1)
    weights = arc_weight.astype(jnp.float32).reshape(-1)
    senone_tiles = state_senone.reshape(-1, LANES)

    def own_utterances(rows):
        return lax.dynamic_slice_in_dim(rows, lax.axis_index("emit") * utts, utts, 1)

    def first_rows(part):
        me = lax.axis_index("emit")
        parts = []
        for ahead in range(n_emit):
            piece = lax.dynamic_slice_in_dim(part, ((me + ahead) % n_emit) * utts, utts, 0)
            if ahead:
                piece = lax.ppermute(
                    piece, "emit", [(n, (n + ahead) % n_emit) for n in range(n_emit)]
                )
            parts.append(piece)
        order = [
            functools.reduce(
                lambda kept, ahead: jnp.where((me - n) % n_emit == ahead, parts[ahead], kept),
                range(1, n_emit),
                parts[0],
            )
            for n in range(n_emit)
        ]
        return jnp.concatenate(order, axis=1)

    values = start_weights
    codes = encode_start(blk_dev, core_no, start_weights)
    log_like = jnp.zeros((utts,), jnp.float32)
    bad = jnp.zeros((utts, LANES), jnp.float32)
    later = own_utterances(lax.all_gather(loglike[1:], "emit", axis=2, tiled=True))
    rows = []
    for frame_no in range(frames):
        short = codes.astype(jnp.int16)
        other = swap(short).astype(jnp.float32)
        outgoing = pack(width, n_chip, core_no, mine[frame_no], others[frame_no], codes, other)
        outgoing = outgoing.astype(jnp.int16)
        row = loglike[0] if frame_no == 0 else later[frame_no - 1]
        outgoing, row = lax.optimization_barrier((outgoing, row))
        rows.append(first_rows(row) if frame_no == 0 else row)
        received = exchange_chips(outgoing)
        emission, level = emissions(rows[-1].astype(jnp.float32), senone_tiles)
        log_like = log_like + level[:, 0]
        values, codes, scale, range_bad = step(
            frame_no == 0, core_no, owners, locals_, weights, received.astype(jnp.float32), values,
            emission, self_trans, entry_trans,
        )
        if frame_no > 0:
            log_like = log_like - jnp.log(scale[:, 0])
        if frame_no < frames - 1:
            bad = jnp.maximum(bad, range_bad)

    total = jnp.sum(values, axis=1)
    last = jnp.concatenate([total, jnp.max(bad)[None]])
    last = last + swap(last)
    sums = jnp.sum(exchange_chips(jnp.broadcast_to(last[None], (n_chip, utts + 1))), axis=0)
    mean = sums[:utts] / (blk_dev * width * n_blk)

    return lax.cond(
        sums[utts] == 0.0,
        lambda: (values * (1.0 / mean)[:, None], log_like + jnp.log(mean)),
        lambda: normalised_path(
            start_weights, jnp.stack(rows), self_trans, entry_trans, arc_weight, arc_src, slots,
            state_senone,
        ),
    )


def solution(mesh):
    in_specs = (
        P(None, None, "emit"),
        P("emit", "blk"),
        P("blk", None, None),
        P("blk", None, None),
        P("blk", None),
        P("blk", None),
        P(None, "blk", None, None),
        P("blk"),
    )
    out_specs = (P("emit", "blk"), P("emit"))
    return jax.shard_map(local, mesh=mesh, in_specs=in_specs, out_specs=out_specs, check_vma=False)
```

```python
import functools

import jax
import jax.numpy as jnp
from jax import lax
from jax.experimental import pallas as pl
from jax.experimental.pallas import tpu as pltpu
from jax.sharding import PartitionSpec as P

LANES = 128
TOP, BIAS, RATIO, TINY = 65535.0, 32768.0, 2.0**-22, 1e-30
META, PEAK_STEPS = 16, 256.0
MEAN_LOW, MEAN_HIGH = 2.0**-4, 4095.0
VMEM_LIMIT = 48 * 2**20


def exchange(outgoing):
    return lax.all_to_all(outgoing, "blk", split_axis=0, concat_axis=0, tiled=True)


def sum_over_blk(part):
    n_blk = lax.axis_size("blk")
    return jnp.sum(exchange(jnp.broadcast_to(part[None], (n_blk,) + part.shape)), axis=0)


def advance(values, matrices):
    return jnp.einsum("juv,jvw->juw", values, matrices, preferred_element_type=jnp.float32)


def normalised_path(
    start, first, later, self_trans, entry_trans, arc_weight, arc_src, send_ids, state_senone
):
    rows = jnp.concatenate([first[None], later], axis=0)
    slots = send_ids[:, 0, :, 0]
    utt_dev, n_blk = start.shape[0], lax.axis_size("blk")
    blk_dev, block_width = self_trans.shape[:2]
    state_count = blk_dev * block_width * n_blk
    senders = lax.broadcasted_iota(jnp.int32, (1, 1, n_blk), 2)
    arc_values = jnp.where(
        (arc_src // blk_dev)[:, :, None] == senders, arc_weight[:, :, None].astype(jnp.float32), 0.0
    )
    mixing = jnp.sum(arc_values, axis=1).astype(jnp.bfloat16)

    def blocks(values):
        return values.reshape(utt_dev, blk_dev, block_width).transpose(1, 0, 2)

    def frame(frame_no, carry):
        forward, log_like = carry
        sent = forward.astype(jnp.bfloat16)
        padded = jnp.concatenate([sent, jnp.zeros_like(sent[:1])], axis=0)
        outgoing = padded.at[slots[frame_no]].get(mode="promise_in_bounds")
        incoming = exchange(outgoing).reshape(n_blk, utt_dev * block_width)
        inflow = jnp.dot(mixing, incoming, preferred_element_type=jnp.float32)
        inflow = inflow.astype(jnp.bfloat16).reshape(blk_dev, utt_dev, block_width)
        raw_mass = advance(sent, self_trans) + advance(inflow, entry_trans)
        scores = rows[frame_no].at[:, state_senone].get(mode="promise_in_bounds")
        raw_mass = raw_mass * jnp.exp(blocks(scores).astype(jnp.float32))
        mass_sum = sum_over_blk(jnp.sum(raw_mass, axis=(0, 2)))
        forward = raw_mass * (state_count / mass_sum)[None, :, None]
        return forward, log_like + jnp.log(mass_sum / state_count)

    log_like = jnp.zeros((utt_dev,), jnp.float32)
    forward, log_like = lax.fori_loop(0, rows.shape[0], frame, (blocks(start), log_like))
    return forward.transpose(1, 0, 2).reshape(start.shape), log_like


def encode(blocks, mean, core, out_ref):
    utts, width = blocks[0].shape
    lane = lax.broadcasted_iota(jnp.int32, (utts, LANES), 1) - core * META
    meta = jnp.zeros((utts, LANES), jnp.float32)
    bad = jnp.where((mean >= MEAN_LOW) & (mean <= MEAN_HIGH), 0.0, 1.0)
    for d, block in enumerate(blocks):
        peak = jnp.max(block, axis=1, keepdims=True)
        least = jnp.min(block, axis=1, keepdims=True)
        bad = jnp.where((least >= peak * RATIO) & (least >= TINY), bad, 1.0)
        steps = jnp.ceil(jnp.log2(peak) * PEAK_STEPS)
        share = block * jnp.exp2(steps * (-1.0 / PEAK_STEPS))
        root = jnp.exp2(jnp.log2(share) * (1.0 / 3.0))
        code = jnp.clip(jnp.round(root * TOP), 0.0, TOP) - BIAS
        out_ref[:, d * width : (d + 1) * width] = code
        meta = jnp.where(lane == d, steps, meta)
    n = len(blocks)
    out_ref[:, n * width : (n + 1) * width] = jnp.full((utts, width), -BIAS, jnp.float32)
    rest = mean * 8.0
    for digit in range(3):
        whole = jnp.floor(rest)
        meta = jnp.where(lane == n + digit, whole, meta)
        rest = (rest - whole) * 2.0**15
    out_ref[:, (n + 1) * width :] = meta
    return jnp.broadcast_to(bad, (utts, LANES))


def encode_kernel(blk_dev, core_ref, start_ref, out_ref):
    width = start_ref.shape[1] // blk_dev
    blocks = [
        start_ref[:, d * width : (d + 1) * width].astype(jnp.bfloat16).astype(jnp.float32)
        for d in range(blk_dev)
    ]
    encode(blocks, jnp.ones((start_ref.shape[0], 1), jnp.float32), core_ref[0], out_ref)


def encode_start(blk_dev, core, start):
    utts, states = start.shape
    return pl.pallas_call(
        functools.partial(encode_kernel, blk_dev),
        out_shape=jax.ShapeDtypeStruct((utts, states + states // blk_dev + LANES), jnp.float32),
        in_specs=[pl.BlockSpec(memory_space=pltpu.SMEM), pl.BlockSpec(memory_space=pltpu.VMEM)],
        out_specs=pl.BlockSpec(memory_space=pltpu.VMEM),
        compiler_params=pltpu.CompilerParams(vmem_limit_bytes=VMEM_LIMIT),
        name="encode",
    )(core, start)


def pack_kernel(width, core_ref, mine_ref, others_ref, own_ref, other_ref, out_ref):
    core = core_ref[0]
    mine_at = pl.multiple_of(core * width, width)
    others_at = pl.multiple_of((1 - core) * width, width)
    meta = own_ref[:, own_ref.shape[1] - LANES :] + other_ref[:, own_ref.shape[1] - LANES :]
    for chip in range(out_ref.shape[0]):
        mine = pl.multiple_of(mine_ref[2 * chip + core] * width, width)
        others = pl.multiple_of(others_ref[2 * chip + core] * width, width)
        out_ref[chip, :, pl.ds(mine_at, width)] = own_ref[:, pl.ds(mine, width)]
        out_ref[chip, :, pl.ds(others_at, width)] = other_ref[:, pl.ds(others, width)]
        out_ref[chip, :, 2 * width :] = meta


def pack(width, n_chip, core, mine, others, own, other):
    smem = pl.BlockSpec(memory_space=pltpu.SMEM)
    vmem = pl.BlockSpec(memory_space=pltpu.VMEM)
    return pl.pallas_call(
        functools.partial(pack_kernel, width),
        out_shape=jax.ShapeDtypeStruct((n_chip, own.shape[0], 2 * width + LANES), jnp.float32),
        in_specs=[smem] * 3 + [vmem] * 2,
        out_specs=vmem,
        compiler_params=pltpu.CompilerParams(vmem_limit_bytes=VMEM_LIMIT),
        name="pack",
    )(core, mine, others, own, other)


def emission_kernel(rows_ref, senone_ref, emission_ref, level_ref):
    frames, utts, senones = rows_ref.shape
    tiles = senones // LANES
    levels = []
    for frame in range(frames):
        rows = rows_ref[frame]
        top = jnp.max(rows, axis=1, keepdims=True)
        mean = jnp.sum(jnp.exp(rows - top), axis=1, keepdims=True) * (1.0 / senones)
        levels.append(top + jnp.log(mean))
        level_ref[frame] = jnp.broadcast_to(levels[-1], (utts, LANES))

    def packed(pair, n):
        at = slice(n * LANES, (n + 1) * LANES)
        low = rows_ref[2 * pair, :, at] * -16.0
        if 2 * pair + 1 < frames:
            low += rows_ref[2 * pair + 1, :, at] * -32768.0
        return low

    pairs = (frames + 1) // 2

    def group(state_group, _):
        senone = jnp.broadcast_to(senone_ref[pl.ds(state_group, 1), :], (utts, LANES))
        lane = senone & (LANES - 1)
        tile = senone >> 7
        found = [jnp.zeros((utts, LANES), jnp.float32)] * pairs
        for n in range(tiles):
            here = tile == n
            for pair in range(pairs):
                picked = jnp.take_along_axis(
                    packed(pair, n), lane, axis=1, mode="promise_in_bounds"
                )
                found[pair] = jnp.where(here, picked, found[pair])
        at = pl.multiple_of(state_group * LANES, LANES)
        for pair in range(pairs):
            high = jnp.floor(found[pair] * (1.0 / 2048.0))
            both = (found[pair] - high * 2048.0, high)
            for frame in range(2 * pair, min(2 * pair + 2, frames)):
                score = both[frame - 2 * pair] * (-1.0 / 16.0)
                emission_ref[frame, :, pl.ds(at, LANES)] = jnp.exp(score - levels[frame])
        return 0

    lax.fori_loop(0, senone_ref.shape[0], group, 0)


def emissions(rows, senone_tiles):
    frames, utts, senones = rows.shape
    groups = senone_tiles.shape[0]
    return pl.pallas_call(
        emission_kernel,
        out_shape=(
            jax.ShapeDtypeStruct((frames, utts, groups * LANES), jnp.float32),
            jax.ShapeDtypeStruct((frames, utts, LANES), jnp.float32),
        ),
        compiler_params=pltpu.CompilerParams(vmem_limit_bytes=VMEM_LIMIT),
        cost_estimate=pl.CostEstimate(
            flops=8 * frames * groups * senones * utts, bytes_accessed=2**20,
            transcendentals=frames * groups * utts * LANES,
        ),
        name="emissions",
    )(rows, senone_tiles)


def step_kernel(
    first, last, core_ref, owner_ref, local_ref, weight_ref, recv_ref, prev_ref, emission_ref,
    self_ref, entry_ref, raw_ref, scale_ref, end_ref, *code_ref,
):
    n_chip, utts = recv_ref.shape[:2]
    blk_dev, width = self_ref.shape[:2]
    arcs = owner_ref.shape[0] // blk_dev
    lane = lax.broadcasted_iota(jnp.int32, (utts, LANES), 1)
    if first:
        scale = jnp.ones((utts, 1), jnp.float32)
    else:
        sums = recv_ref[0, :, 2 * width :]
        for chip in range(1, n_chip):
            sums += recv_ref[chip, :, 2 * width :]
        digit = lane % META - blk_dev
        place = jnp.where(
            digit == 0,
            2.0**-3,
            jnp.where(digit == 1, 2.0**-18, jnp.where(digit == 2, 2.0**-33, 0.0)),
        )
        scale = (2.0 * n_chip) / jnp.sum(sums * place, axis=1, keepdims=True)
    scale_ref[...] = jnp.broadcast_to(scale, scale_ref.shape)
    narrow = jnp.broadcast_to(scale, (utts, LANES)) * TOP**-3
    scale = jnp.broadcast_to(scale, (utts, width))

    def inflow_of(d):
        inflow = jnp.zeros((utts, width), jnp.float32)
        for a in range(arcs):
            owner, block = owner_ref[d * arcs + a], local_ref[d * arcs + a]
            chip, side = owner >> 1, owner & 1
            code = recv_ref[chip, :, pl.ds(pl.multiple_of(side * width, width), width)] + BIAS
            meta = recv_ref[chip, :, 2 * width :]
            at = jnp.full((utts, LANES), side * META + block, jnp.int32)
            steps = jnp.take_along_axis(meta, at, axis=1, mode="promise_in_bounds")
            unit = jnp.exp2(steps * (1.0 / PEAK_STEPS)) * narrow
            unit = jnp.concatenate([unit] * (width // LANES), axis=1)
            sent = (code * unit * code * code).astype(jnp.bfloat16).astype(jnp.float32)
            inflow += sent * weight_ref[d * arcs + a]
        return inflow.astype(jnp.bfloat16)

    blocks = []
    total = jnp.zeros((utts, width), jnp.float32)
    inflow = inflow_of(0)
    for d in range(blk_dev):
        here = slice(d * width, (d + 1) * width)
        own = (prev_ref[:, here] * scale).astype(jnp.bfloat16)
        raw = jnp.dot(own, self_ref[d], preferred_element_type=jnp.float32)
        after = inflow_of(d + 1) if d + 1 < blk_dev else None
        raw += jnp.dot(inflow, entry_ref[d], preferred_element_type=jnp.float32)
        raw = raw * emission_ref[:, here]
        raw_ref[:, here] = raw
        total += raw
        blocks.append(raw)
        inflow = after
    mean = jnp.sum(total, axis=1, keepdims=True) * (1.0 / (blk_dev * width))
    if last:
        end_ref[...] = jnp.broadcast_to(mean, end_ref.shape)
    else:
        end_ref[...] = encode(blocks, mean, core_ref[0], code_ref[0])


def step(
    first, last, core, owners, locals_, weights, received, previous, emission, self_trans, entry_trans
):
    blk_dev, width = self_trans.shape[:2]
    utts = previous.shape[0]
    states = blk_dev * width
    smem = pl.BlockSpec(memory_space=pltpu.SMEM)
    vmem = pl.BlockSpec(memory_space=pltpu.VMEM)
    out_shape = [
        jax.ShapeDtypeStruct((utts, states), jnp.float32),
        jax.ShapeDtypeStruct((utts, LANES), jnp.float32),
        jax.ShapeDtypeStruct((utts, LANES), jnp.float32),
    ]
    if not last:
        out_shape.append(jax.ShapeDtypeStruct((utts, states + width + LANES), jnp.float32))
    return pl.pallas_call(
        functools.partial(step_kernel, first, last),
        out_shape=out_shape,
        in_specs=[smem] * 4 + [vmem] * 5,
        out_specs=[vmem] * len(out_shape),
        compiler_params=pltpu.CompilerParams(vmem_limit_bytes=VMEM_LIMIT),
        cost_estimate=pl.CostEstimate(
            flops=4 * utts * blk_dev * width**2, bytes_accessed=4 * blk_dev * width**2,
            transcendentals=0,
        ),
        name="step",
    )(core, owners, locals_, weights, received, previous, emission, self_trans, entry_trans)


def local(
    loglike, start_weights, self_trans, entry_trans, arc_weight, arc_src, send_ids, state_senone
):
    n_blk = lax.axis_size("blk")
    n_chip = n_blk // 2
    n_emit = lax.axis_size("emit")
    blk_dev, width = self_trans.shape[:2]
    utts = start_weights.shape[0]
    frames = loglike.shape[0]
    core = lax.axis_index("blk") % 2
    core_no = core.astype(jnp.int32).reshape(1)

    other_core = [(n, n ^ 1) for n in range(n_blk)]
    same_core = [[2 * n + c for n in range(n_chip)] for c in range(2)]

    def swap(x):
        return lax.ppermute(x, "blk", other_core)

    def exchange_chips(x):
        return lax.all_to_all(
            x, "blk", split_axis=0, concat_axis=0, tiled=True, axis_index_groups=same_core
        )

    slots = [send_ids[0, 0, :, 0]]
    other_slots = [swap(slots[0])]

    owners = (arc_src // blk_dev).reshape(-1)
    locals_ = (arc_src % blk_dev).reshape(-1)
    weights = arc_weight.astype(jnp.float32).reshape(-1)
    senone_tiles = state_senone.reshape(-1, LANES)

    def own_utterances(rows):
        return lax.dynamic_slice_in_dim(rows, lax.axis_index("emit") * utts, utts, 1)

    def first_rows(part):
        me = lax.axis_index("emit")
        parts = []
        for ahead in range(n_emit):
            piece = lax.dynamic_slice_in_dim(part, ((me + ahead) % n_emit) * utts, utts, 0)
            if ahead:
                piece = lax.ppermute(
                    piece, "emit", [(n, (n + ahead) % n_emit) for n in range(n_emit)]
                )
            parts.append(piece)
        order = [
            functools.reduce(
                lambda kept, ahead: jnp.where((me - n) % n_emit == ahead, parts[ahead], kept),
                range(1, n_emit),
                parts[0],
            )
            for n in range(n_emit)
        ]
        return jnp.concatenate(order, axis=1)

    values = start_weights
    codes = encode_start(blk_dev, core_no, start_weights)
    later = own_utterances(lax.all_gather(loglike[1:], "emit", axis=2, tiled=True))
    first = None
    ends, scales = [], []
    for frame_no in range(frames):
        short = codes.astype(jnp.int16)
        other = swap(short).astype(jnp.float32)
        outgoing = pack(
            width, n_chip, core_no, slots[frame_no], other_slots[frame_no], codes, other
        ).astype(jnp.int16)
        if frame_no == 0:
            outgoing, row, ids = lax.optimization_barrier(
                (outgoing, loglike[0], send_ids[1:, 0, :, 0])
            )
            first = first_rows(row)
            other_ids = swap(ids)
            slots += [ids[n] for n in range(frames - 1)]
            other_slots += [other_ids[n] for n in range(frames - 1)]
            first_emission, first_level = emissions(
                first[None].astype(jnp.float32), senone_tiles
            )
        if frame_no == 1:
            outgoing, later = lax.optimization_barrier((outgoing, later))
            later_emissions, later_levels = emissions(later.astype(jnp.float32), senone_tiles)
        received = exchange_chips(outgoing).astype(jnp.float32)
        emission = first_emission[0] if frame_no == 0 else later_emissions[frame_no - 1]
        values, scale, end, *rest = step(
            frame_no == 0, frame_no == frames - 1, core_no, owners, locals_, weights, received,
            values, emission, self_trans, entry_trans,
        )
        codes = rest[0] if rest else None
        scales.append(scale)
        ends.append(end)

    values, ends, scales = lax.optimization_barrier((values, ends, scales))
    bad = jnp.max(functools.reduce(jnp.maximum, ends[:-1]))
    last = jnp.concatenate([ends[-1][:, 0], bad[None]])
    sums = jnp.sum(exchange(jnp.broadcast_to(last[None], (n_blk, utts + 1))), axis=0)
    mean = sums[:utts] / n_blk
    norms = functools.reduce(lambda a, b: a + b, [jnp.log(scale) for scale in scales[1:]])
    log_like = first_level[0, :, 0] + jnp.sum(later_levels[:, :, 0], axis=0) - norms[:, 0]

    return lax.cond(
        sums[utts] == 0.0,
        lambda: (values * (1.0 / mean)[:, None], log_like + jnp.log(mean)),
        lambda: normalised_path(
            start_weights, first, later, self_trans, entry_trans, arc_weight, arc_src, send_ids,
            state_senone,
        ),
    )


def solution(mesh):
    in_specs = (
        P(None, None, "emit"),
        P("emit", "blk"),
        P("blk", None, None),
        P("blk", None, None),
        P("blk", None),
        P("blk", None),
        P(None, "blk", None, None),
        P("blk"),
    )
    out_specs = (P("emit", "blk"), P("emit"))
    return jax.shard_map(local, mesh=mesh, in_specs=in_specs, out_specs=out_specs, check_vma=False)
```

```python
import functools

import jax
import jax.numpy as jnp
from jax import lax
from jax.experimental import pallas as pl
from jax.experimental.pallas import tpu as pltpu
from jax.sharding import PartitionSpec as P

LANES = 128
TOP, BIAS, RATIO, TINY = 65535.0, 32768.0, 2.0**-22, 1e-30
META, PEAK_STEPS = 16, 256.0
MEAN_LOW, MEAN_HIGH = 2.0**-4, 4095.0
VMEM_LIMIT = 48 * 2**20


def exchange(outgoing):
    return lax.all_to_all(outgoing, "blk", split_axis=0, concat_axis=0, tiled=True)


def sum_over_blk(part):
    n_blk = lax.axis_size("blk")
    return jnp.sum(exchange(jnp.broadcast_to(part[None], (n_blk,) + part.shape)), axis=0)


def advance(values, matrices):
    return jnp.einsum("juv,jvw->juw", values, matrices, preferred_element_type=jnp.float32)


def normalised_path(
    start, first, later, self_trans, entry_trans, arc_weight, arc_src, send_ids, state_senone
):
    rows = jnp.concatenate([first[None], later], axis=0)
    slots = send_ids[:, 0, :, 0]
    utt_dev, n_blk = start.shape[0], lax.axis_size("blk")
    blk_dev, block_width = self_trans.shape[:2]
    state_count = blk_dev * block_width * n_blk
    senders = lax.broadcasted_iota(jnp.int32, (1, 1, n_blk), 2)
    arc_values = jnp.where(
        (arc_src // blk_dev)[:, :, None] == senders, arc_weight[:, :, None].astype(jnp.float32), 0.0
    )
    mixing = jnp.sum(arc_values, axis=1).astype(jnp.bfloat16)

    def blocks(values):
        return values.reshape(utt_dev, blk_dev, block_width).transpose(1, 0, 2)

    def frame(frame_no, carry):
        forward, log_like = carry
        sent = forward.astype(jnp.bfloat16)
        padded = jnp.concatenate([sent, jnp.zeros_like(sent[:1])], axis=0)
        outgoing = padded.at[slots[frame_no]].get(mode="promise_in_bounds")
        incoming = exchange(outgoing).reshape(n_blk, utt_dev * block_width)
        inflow = jnp.dot(mixing, incoming, preferred_element_type=jnp.float32)
        inflow = inflow.astype(jnp.bfloat16).reshape(blk_dev, utt_dev, block_width)
        raw_mass = advance(sent, self_trans) + advance(inflow, entry_trans)
        scores = rows[frame_no].at[:, state_senone].get(mode="promise_in_bounds")
        raw_mass = raw_mass * jnp.exp(blocks(scores).astype(jnp.float32))
        mass_sum = sum_over_blk(jnp.sum(raw_mass, axis=(0, 2)))
        forward = raw_mass * (state_count / mass_sum)[None, :, None]
        return forward, log_like + jnp.log(mass_sum / state_count)

    log_like = jnp.zeros((utt_dev,), jnp.float32)
    forward, log_like = lax.fori_loop(0, rows.shape[0], frame, (blocks(start), log_like))
    return forward.transpose(1, 0, 2).reshape(start.shape), log_like


def encode(blocks, mean, core, out_ref):
    utts, width = blocks[0].shape
    lane = lax.broadcasted_iota(jnp.int32, (utts, LANES), 1) - core * META
    meta = jnp.zeros((utts, LANES), jnp.float32)
    bad = jnp.where((mean >= MEAN_LOW) & (mean <= MEAN_HIGH), 0.0, 1.0)
    for d, block in enumerate(blocks):
        peak = jnp.max(block, axis=1, keepdims=True)
        least = jnp.min(block, axis=1, keepdims=True)
        bad = jnp.where((least >= peak * RATIO) & (least >= TINY), bad, 1.0)
        steps = jnp.ceil(jnp.log2(peak) * PEAK_STEPS)
        share = block * jnp.exp2(steps * (-1.0 / PEAK_STEPS))
        root = jnp.exp2(jnp.log2(share) * (1.0 / 3.0))
        code = jnp.clip(jnp.round(root * TOP), 0.0, TOP) - BIAS
        out_ref[:, d * width : (d + 1) * width] = code
        meta = jnp.where(lane == d, steps, meta)
    n = len(blocks)
    out_ref[:, n * width : (n + 1) * width] = jnp.full((utts, width), -BIAS, jnp.float32)
    rest = mean * 8.0
    for digit in range(3):
        whole = jnp.floor(rest)
        meta = jnp.where(lane == n + digit, whole, meta)
        rest = (rest - whole) * 2.0**15
    out_ref[:, (n + 1) * width :] = meta
    return jnp.broadcast_to(bad, (utts, LANES))


def encode_kernel(blk_dev, core_ref, start_ref, out_ref):
    width = start_ref.shape[1] // blk_dev
    blocks = [
        start_ref[:, d * width : (d + 1) * width].astype(jnp.bfloat16).astype(jnp.float32)
        for d in range(blk_dev)
    ]
    encode(blocks, jnp.ones((start_ref.shape[0], 1), jnp.float32), core_ref[0], out_ref)


def encode_start(blk_dev, core, start):
    utts, states = start.shape
    return pl.pallas_call(
        functools.partial(encode_kernel, blk_dev),
        out_shape=jax.ShapeDtypeStruct((utts, states + states // blk_dev + LANES), jnp.float32),
        in_specs=[pl.BlockSpec(memory_space=pltpu.SMEM), pl.BlockSpec(memory_space=pltpu.VMEM)],
        out_specs=pl.BlockSpec(memory_space=pltpu.VMEM),
        compiler_params=pltpu.CompilerParams(vmem_limit_bytes=VMEM_LIMIT),
        name="encode",
    )(core, start)


def pack_kernel(width, core_ref, mine_ref, others_ref, own_ref, other_ref, out_ref):
    core = core_ref[0]
    mine_at = pl.multiple_of(core * width, width)
    others_at = pl.multiple_of((1 - core) * width, width)
    meta = own_ref[:, own_ref.shape[1] - LANES :] + other_ref[:, own_ref.shape[1] - LANES :]
    for chip in range(out_ref.shape[0]):
        mine = pl.multiple_of(mine_ref[2 * chip + core] * width, width)
        others = pl.multiple_of(others_ref[2 * chip + core] * width, width)
        out_ref[chip, :, pl.ds(mine_at, width)] = own_ref[:, pl.ds(mine, width)]
        out_ref[chip, :, pl.ds(others_at, width)] = other_ref[:, pl.ds(others, width)]
        out_ref[chip, :, 2 * width :] = meta


def pack(width, n_chip, core, mine, others, own, other):
    smem = pl.BlockSpec(memory_space=pltpu.SMEM)
    vmem = pl.BlockSpec(memory_space=pltpu.VMEM)
    return pl.pallas_call(
        functools.partial(pack_kernel, width),
        out_shape=jax.ShapeDtypeStruct((n_chip, own.shape[0], 2 * width + LANES), jnp.float32),
        in_specs=[smem] * 3 + [vmem] * 2,
        out_specs=vmem,
        compiler_params=pltpu.CompilerParams(vmem_limit_bytes=VMEM_LIMIT),
        name="pack",
    )(core, mine, others, own, other)


def emission_kernel(rows_ref, senone_ref, emission_ref, level_ref):
    frames, utts, senones = rows_ref.shape
    tiles = senones // LANES
    levels = []
    for frame in range(frames):
        rows = rows_ref[frame]
        top = jnp.max(rows, axis=1, keepdims=True)
        mean = jnp.sum(jnp.exp(rows - top), axis=1, keepdims=True) * (1.0 / senones)
        levels.append(top + jnp.log(mean))
        level_ref[frame] = jnp.broadcast_to(levels[-1], (utts, LANES))

    def packed(pair, n):
        at = slice(n * LANES, (n + 1) * LANES)
        low = rows_ref[2 * pair, :, at] * -16.0
        if 2 * pair + 1 < frames:
            low += rows_ref[2 * pair + 1, :, at] * -32768.0
        return low

    pairs = (frames + 1) // 2

    def group(state_group, _):
        senone = jnp.broadcast_to(senone_ref[pl.ds(state_group, 1), :], (utts, LANES))
        lane = senone & (LANES - 1)
        tile = senone >> 7
        found = [jnp.zeros((utts, LANES), jnp.float32)] * pairs
        for n in range(tiles):
            here = tile == n
            for pair in range(pairs):
                picked = jnp.take_along_axis(
                    packed(pair, n), lane, axis=1, mode="promise_in_bounds"
                )
                found[pair] = jnp.where(here, picked, found[pair])
        at = pl.multiple_of(state_group * LANES, LANES)
        for pair in range(pairs):
            high = jnp.floor(found[pair] * (1.0 / 2048.0))
            both = (found[pair] - high * 2048.0, high)
            for frame in range(2 * pair, min(2 * pair + 2, frames)):
                score = both[frame - 2 * pair] * (-1.0 / 16.0)
                emission_ref[frame, :, pl.ds(at, LANES)] = jnp.exp(score - levels[frame])
        return 0

    lax.fori_loop(0, senone_ref.shape[0], group, 0)


def emissions(rows, senone_tiles):
    frames, utts, senones = rows.shape
    groups = senone_tiles.shape[0]
    return pl.pallas_call(
        emission_kernel,
        out_shape=(
            jax.ShapeDtypeStruct((frames, utts, groups * LANES), jnp.float32),
            jax.ShapeDtypeStruct((frames, utts, LANES), jnp.float32),
        ),
        compiler_params=pltpu.CompilerParams(vmem_limit_bytes=VMEM_LIMIT),
        cost_estimate=pl.CostEstimate(
            flops=8 * frames * groups * senones * utts, bytes_accessed=2**20,
            transcendentals=frames * groups * utts * LANES,
        ),
        name="emissions",
    )(rows, senone_tiles)


def column_to_row(column):
    n = column.shape[0]
    lane = lax.broadcasted_iota(jnp.int32, (n, LANES), 1)
    place = lax.broadcasted_iota(jnp.int32, (n, LANES), 0)
    return jnp.sum(jnp.where(lane == place, column, 0.0), axis=0, keepdims=True)


def row_to_column(row, n):
    lane = lax.broadcasted_iota(jnp.int32, (n, LANES), 1)
    place = lax.broadcasted_iota(jnp.int32, (n, LANES), 0)
    return jnp.sum(jnp.where(lane == place, row, 0.0), axis=1, keepdims=True)


def step_kernel(
    first, last, streamed, slot, core_ref, owner_ref, local_ref, weight_ref, recv_ref, prev_ref,
    emission_ref, level_ref, log_in_ref, bad_in_ref, self_in, entry_in, raw_ref, log_ref, bad_ref,
    end_ref, *scratch,
):
    n_chip, utts = recv_ref.shape[:2]
    blk_dev, width = self_in.shape[:2]
    arcs = owner_ref.shape[0] // blk_dev
    lane = lax.broadcasted_iota(jnp.int32, (utts, LANES), 1)
    self_ref, entry_ref, copies = self_in, entry_in, []
    if streamed:
        self_ref, entry_ref, arrived = scratch
        for d in range(blk_dev):
            copies.append(
                (
                    pltpu.make_async_copy(self_in.at[d], self_ref.at[d], arrived.at[2 * d]),
                    pltpu.make_async_copy(entry_in.at[d], entry_ref.at[d], arrived.at[2 * d + 1]),
                )
            )
            copies[d][0].start()
            copies[d][1].start()
    log_like = log_in_ref[...] + level_ref[slot]
    if first:
        scale = jnp.ones((utts, 1), jnp.float32)
    else:
        sums = recv_ref[0, :, 2 * width :]
        for chip in range(1, n_chip):
            sums += recv_ref[chip, :, 2 * width :]
        digit = lane % META - blk_dev
        place = jnp.where(
            digit == 0,
            2.0**-3,
            jnp.where(digit == 1, 2.0**-18, jnp.where(digit == 2, 2.0**-33, 0.0)),
        )
        scale = (2.0 * n_chip) / jnp.sum(sums * place, axis=1, keepdims=True)
        log_like = log_like - jnp.log(scale)
    log_ref[...] = log_like
    narrow = jnp.broadcast_to(scale, (utts, LANES)) * TOP**-3
    scale = jnp.broadcast_to(scale, (utts, width))

    def inflow_of(d):
        inflow = jnp.zeros((utts, width), jnp.float32)
        for a in range(arcs):
            owner, block = owner_ref[d * arcs + a], local_ref[d * arcs + a]
            chip, side = owner >> 1, owner & 1
            code = recv_ref[chip, :, pl.ds(pl.multiple_of(side * width, width), width)] + BIAS
            meta = recv_ref[chip, :, 2 * width :]
            at = jnp.full((utts, LANES), side * META + block, jnp.int32)
            steps = jnp.take_along_axis(meta, at, axis=1, mode="promise_in_bounds")
            unit = jnp.exp2(steps * (1.0 / PEAK_STEPS)) * narrow
            unit = jnp.concatenate([unit] * (width // LANES), axis=1)
            sent = (code * unit * code * code).astype(jnp.bfloat16).astype(jnp.float32)
            inflow += sent * weight_ref[d * arcs + a]
        return inflow.astype(jnp.bfloat16)

    blocks = []
    total = jnp.zeros((utts, width), jnp.float32)
    inflow = inflow_of(0)
    for d in range(blk_dev):
        here = slice(d * width, (d + 1) * width)
        own = (prev_ref[:, here] * scale).astype(jnp.bfloat16)
        if streamed:
            copies[d][0].wait()
            copies[d][1].wait()
        raw = jnp.dot(own, self_ref[d], preferred_element_type=jnp.float32)
        after = inflow_of(d + 1) if d + 1 < blk_dev else None
        raw += jnp.dot(inflow, entry_ref[d], preferred_element_type=jnp.float32)
        raw = raw * emission_ref[slot, :, here]
        raw_ref[:, here] = raw
        total += raw
        blocks.append(raw)
        inflow = after
    mean = jnp.sum(total, axis=1, keepdims=True) * (1.0 / (blk_dev * width))
    if last:
        bad_ref[...] = bad_in_ref[...]
        row = column_to_row(mean)
        bad = jnp.max(bad_in_ref[...], axis=0, keepdims=True)
        row = jnp.where(lane[:1] == utts, bad, row)
        end_ref[...] = jnp.broadcast_to(row, end_ref.shape)
    else:
        bad_ref[...] = jnp.maximum(bad_in_ref[...], encode(blocks, mean, core_ref[0], end_ref))


def step(frame_no, last, indices, received, previous, emission, level, slot, tallies, matrices):
    blk_dev, width = matrices[0].shape[:2]
    n_chip = received.shape[0]
    utts, states = previous.shape
    streamed = frame_no < 2
    smem = pl.BlockSpec(memory_space=pltpu.SMEM)
    vmem = pl.BlockSpec(memory_space=pltpu.VMEM)
    matrix = pl.BlockSpec(memory_space=pl.ANY) if streamed else vmem
    end = (2 * n_chip, LANES) if last else (utts, states + width + LANES)
    tile = jax.ShapeDtypeStruct((utts, LANES), jnp.float32)
    scratch = []
    if streamed:
        scratch = [pltpu.VMEM(m.shape, m.dtype) for m in matrices]
        scratch.append(pltpu.SemaphoreType.DMA((2 * blk_dev,)))
    return pl.pallas_call(
        functools.partial(step_kernel, frame_no == 0, last, streamed, slot),
        out_shape=[
            jax.ShapeDtypeStruct((utts, states), jnp.float32),
            tile,
            tile,
            jax.ShapeDtypeStruct(end, jnp.float32),
        ],
        in_specs=[smem] * 4 + [vmem] * 6 + [matrix] * 2,
        out_specs=[vmem] * 4,
        scratch_shapes=scratch,
        compiler_params=pltpu.CompilerParams(vmem_limit_bytes=VMEM_LIMIT),
        cost_estimate=pl.CostEstimate(
            flops=4 * utts * blk_dev * width**2, bytes_accessed=4 * blk_dev * width**2,
            transcendentals=0,
        ),
        name="step",
    )(*indices, received, previous, emission, level, *tallies, *matrices)


def finish_kernel(recv_ref, raw_ref, log_ref, out_ref, log_row_ref, bad_ref):
    utts = raw_ref.shape[0]
    sums = jnp.sum(recv_ref[...], axis=0, keepdims=True)
    mean = row_to_column(sums, utts) * (1.0 / recv_ref.shape[0])
    out_ref[...] = raw_ref[...] * (1.0 / mean)
    log_row_ref[...] = column_to_row((log_ref[...] + jnp.log(mean))[:, :1])
    lane = lax.broadcasted_iota(jnp.int32, (1, LANES), 1)
    bad_ref[0] = jnp.sum(jnp.where(lane == utts, sums, 0.0))


def finish(received, raw, log_like):
    vmem = pl.BlockSpec(memory_space=pltpu.VMEM)
    return pl.pallas_call(
        finish_kernel,
        out_shape=[
            jax.ShapeDtypeStruct(raw.shape, jnp.float32),
            jax.ShapeDtypeStruct((1, LANES), jnp.float32),
            jax.ShapeDtypeStruct((1,), jnp.float32),
        ],
        in_specs=[vmem] * 3,
        out_specs=[vmem, vmem, pl.BlockSpec(memory_space=pltpu.SMEM)],
        compiler_params=pltpu.CompilerParams(vmem_limit_bytes=VMEM_LIMIT),
        name="finish",
    )(received, raw, log_like)


def local(
    loglike, start_weights, self_trans, entry_trans, arc_weight, arc_src, send_ids, state_senone
):
    n_blk = lax.axis_size("blk")
    n_chip = n_blk // 2
    n_emit = lax.axis_size("emit")
    blk_dev, width = self_trans.shape[:2]
    utts = start_weights.shape[0]
    frames = loglike.shape[0]
    core = lax.axis_index("blk") % 2
    core_no = core.astype(jnp.int32).reshape(1)

    other_core = [(n, n ^ 1) for n in range(n_blk)]
    same_core = [[2 * n + c for n in range(n_chip)] for c in range(2)]

    def swap(x):
        return lax.ppermute(x, "blk", other_core)

    def exchange_chips(x):
        return lax.all_to_all(
            x, "blk", split_axis=0, concat_axis=0, tiled=True, axis_index_groups=same_core
        )

    slots = [send_ids[0, 0, :, 0]]
    other_slots = [swap(slots[0])]

    owners = (arc_src // blk_dev).reshape(-1)
    locals_ = (arc_src % blk_dev).reshape(-1)
    weights = arc_weight.astype(jnp.float32).reshape(-1)
    senone_tiles = state_senone.reshape(-1, LANES)

    def own_utterances(rows):
        return lax.dynamic_slice_in_dim(rows, lax.axis_index("emit") * utts, utts, 1)

    def first_rows(part):
        me = lax.axis_index("emit")
        parts = []
        for ahead in range(n_emit):
            piece = lax.dynamic_slice_in_dim(part, ((me + ahead) % n_emit) * utts, utts, 0)
            if ahead:
                piece = lax.ppermute(
                    piece, "emit", [(n, (n + ahead) % n_emit) for n in range(n_emit)]
                )
            parts.append(piece)
        order = [
            functools.reduce(
                lambda kept, ahead: jnp.where((me - n) % n_emit == ahead, parts[ahead], kept),
                range(1, n_emit),
                parts[0],
            )
            for n in range(n_emit)
        ]
        return jnp.concatenate(order, axis=1)

    values = start_weights
    codes = encode_start(blk_dev, core_no, start_weights)
    gathered = lax.all_gather(loglike, "emit", axis=2, tiled=True)
    indices = (core_no, owners, locals_, weights)
    tallies = (jnp.zeros((utts, LANES), jnp.float32),) * 2
    for frame_no in range(frames):
        short = codes.astype(jnp.int16)
        other = swap(short).astype(jnp.float32)
        outgoing = pack(
            width, n_chip, core_no, slots[frame_no], other_slots[frame_no], codes, other
        ).astype(jnp.int16)
        if frame_no == 0:
            outgoing, scores, ids = lax.optimization_barrier((outgoing, loglike, send_ids))
            first = first_rows(scores[0])
            ids = ids[1:, 0, :, 0]
            other_ids = swap(ids)
            slots += [ids[n] for n in range(frames - 1)]
            other_slots += [other_ids[n] for n in range(frames - 1)]
            emission, level = emissions(first[None].astype(jnp.float32), senone_tiles)
        if frame_no == 1:
            outgoing, gathered = lax.optimization_barrier((outgoing, gathered))
            later = own_utterances(gathered[1:])
            emission, level = emissions(later.astype(jnp.float32), senone_tiles)
        received = exchange_chips(outgoing).astype(jnp.float32)
        values, *tallies, codes = step(
            frame_no, frame_no == frames - 1, indices, received, values, emission, level,
            max(frame_no - 1, 0), tallies, (self_trans, entry_trans),
        )

    scaled, log_like, bad = finish(exchange(codes), values, tallies[0])
    return lax.cond(
        bad[0] == 0.0,
        lambda: (scaled, log_like[0, :utts]),
        lambda: normalised_path(
            start_weights, first, later, self_trans, entry_trans, arc_weight, arc_src, send_ids,
            state_senone,
        ),
    )


def solution(mesh):
    in_specs = (
        P(None, None, "emit"),
        P("emit", "blk"),
        P("blk", None, None),
        P("blk", None, None),
        P("blk", None),
        P("blk", None),
        P(None, "blk", None, None),
        P("blk"),
    )
    out_specs = (P("emit", "blk"), P("emit"))
    return jax.shard_map(local, mesh=mesh, in_specs=in_specs, out_specs=out_specs, check_vma=False)
```

```python
import functools

import jax
import jax.numpy as jnp
from jax import lax
from jax.experimental import pallas as pl
from jax.experimental.pallas import tpu as pltpu
from jax.sharding import PartitionSpec as P

LANES = 128
TOP, BIAS, RATIO, TINY = 65535.0, 32768.0, 2.0**-22, 1e-30
META, PEAK_STEPS = 16, 256.0
MEAN_LOW, MEAN_HIGH = 2.0**-4, 4095.0
VMEM_LIMIT = 48 * 2**20


def exchange(outgoing):
    return lax.all_to_all(outgoing, "blk", split_axis=0, concat_axis=0, tiled=True)


def sum_over_blk(part):
    n_blk = lax.axis_size("blk")
    return jnp.sum(exchange(jnp.broadcast_to(part[None], (n_blk,) + part.shape)), axis=0)


def advance(values, matrices):
    return jnp.einsum("juv,jvw->juw", values, matrices, preferred_element_type=jnp.float32)


def normalised_path(
    start, first, later, self_trans, entry_trans, arc_weight, arc_src, send_ids, state_senone
):
    rows = jnp.concatenate([first[None], later], axis=0)
    slots = send_ids[:, 0, :, 0]
    utt_dev, n_blk = start.shape[0], lax.axis_size("blk")
    blk_dev, block_width = self_trans.shape[:2]
    state_count = blk_dev * block_width * n_blk
    senders = lax.broadcasted_iota(jnp.int32, (1, 1, n_blk), 2)
    arc_values = jnp.where(
        (arc_src // blk_dev)[:, :, None] == senders, arc_weight[:, :, None].astype(jnp.float32), 0.0
    )
    mixing = jnp.sum(arc_values, axis=1).astype(jnp.bfloat16)

    def blocks(values):
        return values.reshape(utt_dev, blk_dev, block_width).transpose(1, 0, 2)

    def frame(frame_no, carry):
        forward, log_like = carry
        sent = forward.astype(jnp.bfloat16)
        padded = jnp.concatenate([sent, jnp.zeros_like(sent[:1])], axis=0)
        outgoing = padded.at[slots[frame_no]].get(mode="promise_in_bounds")
        incoming = exchange(outgoing).reshape(n_blk, utt_dev * block_width)
        inflow = jnp.dot(mixing, incoming, preferred_element_type=jnp.float32)
        inflow = inflow.astype(jnp.bfloat16).reshape(blk_dev, utt_dev, block_width)
        raw_mass = advance(sent, self_trans) + advance(inflow, entry_trans)
        scores = rows[frame_no].at[:, state_senone].get(mode="promise_in_bounds")
        raw_mass = raw_mass * jnp.exp(blocks(scores).astype(jnp.float32))
        mass_sum = sum_over_blk(jnp.sum(raw_mass, axis=(0, 2)))
        forward = raw_mass * (state_count / mass_sum)[None, :, None]
        return forward, log_like + jnp.log(mass_sum / state_count)

    log_like = jnp.zeros((utt_dev,), jnp.float32)
    forward, log_like = lax.fori_loop(0, rows.shape[0], frame, (blocks(start), log_like))
    return forward.transpose(1, 0, 2).reshape(start.shape), log_like


def short(values):
    return values.astype(jnp.int32).astype(jnp.int16)


def wide(codes):
    return codes.astype(jnp.int32).astype(jnp.float32)


def encode(blocks, mean, core, out_ref):
    utts, width = blocks[0].shape
    lane = lax.broadcasted_iota(jnp.int32, (utts, LANES), 1) - core * META
    meta = jnp.zeros((utts, LANES), jnp.float32)
    bad = jnp.where((mean >= MEAN_LOW) & (mean <= MEAN_HIGH), 0.0, 1.0)
    for d, block in enumerate(blocks):
        peak = jnp.max(block, axis=1, keepdims=True)
        least = jnp.min(block, axis=1, keepdims=True)
        bad = jnp.where((least >= peak * RATIO) & (least >= TINY), bad, 1.0)
        steps = jnp.ceil(jnp.log2(peak) * PEAK_STEPS)
        share = block * jnp.exp2(steps * (-1.0 / PEAK_STEPS))
        root = jnp.exp2(jnp.log2(share) * (1.0 / 3.0))
        code = jnp.clip(jnp.round(root * TOP), 0.0, TOP) - BIAS
        out_ref[:, d * width : (d + 1) * width] = short(code)
        meta = jnp.where(lane == d, steps, meta)
    n = len(blocks)
    out_ref[:, n * width : (n + 1) * width] = short(jnp.full((utts, width), -BIAS, jnp.float32))
    rest = mean * 8.0
    for digit in range(3):
        whole = jnp.floor(rest)
        meta = jnp.where(lane == n + digit, whole, meta)
        rest = (rest - whole) * 2.0**15
    out_ref[:, (n + 1) * width :] = short(meta)
    return jnp.broadcast_to(bad, (utts, LANES))


def encode_kernel(blk_dev, core_ref, start_ref, out_ref):
    width = start_ref.shape[1] // blk_dev
    blocks = [
        start_ref[:, d * width : (d + 1) * width].astype(jnp.bfloat16).astype(jnp.float32)
        for d in range(blk_dev)
    ]
    encode(blocks, jnp.ones((start_ref.shape[0], 1), jnp.float32), core_ref[0], out_ref)


def encode_start(blk_dev, core, start):
    utts, states = start.shape
    return pl.pallas_call(
        functools.partial(encode_kernel, blk_dev),
        out_shape=jax.ShapeDtypeStruct((utts, states + states // blk_dev + LANES), jnp.int16),
        in_specs=[pl.BlockSpec(memory_space=pltpu.SMEM), pl.BlockSpec(memory_space=pltpu.VMEM)],
        out_specs=pl.BlockSpec(memory_space=pltpu.VMEM),
        compiler_params=pltpu.CompilerParams(vmem_limit_bytes=VMEM_LIMIT),
        name="encode",
    )(core, start)


def pack_kernel(width, core_ref, mine_ref, others_ref, own_ref, other_ref, out_ref):
    core = core_ref[0]
    mine_at = pl.multiple_of(core * width, width)
    others_at = pl.multiple_of((1 - core) * width, width)
    last = slice(own_ref.shape[1] - LANES, own_ref.shape[1])
    meta = short(wide(own_ref[:, last]) + wide(other_ref[:, last]))
    for chip in range(out_ref.shape[0]):
        mine = pl.multiple_of(mine_ref[2 * chip + core] * width, width)
        others = pl.multiple_of(others_ref[2 * chip + core] * width, width)
        out_ref[chip, :, pl.ds(mine_at, width)] = own_ref[:, pl.ds(mine, width)]
        out_ref[chip, :, pl.ds(others_at, width)] = other_ref[:, pl.ds(others, width)]
        out_ref[chip, :, 2 * width :] = meta


def pack(width, n_chip, core, mine, others, own, other):
    smem = pl.BlockSpec(memory_space=pltpu.SMEM)
    vmem = pl.BlockSpec(memory_space=pltpu.VMEM)
    return pl.pallas_call(
        functools.partial(pack_kernel, width),
        out_shape=jax.ShapeDtypeStruct((n_chip, own.shape[0], 2 * width + LANES), jnp.int16),
        in_specs=[smem] * 3 + [vmem] * 2,
        out_specs=vmem,
        compiler_params=pltpu.CompilerParams(vmem_limit_bytes=VMEM_LIMIT),
        name="pack",
    )(core, mine, others, own, other)


def emission_kernel(rows_ref, senone_ref, emission_ref, level_ref):
    frames, utts, senones = rows_ref.shape
    tiles = senones // LANES
    levels = []
    for frame in range(frames):
        rows = rows_ref[frame]
        top = jnp.max(rows, axis=1, keepdims=True)
        mean = jnp.sum(jnp.exp(rows - top), axis=1, keepdims=True) * (1.0 / senones)
        levels.append(top + jnp.log(mean))
        level_ref[frame] = jnp.broadcast_to(levels[-1], (utts, LANES))

    def packed(pair, n):
        at = slice(n * LANES, (n + 1) * LANES)
        low = rows_ref[2 * pair, :, at] * -16.0
        if 2 * pair + 1 < frames:
            low += rows_ref[2 * pair + 1, :, at] * -32768.0
        return low

    pairs = (frames + 1) // 2

    def group(state_group, _):
        senone = jnp.broadcast_to(senone_ref[pl.ds(state_group, 1), :], (utts, LANES))
        lane = senone & (LANES - 1)
        tile = senone >> 7
        found = [jnp.zeros((utts, LANES), jnp.float32)] * pairs
        for n in range(tiles):
            here = tile == n
            for pair in range(pairs):
                picked = jnp.take_along_axis(
                    packed(pair, n), lane, axis=1, mode="promise_in_bounds"
                )
                found[pair] = jnp.where(here, picked, found[pair])
        at = pl.multiple_of(state_group * LANES, LANES)
        for pair in range(pairs):
            high = jnp.floor(found[pair] * (1.0 / 2048.0))
            both = (found[pair] - high * 2048.0, high)
            for frame in range(2 * pair, min(2 * pair + 2, frames)):
                score = both[frame - 2 * pair] * (-1.0 / 16.0)
                emission_ref[frame, :, pl.ds(at, LANES)] = jnp.exp(score - levels[frame])
        return 0

    lax.fori_loop(0, senone_ref.shape[0], group, 0)


def emissions(rows, senone_tiles):
    frames, utts, senones = rows.shape
    groups = senone_tiles.shape[0]
    return pl.pallas_call(
        emission_kernel,
        out_shape=(
            jax.ShapeDtypeStruct((frames, utts, groups * LANES), jnp.float32),
            jax.ShapeDtypeStruct((frames, utts, LANES), jnp.float32),
        ),
        compiler_params=pltpu.CompilerParams(vmem_limit_bytes=VMEM_LIMIT),
        cost_estimate=pl.CostEstimate(
            flops=8 * frames * groups * senones * utts, bytes_accessed=2**20,
            transcendentals=frames * groups * utts * LANES,
        ),
        name="emissions",
    )(rows, senone_tiles)


def column_to_row(column):
    n = column.shape[0]
    lane = lax.broadcasted_iota(jnp.int32, (n, LANES), 1)
    place = lax.broadcasted_iota(jnp.int32, (n, LANES), 0)
    return jnp.sum(jnp.where(lane == place, column, 0.0), axis=0, keepdims=True)


def row_to_column(row, n):
    lane = lax.broadcasted_iota(jnp.int32, (n, LANES), 1)
    place = lax.broadcasted_iota(jnp.int32, (n, LANES), 0)
    return jnp.sum(jnp.where(lane == place, row, 0.0), axis=1, keepdims=True)


def step_kernel(
    first, last, streamed, slot, core_ref, owner_ref, local_ref, weight_ref, recv_ref, prev_ref,
    emission_ref, level_ref, log_in_ref, bad_in_ref, self_in, entry_in, raw_ref, log_ref, bad_ref,
    end_ref, *scratch,
):
    n_chip, utts = recv_ref.shape[:2]
    blk_dev, width = self_in.shape[:2]
    arcs = owner_ref.shape[0] // blk_dev
    lane = lax.broadcasted_iota(jnp.int32, (utts, LANES), 1)
    self_ref, entry_ref, copies = self_in, entry_in, []
    if streamed:
        self_ref, entry_ref, arrived = scratch
        for d in range(blk_dev):
            copies.append(
                (
                    pltpu.make_async_copy(self_in.at[d], self_ref.at[d], arrived.at[2 * d]),
                    pltpu.make_async_copy(entry_in.at[d], entry_ref.at[d], arrived.at[2 * d + 1]),
                )
            )
            copies[d][0].start()
            copies[d][1].start()
    log_like = log_in_ref[...] + level_ref[slot]
    if first:
        scale = jnp.ones((utts, 1), jnp.float32)
    else:
        sums = wide(recv_ref[0, :, 2 * width :])
        for chip in range(1, n_chip):
            sums += wide(recv_ref[chip, :, 2 * width :])
        digit = lane % META - blk_dev
        place = jnp.where(
            digit == 0,
            2.0**-3,
            jnp.where(digit == 1, 2.0**-18, jnp.where(digit == 2, 2.0**-33, 0.0)),
        )
        scale = (2.0 * n_chip) / jnp.sum(sums * place, axis=1, keepdims=True)
        log_like = log_like - jnp.log(scale)
    log_ref[...] = log_like
    narrow = jnp.broadcast_to(scale, (utts, LANES)) * TOP**-3
    scale = jnp.broadcast_to(scale, (utts, width))

    def inflow_of(d):
        inflow = jnp.zeros((utts, width), jnp.float32)
        for a in range(arcs):
            owner, block = owner_ref[d * arcs + a], local_ref[d * arcs + a]
            chip, side = owner >> 1, owner & 1
            code = wide(recv_ref[chip, :, pl.ds(pl.multiple_of(side * width, width), width)])
            code += BIAS
            meta = wide(recv_ref[chip, :, 2 * width :])
            at = jnp.full((utts, LANES), side * META + block, jnp.int32)
            steps = jnp.take_along_axis(meta, at, axis=1, mode="promise_in_bounds")
            unit = jnp.exp2(steps * (1.0 / PEAK_STEPS)) * narrow
            unit = jnp.concatenate([unit] * (width // LANES), axis=1)
            sent = (code * unit * code * code).astype(jnp.bfloat16).astype(jnp.float32)
            inflow += sent * weight_ref[d * arcs + a]
        return inflow.astype(jnp.bfloat16)

    blocks = []
    total = jnp.zeros((utts, width), jnp.float32)
    inflow = inflow_of(0)
    for d in range(blk_dev):
        here = slice(d * width, (d + 1) * width)
        own = (prev_ref[:, here] * scale).astype(jnp.bfloat16)
        if streamed:
            copies[d][0].wait()
            copies[d][1].wait()
        raw = jnp.dot(own, self_ref[d], preferred_element_type=jnp.float32)
        after = inflow_of(d + 1) if d + 1 < blk_dev else None
        raw += jnp.dot(inflow, entry_ref[d], preferred_element_type=jnp.float32)
        raw = raw * emission_ref[slot, :, here]
        raw_ref[:, here] = raw
        total += raw
        blocks.append(raw)
        inflow = after
    mean = jnp.sum(total, axis=1, keepdims=True) * (1.0 / (blk_dev * width))
    if last:
        bad_ref[...] = bad_in_ref[...]
        row = column_to_row(mean)
        bad = jnp.max(bad_in_ref[...], axis=0, keepdims=True)
        row = jnp.where(lane[:1] == utts, bad, row)
        end_ref[...] = jnp.broadcast_to(row, end_ref.shape)
    else:
        bad_ref[...] = jnp.maximum(bad_in_ref[...], encode(blocks, mean, core_ref[0], end_ref))


def step(frame_no, last, indices, received, previous, emission, level, slot, tallies, matrices):
    blk_dev, width = matrices[0].shape[:2]
    n_chip = received.shape[0]
    utts, states = previous.shape
    streamed = frame_no < 2
    smem = pl.BlockSpec(memory_space=pltpu.SMEM)
    vmem = pl.BlockSpec(memory_space=pltpu.VMEM)
    matrix = pl.BlockSpec(memory_space=pl.ANY) if streamed else vmem
    end = (2 * n_chip, LANES) if last else (utts, states + width + LANES)
    tile = jax.ShapeDtypeStruct((utts, LANES), jnp.float32)
    scratch = []
    if streamed:
        scratch = [pltpu.VMEM(m.shape, m.dtype) for m in matrices]
        scratch.append(pltpu.SemaphoreType.DMA((2 * blk_dev,)))
    return pl.pallas_call(
        functools.partial(step_kernel, frame_no == 0, last, streamed, slot),
        out_shape=[
            jax.ShapeDtypeStruct((utts, states), jnp.float32),
            tile,
            tile,
            jax.ShapeDtypeStruct(end, jnp.float32 if last else jnp.int16),
        ],
        in_specs=[smem] * 4 + [vmem] * 6 + [matrix] * 2,
        out_specs=[vmem] * 4,
        scratch_shapes=scratch,
        compiler_params=pltpu.CompilerParams(vmem_limit_bytes=VMEM_LIMIT),
        cost_estimate=pl.CostEstimate(
            flops=4 * utts * blk_dev * width**2, bytes_accessed=4 * blk_dev * width**2,
            transcendentals=0,
        ),
        name="step",
    )(*indices, received, previous, emission, level, *tallies, *matrices)


def finish_kernel(recv_ref, raw_ref, log_ref, out_ref, log_row_ref, bad_ref):
    utts = raw_ref.shape[0]
    sums = jnp.sum(recv_ref[...], axis=0, keepdims=True)
    mean = row_to_column(sums, utts) * (1.0 / recv_ref.shape[0])
    out_ref[...] = raw_ref[...] * (1.0 / mean)
    log_row_ref[...] = column_to_row((log_ref[...] + jnp.log(mean))[:, :1])
    lane = lax.broadcasted_iota(jnp.int32, (1, LANES), 1)
    bad_ref[0] = jnp.sum(jnp.where(lane == utts, sums, 0.0))


def finish(received, raw, log_like):
    vmem = pl.BlockSpec(memory_space=pltpu.VMEM)
    return pl.pallas_call(
        finish_kernel,
        out_shape=[
            jax.ShapeDtypeStruct(raw.shape, jnp.float32),
            jax.ShapeDtypeStruct((1, LANES), jnp.float32),
            jax.ShapeDtypeStruct((1,), jnp.float32),
        ],
        in_specs=[vmem] * 3,
        out_specs=[vmem, vmem, pl.BlockSpec(memory_space=pltpu.SMEM)],
        compiler_params=pltpu.CompilerParams(vmem_limit_bytes=VMEM_LIMIT),
        name="finish",
    )(received, raw, log_like)


def local(
    loglike, start_weights, self_trans, entry_trans, arc_weight, arc_src, send_ids, state_senone
):
    n_blk = lax.axis_size("blk")
    n_chip = n_blk // 2
    n_emit = lax.axis_size("emit")
    blk_dev, width = self_trans.shape[:2]
    utts = start_weights.shape[0]
    frames = loglike.shape[0]
    core = lax.axis_index("blk") % 2
    core_no = core.astype(jnp.int32).reshape(1)

    other_core = [(n, n ^ 1) for n in range(n_blk)]
    same_core = [[2 * n + c for n in range(n_chip)] for c in range(2)]

    def swap(x):
        return lax.ppermute(x, "blk", other_core)

    def exchange_chips(x):
        return lax.all_to_all(
            x, "blk", split_axis=0, concat_axis=0, tiled=True, axis_index_groups=same_core
        )

    slots = [send_ids[0, 0, :, 0]]
    other_slots = [swap(slots[0])]

    owners = (arc_src // blk_dev).reshape(-1)
    locals_ = (arc_src % blk_dev).reshape(-1)
    weights = arc_weight.astype(jnp.float32).reshape(-1)
    senone_tiles = state_senone.reshape(-1, LANES)

    def own_utterances(rows):
        return lax.dynamic_slice_in_dim(rows, lax.axis_index("emit") * utts, utts, 1)

    def first_rows(part):
        me = lax.axis_index("emit")
        parts = []
        for ahead in range(n_emit):
            piece = lax.dynamic_slice_in_dim(part, ((me + ahead) % n_emit) * utts, utts, 0)
            if ahead:
                piece = lax.ppermute(
                    piece, "emit", [(n, (n + ahead) % n_emit) for n in range(n_emit)]
                )
            parts.append(piece)
        order = [
            functools.reduce(
                lambda kept, ahead: jnp.where((me - n) % n_emit == ahead, parts[ahead], kept),
                range(1, n_emit),
                parts[0],
            )
            for n in range(n_emit)
        ]
        return jnp.concatenate(order, axis=1)

    values = start_weights
    codes = encode_start(blk_dev, core_no, start_weights)
    gathered = lax.all_gather(loglike, "emit", axis=2, tiled=True)
    indices = (core_no, owners, locals_, weights)
    tallies = (jnp.zeros((utts, LANES), jnp.float32),) * 2
    for frame_no in range(frames):
        outgoing = pack(
            width, n_chip, core_no, slots[frame_no], other_slots[frame_no], codes, swap(codes)
        )
        if frame_no == 0:
            outgoing, scores, ids = lax.optimization_barrier((outgoing, loglike, send_ids))
            first = first_rows(scores[0])
            ids = ids[1:, 0, :, 0]
            other_ids = swap(ids)
            slots += [ids[n] for n in range(frames - 1)]
            other_slots += [other_ids[n] for n in range(frames - 1)]
            emission, level = emissions(first[None].astype(jnp.float32), senone_tiles)
        if frame_no == 1:
            outgoing, gathered = lax.optimization_barrier((outgoing, gathered))
            later = own_utterances(gathered[1:])
            emission, level = emissions(later.astype(jnp.float32), senone_tiles)
        received = exchange_chips(outgoing)
        values, *tallies, codes = step(
            frame_no, frame_no == frames - 1, indices, received, values, emission, level,
            max(frame_no - 1, 0), tallies, (self_trans, entry_trans),
        )

    scaled, log_like, bad = finish(exchange(codes), values, tallies[0])
    return lax.cond(
        bad[0] == 0.0,
        lambda: (scaled, log_like[0, :utts]),
        lambda: normalised_path(
            start_weights, first, later, self_trans, entry_trans, arc_weight, arc_src, send_ids,
            state_senone,
        ),
    )


def solution(mesh):
    in_specs = (
        P(None, None, "emit"),
        P("emit", "blk"),
        P("blk", None, None),
        P("blk", None, None),
        P("blk", None),
        P("blk", None),
        P(None, "blk", None, None),
        P("blk"),
    )
    out_specs = (P("emit", "blk"), P("emit"))
    return jax.shard_map(local, mesh=mesh, in_specs=in_specs, out_specs=out_specs, check_vma=False)
```

```python
import functools

import jax
import jax.numpy as jnp
from jax import lax
from jax.experimental import pallas as pl
from jax.experimental.pallas import tpu as pltpu
from jax.sharding import PartitionSpec as P

LANES = 128
TOP, BIAS, RATIO, TINY = 65535.0, 32768.0, 2.0**-22, 1e-30
META, PEAK_STEPS = 16, 256.0
MEAN_LOW, MEAN_HIGH = 2.0**-4, 4095.0
VMEM_LIMIT = 48 * 2**20


def exchange(outgoing):
    return lax.all_to_all(outgoing, "blk", split_axis=0, concat_axis=0, tiled=True)


def sum_over_blk(part):
    n_blk = lax.axis_size("blk")
    return jnp.sum(exchange(jnp.broadcast_to(part[None], (n_blk,) + part.shape)), axis=0)


def advance(values, matrices):
    return jnp.einsum("juv,jvw->juw", values, matrices, preferred_element_type=jnp.float32)


def normalised_path(
    start, first, later, self_trans, entry_trans, arc_weight, arc_src, send_ids, state_senone
):
    rows = jnp.concatenate([first[None], later], axis=0)
    slots = send_ids[:, 0, :, 0]
    utt_dev, n_blk = start.shape[0], lax.axis_size("blk")
    blk_dev, block_width = self_trans.shape[:2]
    state_count = blk_dev * block_width * n_blk
    senders = lax.broadcasted_iota(jnp.int32, (1, 1, n_blk), 2)
    arc_values = jnp.where(
        (arc_src // blk_dev)[:, :, None] == senders, arc_weight[:, :, None].astype(jnp.float32), 0.0
    )
    mixing = jnp.sum(arc_values, axis=1).astype(jnp.bfloat16)

    def blocks(values):
        return values.reshape(utt_dev, blk_dev, block_width).transpose(1, 0, 2)

    def frame(frame_no, carry):
        forward, log_like = carry
        sent = forward.astype(jnp.bfloat16)
        padded = jnp.concatenate([sent, jnp.zeros_like(sent[:1])], axis=0)
        outgoing = padded.at[slots[frame_no]].get(mode="promise_in_bounds")
        incoming = exchange(outgoing).reshape(n_blk, utt_dev * block_width)
        inflow = jnp.dot(mixing, incoming, preferred_element_type=jnp.float32)
        inflow = inflow.astype(jnp.bfloat16).reshape(blk_dev, utt_dev, block_width)
        raw_mass = advance(sent, self_trans) + advance(inflow, entry_trans)
        scores = rows[frame_no].at[:, state_senone].get(mode="promise_in_bounds")
        raw_mass = raw_mass * jnp.exp(blocks(scores).astype(jnp.float32))
        mass_sum = sum_over_blk(jnp.sum(raw_mass, axis=(0, 2)))
        forward = raw_mass * (state_count / mass_sum)[None, :, None]
        return forward, log_like + jnp.log(mass_sum / state_count)

    log_like = jnp.zeros((utt_dev,), jnp.float32)
    forward, log_like = lax.fori_loop(0, rows.shape[0], frame, (blocks(start), log_like))
    return forward.transpose(1, 0, 2).reshape(start.shape), log_like


def short(values):
    return values.astype(jnp.int32).astype(jnp.int16)


def wide(codes):
    return codes.astype(jnp.int32).astype(jnp.float32)


def encode(blocks, mean, core, out_ref):
    utts, width = blocks[0].shape
    lane = lax.broadcasted_iota(jnp.int32, (utts, LANES), 1) - core * META
    meta = jnp.zeros((utts, LANES), jnp.float32)
    bad = jnp.where((mean >= MEAN_LOW) & (mean <= MEAN_HIGH), 0.0, 1.0)
    for d, block in enumerate(blocks):
        peak = jnp.max(block, axis=1, keepdims=True)
        least = jnp.min(block, axis=1, keepdims=True)
        bad = jnp.where((least >= peak * RATIO) & (least >= TINY), bad, 1.0)
        steps = jnp.ceil(jnp.log2(peak) * PEAK_STEPS)
        share = block * jnp.exp2(steps * (-1.0 / PEAK_STEPS))
        root = jnp.exp2(jnp.log2(share) * (1.0 / 3.0))
        code = jnp.clip(jnp.round(root * TOP), 0.0, TOP) - BIAS
        out_ref[:, d * width : (d + 1) * width] = short(code)
        meta = jnp.where(lane == d, steps, meta)
    n = len(blocks)
    out_ref[:, n * width : (n + 1) * width] = short(jnp.full((utts, width), -BIAS, jnp.float32))
    rest = mean * 8.0
    for digit in range(3):
        whole = jnp.floor(rest)
        meta = jnp.where(lane == n + digit, whole, meta)
        rest = (rest - whole) * 2.0**15
    out_ref[:, (n + 1) * width :] = short(meta)
    return jnp.broadcast_to(bad, (utts, LANES))


def pack_kernel(width, core_ref, mine_ref, others_ref, own_ref, other_ref, out_ref):
    core = core_ref[0]
    mine_at = pl.multiple_of(core * width, width)
    others_at = pl.multiple_of((1 - core) * width, width)
    with_meta = out_ref.shape[2] > 2 * width
    if with_meta:
        last = slice(own_ref.shape[1] - LANES, own_ref.shape[1])
        meta = short(wide(own_ref[:, last]) + wide(other_ref[:, last]))
    for chip in range(out_ref.shape[0]):
        mine = pl.multiple_of(mine_ref[2 * chip + core] * width, width)
        others = pl.multiple_of(others_ref[2 * chip + core] * width, width)
        out_ref[chip, :, pl.ds(mine_at, width)] = own_ref[:, pl.ds(mine, width)]
        out_ref[chip, :, pl.ds(others_at, width)] = other_ref[:, pl.ds(others, width)]
        if with_meta:
            out_ref[chip, :, 2 * width :] = meta


def pack(width, n_chip, core, mine, others, own, other):
    smem = pl.BlockSpec(memory_space=pltpu.SMEM)
    vmem = pl.BlockSpec(memory_space=pltpu.VMEM)
    return pl.pallas_call(
        functools.partial(pack_kernel, width),
        out_shape=jax.ShapeDtypeStruct(
            (n_chip, own.shape[0], 2 * width + own.shape[1] % width), own.dtype
        ),
        in_specs=[smem] * 3 + [vmem] * 2,
        out_specs=vmem,
        compiler_params=pltpu.CompilerParams(vmem_limit_bytes=VMEM_LIMIT),
        name="pack",
    )(core, mine, others, own, other)


def emission_kernel(rows_ref, senone_ref, emission_ref, level_ref):
    frames, utts, senones = rows_ref.shape
    tiles = senones // LANES
    levels = []
    for frame in range(frames):
        rows = rows_ref[frame]
        top = jnp.max(rows, axis=1, keepdims=True)
        mean = jnp.sum(jnp.exp(rows - top), axis=1, keepdims=True) * (1.0 / senones)
        levels.append(top + jnp.log(mean))
        level_ref[frame] = jnp.broadcast_to(levels[-1], (utts, LANES))

    def packed(pair, n):
        at = slice(n * LANES, (n + 1) * LANES)
        low = rows_ref[2 * pair, :, at] * -16.0
        if 2 * pair + 1 < frames:
            low += rows_ref[2 * pair + 1, :, at] * -32768.0
        return low

    pairs = (frames + 1) // 2

    def groups_at(step, _):
        where = [step * together + n for n in range(together)]
        lanes, places, found = [], [], []
        for state_group in where:
            senone = jnp.broadcast_to(senone_ref[pl.ds(state_group, 1), :], (utts, LANES))
            lanes.append(senone & (LANES - 1))
            places.append(senone >> 7)
            found.append([jnp.zeros((utts, LANES), jnp.float32)] * pairs)
        for n in range(tiles):
            table = [packed(pair, n) for pair in range(pairs)]
            for lane, place, kept in zip(lanes, places, found):
                here = place == n
                for pair in range(pairs):
                    picked = jnp.take_along_axis(
                        table[pair], lane, axis=1, mode="promise_in_bounds"
                    )
                    kept[pair] = jnp.where(here, picked, kept[pair])
        for state_group, kept in zip(where, found):
            at = pl.multiple_of(state_group * LANES, LANES)
            for pair in range(pairs):
                high = jnp.floor(kept[pair] * (1.0 / 2048.0))
                both = (kept[pair] - high * 2048.0, high)
                for frame in range(2 * pair, min(2 * pair + 2, frames)):
                    score = both[frame - 2 * pair] * (-1.0 / 16.0)
                    emission_ref[frame, :, pl.ds(at, LANES)] = jnp.exp(score - levels[frame])
        return 0

    together = 4 if pairs == 1 else 2
    lax.fori_loop(0, senone_ref.shape[0] // together, groups_at, 0)


def emissions(rows, senone_tiles):
    frames, utts, senones = rows.shape
    groups = senone_tiles.shape[0]
    return pl.pallas_call(
        emission_kernel,
        out_shape=(
            jax.ShapeDtypeStruct((frames, utts, groups * LANES), jnp.float32),
            jax.ShapeDtypeStruct((frames, utts, LANES), jnp.float32),
        ),
        compiler_params=pltpu.CompilerParams(vmem_limit_bytes=VMEM_LIMIT),
        cost_estimate=pl.CostEstimate(
            flops=8 * frames * groups * senones * utts, bytes_accessed=2**20,
            transcendentals=frames * groups * utts * LANES,
        ),
        name="emissions",
    )(rows, senone_tiles)


def column_to_row(column):
    n = column.shape[0]
    lane = lax.broadcasted_iota(jnp.int32, (n, LANES), 1)
    place = lax.broadcasted_iota(jnp.int32, (n, LANES), 0)
    return jnp.sum(jnp.where(lane == place, column, 0.0), axis=0, keepdims=True)


def row_to_column(row, n):
    lane = lax.broadcasted_iota(jnp.int32, (n, LANES), 1)
    place = lax.broadcasted_iota(jnp.int32, (n, LANES), 0)
    return jnp.sum(jnp.where(lane == place, row, 0.0), axis=1, keepdims=True)


def step_kernel(
    first, last, streamed, slot, core_ref, owner_ref, local_ref, weight_ref, recv_ref, prev_ref,
    emission_ref, level_ref, log_in_ref, bad_in_ref, self_in, entry_in, raw_ref, log_ref, bad_ref,
    end_ref, *scratch,
):
    n_chip, utts = recv_ref.shape[:2]
    blk_dev, width = self_in.shape[:2]
    arcs = owner_ref.shape[0] // blk_dev
    lane = lax.broadcasted_iota(jnp.int32, (utts, LANES), 1)
    self_ref, entry_ref, copies = self_in, entry_in, []
    if streamed:
        self_ref, entry_ref, arrived = scratch
        for d in range(blk_dev):
            copies.append(
                (
                    pltpu.make_async_copy(self_in.at[d], self_ref.at[d], arrived.at[2 * d]),
                    pltpu.make_async_copy(entry_in.at[d], entry_ref.at[d], arrived.at[2 * d + 1]),
                )
            )
            copies[d][0].start()
            copies[d][1].start()
    log_like = log_in_ref[...] + level_ref[slot]
    if first:
        scale = jnp.ones((utts, 1), jnp.float32)
    else:
        sums = wide(recv_ref[0, :, 2 * width :])
        for chip in range(1, n_chip):
            sums += wide(recv_ref[chip, :, 2 * width :])
        digit = lane % META - blk_dev
        place = jnp.where(
            digit == 0,
            2.0**-3,
            jnp.where(digit == 1, 2.0**-18, jnp.where(digit == 2, 2.0**-33, 0.0)),
        )
        scale = (2.0 * n_chip) / jnp.sum(sums * place, axis=1, keepdims=True)
        log_like = log_like - jnp.log(scale)
    log_ref[...] = log_like
    narrow = jnp.broadcast_to(scale, (utts, LANES)) * TOP**-3
    scale = jnp.broadcast_to(scale, (utts, width))

    def inflow_of(d):
        inflow = jnp.zeros((utts, width), jnp.float32)
        for a in range(arcs):
            owner, block = owner_ref[d * arcs + a], local_ref[d * arcs + a]
            chip, side = owner >> 1, owner & 1
            code = recv_ref[chip, :, pl.ds(pl.multiple_of(side * width, width), width)]
            if first:
                inflow += code.astype(jnp.float32) * weight_ref[d * arcs + a]
                continue
            code = wide(code) + BIAS
            meta = wide(recv_ref[chip, :, 2 * width :])
            at = jnp.full((utts, LANES), side * META + block, jnp.int32)
            steps = jnp.take_along_axis(meta, at, axis=1, mode="promise_in_bounds")
            unit = jnp.exp2(steps * (1.0 / PEAK_STEPS)) * narrow
            unit = jnp.concatenate([unit] * (width // LANES), axis=1)
            sent = (code * unit * code * code).astype(jnp.bfloat16).astype(jnp.float32)
            inflow += sent * weight_ref[d * arcs + a]
        return inflow.astype(jnp.bfloat16)

    blocks = []
    total = jnp.zeros((utts, width), jnp.float32)
    inflow = inflow_of(0)
    for d in range(blk_dev):
        here = slice(d * width, (d + 1) * width)
        own = (prev_ref[:, here] * scale).astype(jnp.bfloat16)
        if streamed:
            copies[d][0].wait()
            copies[d][1].wait()
        raw = jnp.dot(own, self_ref[d], preferred_element_type=jnp.float32)
        after = inflow_of(d + 1) if d + 1 < blk_dev else None
        raw += jnp.dot(inflow, entry_ref[d], preferred_element_type=jnp.float32)
        raw = raw * emission_ref[slot, :, here]
        raw_ref[:, here] = raw
        total += raw
        blocks.append(raw)
        inflow = after
    mean = jnp.sum(total, axis=1, keepdims=True) * (1.0 / (blk_dev * width))
    if last:
        bad_ref[...] = bad_in_ref[...]
        row = column_to_row(mean)
        bad = jnp.max(bad_in_ref[...], axis=0, keepdims=True)
        row = jnp.where(lane[:1] == utts, bad, row)
        end_ref[...] = jnp.broadcast_to(row, end_ref.shape)
    else:
        bad_ref[...] = jnp.maximum(bad_in_ref[...], encode(blocks, mean, core_ref[0], end_ref))


def step(frame_no, last, indices, received, previous, emission, level, slot, tallies, matrices):
    blk_dev, width = matrices[0].shape[:2]
    n_chip = received.shape[0]
    utts, states = previous.shape
    streamed = frame_no < 2
    smem = pl.BlockSpec(memory_space=pltpu.SMEM)
    vmem = pl.BlockSpec(memory_space=pltpu.VMEM)
    matrix = pl.BlockSpec(memory_space=pl.ANY) if streamed else vmem
    end = (2 * n_chip, LANES) if last else (utts, states + width + LANES)
    tile = jax.ShapeDtypeStruct((utts, LANES), jnp.float32)
    scratch = []
    if streamed:
        scratch = [pltpu.VMEM(m.shape, m.dtype) for m in matrices]
        scratch.append(pltpu.SemaphoreType.DMA((2 * blk_dev,)))
    return pl.pallas_call(
        functools.partial(step_kernel, frame_no == 0, last, streamed, slot),
        out_shape=[
            jax.ShapeDtypeStruct((utts, states), jnp.float32),
            tile,
            tile,
            jax.ShapeDtypeStruct(end, jnp.float32 if last else jnp.int16),
        ],
        in_specs=[smem] * 4 + [vmem] * 6 + [matrix] * 2,
        out_specs=[vmem] * 4,
        scratch_shapes=scratch,
        compiler_params=pltpu.CompilerParams(vmem_limit_bytes=VMEM_LIMIT),
        cost_estimate=pl.CostEstimate(
            flops=4 * utts * blk_dev * width**2, bytes_accessed=4 * blk_dev * width**2,
            transcendentals=0,
        ),
        name="step",
    )(*indices, received, previous, emission, level, *tallies, *matrices)


def finish_kernel(recv_ref, raw_ref, log_ref, out_ref, log_row_ref, bad_ref):
    utts = raw_ref.shape[0]
    sums = jnp.sum(recv_ref[...], axis=0, keepdims=True)
    mean = row_to_column(sums, utts) * (1.0 / recv_ref.shape[0])
    out_ref[...] = raw_ref[...] * (1.0 / mean)
    log_row_ref[...] = column_to_row((log_ref[...] + jnp.log(mean))[:, :1])
    lane = lax.broadcasted_iota(jnp.int32, (1, LANES), 1)
    bad_ref[0] = jnp.sum(jnp.where(lane == utts, sums, 0.0))


def finish(received, raw, log_like):
    vmem = pl.BlockSpec(memory_space=pltpu.VMEM)
    return pl.pallas_call(
        finish_kernel,
        out_shape=[
            jax.ShapeDtypeStruct(raw.shape, jnp.float32),
            jax.ShapeDtypeStruct((1, LANES), jnp.float32),
            jax.ShapeDtypeStruct((1,), jnp.float32),
        ],
        in_specs=[vmem] * 3,
        out_specs=[vmem, vmem, pl.BlockSpec(memory_space=pltpu.SMEM)],
        compiler_params=pltpu.CompilerParams(vmem_limit_bytes=VMEM_LIMIT),
        name="finish",
    )(received, raw, log_like)


def local(
    loglike, start_weights, self_trans, entry_trans, arc_weight, arc_src, send_ids, state_senone
):
    n_blk = lax.axis_size("blk")
    n_chip = n_blk // 2
    n_emit = lax.axis_size("emit")
    blk_dev, width = self_trans.shape[:2]
    utts = start_weights.shape[0]
    frames = loglike.shape[0]
    core = lax.axis_index("blk") % 2
    core_no = core.astype(jnp.int32).reshape(1)

    other_core = [(n, n ^ 1) for n in range(n_blk)]
    same_core = [[2 * n + c for n in range(n_chip)] for c in range(2)]

    def swap(x):
        return lax.ppermute(x, "blk", other_core)

    def exchange_chips(x):
        return lax.all_to_all(
            x, "blk", split_axis=0, concat_axis=0, tiled=True, axis_index_groups=same_core
        )

    slots = [send_ids[0, 0, :, 0]]
    other_slots = [swap(slots[0])]

    owners = (arc_src // blk_dev).reshape(-1)
    locals_ = (arc_src % blk_dev).reshape(-1)
    weights = arc_weight.astype(jnp.float32).reshape(-1)
    senone_tiles = state_senone.reshape(-1, LANES)

    def own_utterances(rows):
        return lax.dynamic_slice_in_dim(rows, lax.axis_index("emit") * utts, utts, 1)

    def first_rows(part):
        me = lax.axis_index("emit")
        parts = []
        for ahead in range(n_emit):
            piece = lax.dynamic_slice_in_dim(part, ((me + ahead) % n_emit) * utts, utts, 0)
            if ahead:
                piece = lax.ppermute(
                    piece, "emit", [(n, (n + ahead) % n_emit) for n in range(n_emit)]
                )
            parts.append(piece)
        order = [
            functools.reduce(
                lambda kept, ahead: jnp.where((me - n) % n_emit == ahead, parts[ahead], kept),
                range(1, n_emit),
                parts[0],
            )
            for n in range(n_emit)
        ]
        return jnp.concatenate(order, axis=1)

    values = start_weights
    codes = jnp.concatenate(
        [start_weights.astype(jnp.bfloat16), jnp.zeros((utts, width), jnp.bfloat16)], axis=1
    )
    indices = (core_no, owners, locals_, weights)
    tallies = (jnp.zeros((utts, LANES), jnp.float32),) * 2
    for frame_no in range(frames):
        outgoing = pack(
            width, n_chip, core_no, slots[frame_no], other_slots[frame_no], codes, swap(codes)
        )
        if frame_no == 0:
            outgoing, scores, ids = lax.optimization_barrier((outgoing, loglike, send_ids))
            gathered = lax.all_gather(scores, "emit", axis=2, tiled=True)
            first = first_rows(scores[0])
            ids = ids[1:, 0, :, 0]
            other_ids = swap(ids)
            slots += [ids[n] for n in range(frames - 1)]
            other_slots += [other_ids[n] for n in range(frames - 1)]
            emission, level = emissions(first[None].astype(jnp.float32), senone_tiles)
        if frame_no == 1:
            outgoing, gathered = lax.optimization_barrier((outgoing, gathered))
            later = own_utterances(gathered[1:])
            emission, level = emissions(later.astype(jnp.float32), senone_tiles)
        received = exchange_chips(outgoing)
        values, *tallies, codes = step(
            frame_no, frame_no == frames - 1, indices, received, values, emission, level,
            max(frame_no - 1, 0), tallies, (self_trans, entry_trans),
        )

    scaled, log_like, bad = finish(exchange(codes), values, tallies[0])
    return lax.cond(
        bad[0] == 0.0,
        lambda: (scaled, log_like[0, :utts]),
        lambda: normalised_path(
            start_weights, first, later, self_trans, entry_trans, arc_weight, arc_src, send_ids,
            state_senone,
        ),
    )


def solution(mesh):
    in_specs = (
        P(None, None, "emit"),
        P("emit", "blk"),
        P("blk", None, None),
        P("blk", None, None),
        P("blk", None),
        P("blk", None),
        P(None, "blk", None, None),
        P("blk"),
    )
    out_specs = (P("emit", "blk"), P("emit"))
    return jax.shard_map(local, mesh=mesh, in_specs=in_specs, out_specs=out_specs, check_vma=False)
```

```python
import functools

import jax
import jax.numpy as jnp
from jax import lax
from jax.experimental import pallas as pl
from jax.experimental.pallas import tpu as pltpu
from jax.sharding import PartitionSpec as P

LANES = 128
TOP, BIAS, RATIO, TINY = 65535.0, 32768.0, 2.0**-22, 1e-30
META, PEAK_STEPS = 16, 256.0
MEAN_LOW, MEAN_HIGH = 2.0**-4, 4095.0
VMEM_LIMIT = 48 * 2**20


def exchange(outgoing):
    return lax.all_to_all(outgoing, "blk", split_axis=0, concat_axis=0, tiled=True)


def sum_over_blk(part):
    n_blk = lax.axis_size("blk")
    return jnp.sum(exchange(jnp.broadcast_to(part[None], (n_blk,) + part.shape)), axis=0)


def advance(values, matrices):
    return jnp.einsum("juv,jvw->juw", values, matrices, preferred_element_type=jnp.float32)


def normalised_path(
    start, first, later, self_trans, entry_trans, arc_weight, arc_src, send_ids, state_senone
):
    rows = jnp.concatenate([first[None], later], axis=0)
    slots = send_ids[:, 0, :, 0]
    utt_dev, n_blk = start.shape[0], lax.axis_size("blk")
    blk_dev, block_width = self_trans.shape[:2]
    state_count = blk_dev * block_width * n_blk
    senders = lax.broadcasted_iota(jnp.int32, (1, 1, n_blk), 2)
    arc_values = jnp.where(
        (arc_src // blk_dev)[:, :, None] == senders, arc_weight[:, :, None].astype(jnp.float32), 0.0
    )
    mixing = jnp.sum(arc_values, axis=1).astype(jnp.bfloat16)

    def blocks(values):
        return values.reshape(utt_dev, blk_dev, block_width).transpose(1, 0, 2)

    def frame(frame_no, carry):
        forward, log_like = carry
        sent = forward.astype(jnp.bfloat16)
        padded = jnp.concatenate([sent, jnp.zeros_like(sent[:1])], axis=0)
        outgoing = padded.at[slots[frame_no]].get(mode="promise_in_bounds")
        incoming = exchange(outgoing).reshape(n_blk, utt_dev * block_width)
        inflow = jnp.dot(mixing, incoming, preferred_element_type=jnp.float32)
        inflow = inflow.astype(jnp.bfloat16).reshape(blk_dev, utt_dev, block_width)
        raw_mass = advance(sent, self_trans) + advance(inflow, entry_trans)
        scores = rows[frame_no].at[:, state_senone].get(mode="promise_in_bounds")
        raw_mass = raw_mass * jnp.exp(blocks(scores).astype(jnp.float32))
        mass_sum = sum_over_blk(jnp.sum(raw_mass, axis=(0, 2)))
        forward = raw_mass * (state_count / mass_sum)[None, :, None]
        return forward, log_like + jnp.log(mass_sum / state_count)

    log_like = jnp.zeros((utt_dev,), jnp.float32)
    forward, log_like = lax.fori_loop(0, rows.shape[0], frame, (blocks(start), log_like))
    return forward.transpose(1, 0, 2).reshape(start.shape), log_like


def short(values):
    return values.astype(jnp.int32).astype(jnp.int16)


def wide(codes):
    return codes.astype(jnp.int32).astype(jnp.float32)


def encode(blocks, mean, core, out_ref):
    utts, width = blocks[0].shape
    lane = lax.broadcasted_iota(jnp.int32, (utts, LANES), 1) - core * META
    meta = jnp.zeros((utts, LANES), jnp.float32)
    bad = jnp.where((mean >= MEAN_LOW) & (mean <= MEAN_HIGH), 0.0, 1.0)
    for d, block in enumerate(blocks):
        peak = jnp.max(block, axis=1, keepdims=True)
        least = jnp.min(block, axis=1, keepdims=True)
        bad = jnp.where((least >= peak * RATIO) & (least >= TINY), bad, 1.0)
        steps = jnp.ceil(jnp.log2(peak) * PEAK_STEPS)
        share = block * jnp.exp2(steps * (-1.0 / PEAK_STEPS))
        root = jnp.exp2(jnp.log2(share) * (1.0 / 3.0))
        code = jnp.clip(jnp.round(root * TOP), 0.0, TOP) - BIAS
        out_ref[:, d * width : (d + 1) * width] = short(code)
        meta = jnp.where(lane == d, steps, meta)
    n = len(blocks)
    out_ref[:, n * width : (n + 1) * width] = short(jnp.full((utts, width), -BIAS, jnp.float32))
    rest = mean * 8.0
    for digit in range(3):
        whole = jnp.floor(rest)
        meta = jnp.where(lane == n + digit, whole, meta)
        rest = (rest - whole) * 2.0**15
    out_ref[:, (n + 1) * width :] = short(meta)
    return jnp.broadcast_to(bad, (utts, LANES))


def pack_kernel(width, core_ref, mine_ref, others_ref, own_ref, other_ref, out_ref):
    core = core_ref[0]
    mine_at = pl.multiple_of(core * width, width)
    others_at = pl.multiple_of((1 - core) * width, width)
    with_meta = out_ref.shape[2] > 2 * width
    if with_meta:
        last = slice(own_ref.shape[1] - LANES, own_ref.shape[1])
        meta = short(wide(own_ref[:, last]) + wide(other_ref[:, last]))
    for chip in range(out_ref.shape[0]):
        mine = pl.multiple_of(mine_ref[2 * chip + core] * width, width)
        others = pl.multiple_of(others_ref[2 * chip + core] * width, width)
        out_ref[chip, :, pl.ds(mine_at, width)] = own_ref[:, pl.ds(mine, width)]
        out_ref[chip, :, pl.ds(others_at, width)] = other_ref[:, pl.ds(others, width)]
        if with_meta:
            out_ref[chip, :, 2 * width :] = meta


def pack(width, n_chip, core, mine, others, own, other):
    smem = pl.BlockSpec(memory_space=pltpu.SMEM)
    vmem = pl.BlockSpec(memory_space=pltpu.VMEM)
    return pl.pallas_call(
        functools.partial(pack_kernel, width),
        out_shape=jax.ShapeDtypeStruct(
            (n_chip, own.shape[0], 2 * width + own.shape[1] % width), own.dtype
        ),
        in_specs=[smem] * 3 + [vmem] * 2,
        out_specs=vmem,
        compiler_params=pltpu.CompilerParams(vmem_limit_bytes=VMEM_LIMIT),
        name="pack",
    )(core, mine, others, own, other)


def emission_kernel(rows_ref, senone_ref, emission_ref, level_ref):
    frames, utts, senones = rows_ref.shape
    tiles = senones // LANES
    levels = []
    for frame in range(frames):
        rows = rows_ref[frame]
        top = jnp.max(rows, axis=1, keepdims=True)
        mean = jnp.sum(jnp.exp(rows - top), axis=1, keepdims=True) * (1.0 / senones)
        levels.append(top + jnp.log(mean))
        level_ref[frame] = jnp.broadcast_to(levels[-1], (utts, LANES))

    def packed(pair, n):
        at = slice(n * LANES, (n + 1) * LANES)
        low = rows_ref[2 * pair, :, at] * -16.0
        if 2 * pair + 1 < frames:
            low += rows_ref[2 * pair + 1, :, at] * -32768.0
        return low

    pairs = (frames + 1) // 2

    def group(state_group, _):
        senone = jnp.broadcast_to(senone_ref[pl.ds(state_group, 1), :], (utts, LANES))
        lane = senone & (LANES - 1)
        tile = senone >> 7
        found = [jnp.zeros((utts, LANES), jnp.float32)] * pairs
        for n in range(tiles):
            here = tile == n
            for pair in range(pairs):
                picked = jnp.take_along_axis(
                    packed(pair, n), lane, axis=1, mode="promise_in_bounds"
                )
                found[pair] = jnp.where(here, picked, found[pair])
        at = pl.multiple_of(state_group * LANES, LANES)
        for pair in range(pairs):
            high = jnp.floor(found[pair] * (1.0 / 2048.0))
            both = (found[pair] - high * 2048.0, high)
            for frame in range(2 * pair, min(2 * pair + 2, frames)):
                score = both[frame - 2 * pair] * (-1.0 / 16.0)
                emission_ref[frame, :, pl.ds(at, LANES)] = jnp.exp(score - levels[frame])
        return 0

    lax.fori_loop(0, senone_ref.shape[0], group, 0)


def emissions(rows, senone_tiles):
    frames, utts, senones = rows.shape
    groups = senone_tiles.shape[0]
    return pl.pallas_call(
        emission_kernel,
        out_shape=(
            jax.ShapeDtypeStruct((frames, utts, groups * LANES), jnp.float32),
            jax.ShapeDtypeStruct((frames, utts, LANES), jnp.float32),
        ),
        compiler_params=pltpu.CompilerParams(vmem_limit_bytes=VMEM_LIMIT),
        cost_estimate=pl.CostEstimate(
            flops=8 * frames * groups * senones * utts, bytes_accessed=2**20,
            transcendentals=frames * groups * utts * LANES,
        ),
        name="emissions",
    )(rows, senone_tiles)


def column_to_row(column):
    n = column.shape[0]
    lane = lax.broadcasted_iota(jnp.int32, (n, LANES), 1)
    place = lax.broadcasted_iota(jnp.int32, (n, LANES), 0)
    return jnp.sum(jnp.where(lane == place, column, 0.0), axis=0, keepdims=True)


def row_to_column(row, n):
    lane = lax.broadcasted_iota(jnp.int32, (n, LANES), 1)
    place = lax.broadcasted_iota(jnp.int32, (n, LANES), 0)
    return jnp.sum(jnp.where(lane == place, row, 0.0), axis=1, keepdims=True)


def step_kernel(
    first, last, streamed, slot, core_ref, arc_ref, weight_ref, recv_ref, prev_ref, emission_ref,
    level_ref, log_in_ref, bad_in_ref, self_in, entry_in, raw_ref, log_ref, bad_ref,
    end_ref, *scratch,
):
    n_chip, utts = recv_ref.shape[:2]
    blk_dev, width = self_in.shape[:2]
    arcs = arc_ref.shape[1]
    lane = lax.broadcasted_iota(jnp.int32, (utts, LANES), 1)
    self_ref, entry_ref, copies = self_in, entry_in, []
    if streamed:
        self_ref, entry_ref, arrived = scratch
        for d in range(blk_dev):
            pairs = [(entry_in, entry_ref)] if first else [(self_in, self_ref), (entry_in, entry_ref)]
            copies.append(
                [
                    pltpu.make_async_copy(src.at[d], dst.at[d], arrived.at[2 * d + n])
                    for n, (src, dst) in enumerate(pairs)
                ]
            )
            for copy in copies[d]:
                copy.start()
    log_like = log_in_ref[...] + level_ref[slot]
    if first:
        scale = jnp.ones((utts, 1), jnp.float32)
    else:
        sums = wide(recv_ref[0, :, 2 * width :])
        for chip in range(1, n_chip):
            sums += wide(recv_ref[chip, :, 2 * width :])
        digit = lane % META - blk_dev
        place = jnp.where(
            digit == 0,
            2.0**-3,
            jnp.where(digit == 1, 2.0**-18, jnp.where(digit == 2, 2.0**-33, 0.0)),
        )
        scale = (2.0 * n_chip) / jnp.sum(sums * place, axis=1, keepdims=True)
        log_like = log_like - jnp.log(scale)
    log_ref[...] = log_like
    narrow = jnp.broadcast_to(scale, (utts, LANES)) * TOP**-3
    scale = jnp.broadcast_to(scale, (utts, width))

    def inflow_of(d):
        inflow = jnp.zeros((utts, width), jnp.float32)
        for a in range(arcs):
            owner, block = lax.div(arc_ref[d, a], blk_dev), lax.rem(arc_ref[d, a], blk_dev)
            chip, side = owner >> 1, owner & 1
            code = recv_ref[chip, :, pl.ds(pl.multiple_of(side * width, width), width)]
            if first:
                inflow += code.astype(jnp.float32) * weight_ref[d, a]
                continue
            code = wide(code) + BIAS
            meta = wide(recv_ref[chip, :, 2 * width :])
            at = jnp.full((utts, LANES), side * META + block, jnp.int32)
            steps = jnp.take_along_axis(meta, at, axis=1, mode="promise_in_bounds")
            unit = jnp.exp2(steps * (1.0 / PEAK_STEPS)) * narrow
            unit = jnp.concatenate([unit] * (width // LANES), axis=1)
            sent = (code * unit * code * code).astype(jnp.bfloat16).astype(jnp.float32)
            inflow += sent * weight_ref[d, a]
        return inflow.astype(jnp.bfloat16)

    blocks = []
    total = jnp.zeros((utts, width), jnp.float32)
    inflow = inflow_of(0)
    for d in range(blk_dev):
        here = slice(d * width, (d + 1) * width)
        if streamed:
            for copy in copies[d]:
                copy.wait()
        if first:
            raw = prev_ref[:, here]
        else:
            own = (prev_ref[:, here] * scale).astype(jnp.bfloat16)
            raw = jnp.dot(own, self_ref[d], preferred_element_type=jnp.float32)
        after = inflow_of(d + 1) if d + 1 < blk_dev else None
        raw += jnp.dot(inflow, entry_ref[d], preferred_element_type=jnp.float32)
        raw = raw * emission_ref[slot, :, here]
        raw_ref[:, here] = raw
        total += raw
        blocks.append(raw)
        inflow = after
    mean = jnp.sum(total, axis=1, keepdims=True) * (1.0 / (blk_dev * width))
    if last:
        bad_ref[...] = bad_in_ref[...]
        row = column_to_row(mean)
        bad = jnp.max(bad_in_ref[...], axis=0, keepdims=True)
        row = jnp.where(lane[:1] == utts, bad, row)
        end_ref[...] = jnp.broadcast_to(row, end_ref.shape)
    else:
        bad_ref[...] = jnp.maximum(bad_in_ref[...], encode(blocks, mean, core_ref[0], end_ref))


def step(frame_no, last, indices, received, previous, emission, level, slot, tallies, matrices):
    blk_dev, width = matrices[0].shape[:2]
    n_chip = received.shape[0]
    utts, states = previous.shape
    streamed = frame_no < 2
    smem = pl.BlockSpec(memory_space=pltpu.SMEM)
    vmem = pl.BlockSpec(memory_space=pltpu.VMEM)
    matrix = pl.BlockSpec(memory_space=pl.ANY) if streamed else vmem
    end = (2 * n_chip, LANES) if last else (utts, states + width + LANES)
    tile = jax.ShapeDtypeStruct((utts, LANES), jnp.float32)
    scratch = []
    if streamed:
        scratch = [pltpu.VMEM(m.shape, m.dtype) for m in matrices]
        scratch.append(pltpu.SemaphoreType.DMA((2 * blk_dev,)))
    return pl.pallas_call(
        functools.partial(step_kernel, frame_no == 0, last, streamed, slot),
        out_shape=[
            jax.ShapeDtypeStruct((utts, states), jnp.float32),
            tile,
            tile,
            jax.ShapeDtypeStruct(end, jnp.float32 if last else jnp.int16),
        ],
        in_specs=[smem] * 3 + [vmem] * 6 + [matrix] * 2,
        out_specs=[vmem] * 4,
        scratch_shapes=scratch,
        compiler_params=pltpu.CompilerParams(vmem_limit_bytes=VMEM_LIMIT),
        cost_estimate=pl.CostEstimate(
            flops=4 * utts * blk_dev * width**2, bytes_accessed=4 * blk_dev * width**2,
            transcendentals=0,
        ),
        name="step",
    )(*indices, received, previous, emission, level, *tallies, *matrices)


def own_kernel(start_ref, self_ref, out_ref):
    out_ref[...] = jnp.dot(start_ref[...], self_ref[0], preferred_element_type=jnp.float32)


def own_product(start, self_trans):
    blk_dev, width = self_trans.shape[:2]
    utts = start.shape[0]
    block = pl.BlockSpec((utts, width), lambda d: (0, d))
    return pl.pallas_call(
        own_kernel,
        out_shape=jax.ShapeDtypeStruct((utts, blk_dev * width), jnp.float32),
        grid=(blk_dev,),
        in_specs=[block, pl.BlockSpec((1, width, width), lambda d: (d, 0, 0))],
        out_specs=block,
        compiler_params=pltpu.CompilerParams(vmem_limit_bytes=VMEM_LIMIT),
        cost_estimate=pl.CostEstimate(
            flops=2 * utts * blk_dev * width**2, bytes_accessed=2 * blk_dev * width**2,
            transcendentals=0,
        ),
        name="own",
    )(start, self_trans)


def finish_kernel(recv_ref, raw_ref, log_ref, out_ref, log_row_ref, bad_ref):
    utts = raw_ref.shape[0]
    sums = jnp.sum(recv_ref[...], axis=0, keepdims=True)
    mean = row_to_column(sums, utts) * (1.0 / recv_ref.shape[0])
    out_ref[...] = raw_ref[...] * (1.0 / mean)
    log_row_ref[...] = column_to_row((log_ref[...] + jnp.log(mean))[:, :1])
    lane = lax.broadcasted_iota(jnp.int32, (1, LANES), 1)
    bad_ref[0] = jnp.sum(jnp.where(lane == utts, sums, 0.0))


def finish(received, raw, log_like):
    vmem = pl.BlockSpec(memory_space=pltpu.VMEM)
    return pl.pallas_call(
        finish_kernel,
        out_shape=[
            jax.ShapeDtypeStruct(raw.shape, jnp.float32),
            jax.ShapeDtypeStruct((1, LANES), jnp.float32),
            jax.ShapeDtypeStruct((1,), jnp.float32),
        ],
        in_specs=[vmem] * 3,
        out_specs=[vmem, vmem, pl.BlockSpec(memory_space=pltpu.SMEM)],
        compiler_params=pltpu.CompilerParams(vmem_limit_bytes=VMEM_LIMIT),
        name="finish",
    )(received, raw, log_like)


def local(
    loglike, start_weights, self_trans, entry_trans, arc_weight, arc_src, send_ids, state_senone
):
    n_blk = lax.axis_size("blk")
    n_chip = n_blk // 2
    n_emit = lax.axis_size("emit")
    blk_dev, width = self_trans.shape[:2]
    utts = start_weights.shape[0]
    frames = loglike.shape[0]
    core = lax.axis_index("blk") % 2
    core_no = core.astype(jnp.int32).reshape(1)

    other_core = [(n, n ^ 1) for n in range(n_blk)]
    same_core = [[2 * n + c for n in range(n_chip)] for c in range(2)]

    def swap(x):
        return lax.ppermute(x, "blk", other_core)

    def exchange_chips(x):
        return lax.all_to_all(
            x, "blk", split_axis=0, concat_axis=0, tiled=True, axis_index_groups=same_core
        )

    slots = [send_ids[0, 0, :, 0]]
    other_slots = [swap(slots[0])]

    senone_tiles = state_senone.reshape(-1, LANES)

    def own_utterances(rows):
        return lax.dynamic_slice_in_dim(rows, lax.axis_index("emit") * utts, utts, 1)

    def first_rows(part):
        me = lax.axis_index("emit")
        parts = []
        for ahead in range(n_emit):
            piece = lax.dynamic_slice_in_dim(part, ((me + ahead) % n_emit) * utts, utts, 0)
            if ahead:
                piece = lax.ppermute(
                    piece, "emit", [(n, (n + ahead) % n_emit) for n in range(n_emit)]
                )
            parts.append(piece)
        order = [
            functools.reduce(
                lambda kept, ahead: jnp.where((me - n) % n_emit == ahead, parts[ahead], kept),
                range(1, n_emit),
                parts[0],
            )
            for n in range(n_emit)
        ]
        return jnp.concatenate(order, axis=1)

    codes = jnp.concatenate(
        [start_weights.astype(jnp.bfloat16), jnp.zeros((utts, width), jnp.bfloat16)], axis=1
    )
    gathered = lax.all_gather(loglike, "emit", axis=2, tiled=True)
    indices = (core_no, arc_src, arc_weight.astype(jnp.float32))
    tallies = (jnp.zeros((utts, LANES), jnp.float32),) * 2
    for frame_no in range(frames):
        outgoing = pack(
            width, n_chip, core_no, slots[frame_no], other_slots[frame_no], codes, swap(codes)
        )
        if frame_no == 0:
            outgoing, scores, ids = lax.optimization_barrier((outgoing, loglike, send_ids))
            values = own_product(codes, self_trans)
            first = first_rows(scores[0])
            ids = ids[1:, 0, :, 0]
            other_ids = swap(ids)
            slots += [ids[n] for n in range(frames - 1)]
            other_slots += [other_ids[n] for n in range(frames - 1)]
            emission, level = emissions(first[None].astype(jnp.float32), senone_tiles)
        if frame_no == 1:
            outgoing, gathered = lax.optimization_barrier((outgoing, gathered))
            later = own_utterances(gathered[1:])
            emission, level = emissions(later.astype(jnp.float32), senone_tiles)
        received = exchange_chips(outgoing)
        values, *tallies, codes = step(
            frame_no, frame_no == frames - 1, indices, received, values, emission, level,
            max(frame_no - 1, 0), tallies, (self_trans, entry_trans),
        )

    scaled, log_like, bad = finish(exchange(codes), values, tallies[0])
    return lax.cond(
        bad[0] == 0.0,
        lambda: (scaled, log_like[0, :utts]),
        lambda: normalised_path(
            start_weights, first, later, self_trans, entry_trans, arc_weight, arc_src, send_ids,
            state_senone,
        ),
    )


def solution(mesh):
    in_specs = (
        P(None, None, "emit"),
        P("emit", "blk"),
        P("blk", None, None),
        P("blk", None, None),
        P("blk", None),
        P("blk", None),
        P(None, "blk", None, None),
        P("blk"),
    )
    out_specs = (P("emit", "blk"), P("emit"))
    return jax.shard_map(local, mesh=mesh, in_specs=in_specs, out_specs=out_specs, check_vma=False)
```

```python
import functools

import jax
import jax.numpy as jnp
from jax import lax
from jax.experimental import pallas as pl
from jax.experimental.pallas import tpu as pltpu
from jax.sharding import PartitionSpec as P

LANES = 128
TOP, BIAS, RATIO, TINY = 65535.0, 32768.0, 2.0**-22, 1e-30
META, PEAK_STEPS = 16, 256.0
MEAN_LOW, MEAN_HIGH = 2.0**-4, 4095.0
VMEM_LIMIT = 48 * 2**20


def exchange(outgoing):
    return lax.all_to_all(outgoing, "blk", split_axis=0, concat_axis=0, tiled=True)


def sum_over_blk(part):
    n_blk = lax.axis_size("blk")
    return jnp.sum(exchange(jnp.broadcast_to(part[None], (n_blk,) + part.shape)), axis=0)


def advance(values, matrices):
    return jnp.einsum("juv,jvw->juw", values, matrices, preferred_element_type=jnp.float32)


def normalised_path(
    start, first, later, self_trans, entry_trans, arc_weight, arc_src, send_ids, state_senone
):
    rows = jnp.concatenate([first[None], later], axis=0)
    slots = send_ids[:, 0, :, 0]
    utt_dev, n_blk = start.shape[0], lax.axis_size("blk")
    blk_dev, block_width = self_trans.shape[:2]
    state_count = blk_dev * block_width * n_blk
    senders = lax.broadcasted_iota(jnp.int32, (1, 1, n_blk), 2)
    arc_values = jnp.where(
        (arc_src // blk_dev)[:, :, None] == senders, arc_weight[:, :, None].astype(jnp.float32), 0.0
    )
    mixing = jnp.sum(arc_values, axis=1).astype(jnp.bfloat16)

    def blocks(values):
        return values.reshape(utt_dev, blk_dev, block_width).transpose(1, 0, 2)

    def frame(frame_no, carry):
        forward, log_like = carry
        sent = forward.astype(jnp.bfloat16)
        padded = jnp.concatenate([sent, jnp.zeros_like(sent[:1])], axis=0)
        outgoing = padded.at[slots[frame_no]].get(mode="promise_in_bounds")
        incoming = exchange(outgoing).reshape(n_blk, utt_dev * block_width)
        inflow = jnp.dot(mixing, incoming, preferred_element_type=jnp.float32)
        inflow = inflow.astype(jnp.bfloat16).reshape(blk_dev, utt_dev, block_width)
        raw_mass = advance(sent, self_trans) + advance(inflow, entry_trans)
        scores = rows[frame_no].at[:, state_senone].get(mode="promise_in_bounds")
        raw_mass = raw_mass * jnp.exp(blocks(scores).astype(jnp.float32))
        mass_sum = sum_over_blk(jnp.sum(raw_mass, axis=(0, 2)))
        forward = raw_mass * (state_count / mass_sum)[None, :, None]
        return forward, log_like + jnp.log(mass_sum / state_count)

    log_like = jnp.zeros((utt_dev,), jnp.float32)
    forward, log_like = lax.fori_loop(0, rows.shape[0], frame, (blocks(start), log_like))
    return forward.transpose(1, 0, 2).reshape(start.shape), log_like


def short(values):
    return values.astype(jnp.int32).astype(jnp.int16)


def wide(codes):
    return codes.astype(jnp.int32).astype(jnp.float32)


def encode(blocks, mean, core, out_ref):
    utts, width = blocks[0].shape
    lane = lax.broadcasted_iota(jnp.int32, (utts, LANES), 1) - core * META
    meta = jnp.zeros((utts, LANES), jnp.float32)
    bad = jnp.where((mean >= MEAN_LOW) & (mean <= MEAN_HIGH), 0.0, 1.0)
    for d, block in enumerate(blocks):
        peak = jnp.max(block, axis=1, keepdims=True)
        least = jnp.min(block, axis=1, keepdims=True)
        bad = jnp.where((least >= peak * RATIO) & (least >= TINY), bad, 1.0)
        steps = jnp.ceil(jnp.log2(peak) * PEAK_STEPS)
        share = block * jnp.exp2(steps * (-1.0 / PEAK_STEPS))
        root = jnp.exp2(jnp.log2(share) * (1.0 / 3.0))
        code = jnp.clip(jnp.round(root * TOP), 0.0, TOP) - BIAS
        out_ref[:, d * width : (d + 1) * width] = short(code)
        meta = jnp.where(lane == d, steps, meta)
    n = len(blocks)
    out_ref[:, n * width : (n + 1) * width] = short(jnp.full((utts, width), -BIAS, jnp.float32))
    rest = mean * 8.0
    for digit in range(3):
        whole = jnp.floor(rest)
        meta = jnp.where(lane == n + digit, whole, meta)
        rest = (rest - whole) * 2.0**15
    out_ref[:, (n + 1) * width :] = short(meta)
    return jnp.broadcast_to(bad, (utts, LANES))


def pack_kernel(width, core_ref, mine_ref, others_ref, own_ref, other_ref, out_ref):
    core = core_ref[0]
    mine_at = pl.multiple_of(core * width, width)
    others_at = pl.multiple_of((1 - core) * width, width)
    with_meta = out_ref.shape[2] > 2 * width
    if with_meta:
        last = slice(own_ref.shape[1] - LANES, own_ref.shape[1])
        meta = short(wide(own_ref[:, last]) + wide(other_ref[:, last]))
    for chip in range(out_ref.shape[0]):
        mine = pl.multiple_of(mine_ref[2 * chip + core] * width, width)
        others = pl.multiple_of(others_ref[2 * chip + core] * width, width)
        out_ref[chip, :, pl.ds(mine_at, width)] = own_ref[:, pl.ds(mine, width)]
        out_ref[chip, :, pl.ds(others_at, width)] = other_ref[:, pl.ds(others, width)]
        if with_meta:
            out_ref[chip, :, 2 * width :] = meta


def pack(width, n_chip, core, mine, others, own, other):
    smem = pl.BlockSpec(memory_space=pltpu.SMEM)
    vmem = pl.BlockSpec(memory_space=pltpu.VMEM)
    return pl.pallas_call(
        functools.partial(pack_kernel, width),
        out_shape=jax.ShapeDtypeStruct(
            (n_chip, own.shape[0], 2 * width + own.shape[1] % width), own.dtype
        ),
        in_specs=[smem] * 3 + [vmem] * 2,
        out_specs=vmem,
        compiler_params=pltpu.CompilerParams(vmem_limit_bytes=VMEM_LIMIT),
        name="pack",
    )(core, mine, others, own, other)


def emission_kernel(rows_ref, senone_ref, emission_ref, level_ref):
    frames, utts, senones = rows_ref.shape
    tiles = senones // LANES
    levels = []
    for frame in range(frames):
        rows = rows_ref[frame]
        top = jnp.max(rows, axis=1, keepdims=True)
        mean = jnp.sum(jnp.exp(rows - top), axis=1, keepdims=True) * (1.0 / senones)
        levels.append(top + jnp.log(mean))
        level_ref[frame] = jnp.broadcast_to(levels[-1], (utts, LANES))

    def packed(pair, n):
        at = slice(n * LANES, (n + 1) * LANES)
        low = rows_ref[2 * pair, :, at] * -16.0
        if 2 * pair + 1 < frames:
            low += rows_ref[2 * pair + 1, :, at] * -32768.0
        return low

    pairs = (frames + 1) // 2

    def group(state_group, _):
        senone = jnp.broadcast_to(senone_ref[pl.ds(state_group, 1), :], (utts, LANES))
        lane = senone & (LANES - 1)
        tile = senone >> 7
        found = [jnp.zeros((utts, LANES), jnp.float32)] * pairs
        for n in range(tiles):
            here = tile == n
            for pair in range(pairs):
                picked = jnp.take_along_axis(
                    packed(pair, n), lane, axis=1, mode="promise_in_bounds"
                )
                found[pair] = jnp.where(here, picked, found[pair])
        at = pl.multiple_of(state_group * LANES, LANES)
        for pair in range(pairs):
            high = jnp.floor(found[pair] * (1.0 / 2048.0))
            both = (found[pair] - high * 2048.0, high)
            for frame in range(2 * pair, min(2 * pair + 2, frames)):
                score = both[frame - 2 * pair] * (-1.0 / 16.0)
                emission_ref[frame, :, pl.ds(at, LANES)] = jnp.exp(score - levels[frame])
        return 0

    lax.fori_loop(0, senone_ref.shape[0], group, 0)


def emissions(rows, senone_tiles):
    frames, utts, senones = rows.shape
    groups = senone_tiles.shape[0]
    return pl.pallas_call(
        emission_kernel,
        out_shape=(
            jax.ShapeDtypeStruct((frames, utts, groups * LANES), jnp.float32),
            jax.ShapeDtypeStruct((frames, utts, LANES), jnp.float32),
        ),
        compiler_params=pltpu.CompilerParams(vmem_limit_bytes=VMEM_LIMIT),
        cost_estimate=pl.CostEstimate(
            flops=8 * frames * groups * senones * utts, bytes_accessed=2**20,
            transcendentals=frames * groups * utts * LANES,
        ),
        name="emissions",
    )(rows, senone_tiles)


def column_to_row(column):
    n = column.shape[0]
    lane = lax.broadcasted_iota(jnp.int32, (n, LANES), 1)
    place = lax.broadcasted_iota(jnp.int32, (n, LANES), 0)
    return jnp.sum(jnp.where(lane == place, column, 0.0), axis=0, keepdims=True)


def row_to_column(row, n):
    lane = lax.broadcasted_iota(jnp.int32, (n, LANES), 1)
    place = lax.broadcasted_iota(jnp.int32, (n, LANES), 0)
    return jnp.sum(jnp.where(lane == place, row, 0.0), axis=1, keepdims=True)


def step_kernel(
    first, last, streamed, slot, core_ref, arc_ref, weight_ref, recv_ref, prev_ref, emission_ref,
    level_ref, log_in_ref, bad_in_ref, self_in, entry_in, raw_ref, log_ref, bad_ref,
    end_ref, *scratch,
):
    n_chip, utts = recv_ref.shape[:2]
    blk_dev, width = self_in.shape[:2]
    arcs = arc_ref.shape[1]
    bits = blk_dev.bit_length() - 1
    lane = lax.broadcasted_iota(jnp.int32, (utts, LANES), 1)
    self_ref, entry_ref, copies = self_in, entry_in, []
    if streamed:
        self_ref, entry_ref, arrived = scratch
        for d in range(blk_dev):
            pairs = [(entry_in, entry_ref)] if first else [(self_in, self_ref), (entry_in, entry_ref)]
            copies.append(
                [
                    pltpu.make_async_copy(src.at[d], dst.at[d], arrived.at[2 * d + n])
                    for n, (src, dst) in enumerate(pairs)
                ]
            )
            for copy in copies[d]:
                copy.start()
    log_like = log_in_ref[...] + level_ref[slot]
    if first:
        scale = jnp.ones((utts, 1), jnp.float32)
    else:
        sums = wide(recv_ref[0, :, 2 * width :])
        for chip in range(1, n_chip):
            sums += wide(recv_ref[chip, :, 2 * width :])
        digit = lane % META - blk_dev
        place = jnp.where(
            digit == 0,
            2.0**-3,
            jnp.where(digit == 1, 2.0**-18, jnp.where(digit == 2, 2.0**-33, 0.0)),
        )
        scale = (2.0 * n_chip) / jnp.sum(sums * place, axis=1, keepdims=True)
        log_like = log_like - jnp.log(scale)
    log_ref[...] = log_like
    narrow = jnp.broadcast_to(scale, (utts, LANES)) * TOP**-3
    scale = jnp.broadcast_to(scale, (utts, width))

    def inflow_of(d):
        inflow = jnp.zeros((utts, width), jnp.float32)
        for a in range(arcs):
            source = arc_ref[d, a]
            chip, side, block = source >> (bits + 1), (source >> bits) & 1, source & (blk_dev - 1)
            code = recv_ref[chip, :, pl.ds(pl.multiple_of(side * width, width), width)]
            if first:
                inflow += code.astype(jnp.float32) * weight_ref[d, a]
                continue
            code = wide(code) + BIAS
            meta = wide(recv_ref[chip, :, 2 * width :])
            at = jnp.full((utts, LANES), side * META + block, jnp.int32)
            steps = jnp.take_along_axis(meta, at, axis=1, mode="promise_in_bounds")
            unit = jnp.exp2(steps * (1.0 / PEAK_STEPS)) * narrow
            unit = jnp.concatenate([unit] * (width // LANES), axis=1)
            sent = (code * unit * code * code).astype(jnp.bfloat16).astype(jnp.float32)
            inflow += sent * weight_ref[d, a]
        return inflow.astype(jnp.bfloat16)

    blocks = []
    total = jnp.zeros((utts, width), jnp.float32)
    inflow = inflow_of(0)
    for d in range(blk_dev):
        here = slice(d * width, (d + 1) * width)
        if streamed:
            for copy in copies[d]:
                copy.wait()
        if first:
            raw = prev_ref[:, here]
        else:
            own = (prev_ref[:, here] * scale).astype(jnp.bfloat16)
            raw = jnp.dot(own, self_ref[d], preferred_element_type=jnp.float32)
        after = inflow_of(d + 1) if d + 1 < blk_dev else None
        raw += jnp.dot(inflow, entry_ref[d], preferred_element_type=jnp.float32)
        raw = raw * emission_ref[slot, :, here]
        raw_ref[:, here] = raw
        total += raw
        blocks.append(raw)
        inflow = after
    mean = jnp.sum(total, axis=1, keepdims=True) * (1.0 / (blk_dev * width))
    if last:
        bad_ref[...] = bad_in_ref[...]
        row = column_to_row(mean)
        bad = jnp.max(bad_in_ref[...], axis=0, keepdims=True)
        row = jnp.where(lane[:1] == utts, bad, row)
        end_ref[...] = jnp.broadcast_to(row, end_ref.shape)
    else:
        bad_ref[...] = jnp.maximum(bad_in_ref[...], encode(blocks, mean, core_ref[0], end_ref))


def step(frame_no, last, indices, received, previous, emission, level, slot, tallies, matrices):
    blk_dev, width = matrices[0].shape[:2]
    n_chip = received.shape[0]
    utts, states = previous.shape
    streamed = frame_no < 2
    smem = pl.BlockSpec(memory_space=pltpu.SMEM)
    vmem = pl.BlockSpec(memory_space=pltpu.VMEM)
    matrix = pl.BlockSpec(memory_space=pl.ANY) if streamed else vmem
    end = (2 * n_chip, LANES) if last else (utts, states + width + LANES)
    tile = jax.ShapeDtypeStruct((utts, LANES), jnp.float32)
    scratch = []
    if streamed:
        scratch = [pltpu.VMEM(m.shape, m.dtype) for m in matrices]
        scratch.append(pltpu.SemaphoreType.DMA((2 * blk_dev,)))
    return pl.pallas_call(
        functools.partial(step_kernel, frame_no == 0, last, streamed, slot),
        out_shape=[
            jax.ShapeDtypeStruct((utts, states), jnp.float32),
            tile,
            tile,
            jax.ShapeDtypeStruct(end, jnp.float32 if last else jnp.int16),
        ],
        in_specs=[smem] * 3 + [vmem] * 6 + [matrix] * 2,
        out_specs=[vmem] * 4,
        scratch_shapes=scratch,
        compiler_params=pltpu.CompilerParams(vmem_limit_bytes=VMEM_LIMIT),
        cost_estimate=pl.CostEstimate(
            flops=4 * utts * blk_dev * width**2, bytes_accessed=4 * blk_dev * width**2,
            transcendentals=0,
        ),
        name="step",
    )(*indices, received, previous, emission, level, *tallies, *matrices)


def own_kernel(start_ref, self_ref, after_ref, out_ref):
    del after_ref
    out_ref[...] = jnp.dot(start_ref[...], self_ref[0], preferred_element_type=jnp.float32)


def own_product(start, self_trans, after):
    blk_dev, width = self_trans.shape[:2]
    utts = start.shape[0]
    block = pl.BlockSpec((utts, width), lambda d: (0, d))
    return pl.pallas_call(
        own_kernel,
        out_shape=jax.ShapeDtypeStruct((utts, blk_dev * width), jnp.float32),
        grid=(blk_dev,),
        in_specs=[
            block,
            pl.BlockSpec((1, width, width), lambda d: (d, 0, 0)),
            pl.BlockSpec(memory_space=pl.ANY),
        ],
        out_specs=block,
        compiler_params=pltpu.CompilerParams(vmem_limit_bytes=VMEM_LIMIT),
        cost_estimate=pl.CostEstimate(
            flops=2 * utts * blk_dev * width**2, bytes_accessed=2 * blk_dev * width**2,
            transcendentals=0,
        ),
        name="own",
    )(start, self_trans, after)


def finish_kernel(recv_ref, raw_ref, log_ref, out_ref, log_row_ref, bad_ref):
    utts = raw_ref.shape[0]
    sums = jnp.sum(recv_ref[...], axis=0, keepdims=True)
    mean = row_to_column(sums, utts) * (1.0 / recv_ref.shape[0])
    out_ref[...] = raw_ref[...] * (1.0 / mean)
    log_row_ref[...] = column_to_row((log_ref[...] + jnp.log(mean))[:, :1])
    lane = lax.broadcasted_iota(jnp.int32, (1, LANES), 1)
    bad_ref[0] = jnp.sum(jnp.where(lane == utts, sums, 0.0))


def finish(received, raw, log_like):
    vmem = pl.BlockSpec(memory_space=pltpu.VMEM)
    return pl.pallas_call(
        finish_kernel,
        out_shape=[
            jax.ShapeDtypeStruct(raw.shape, jnp.float32),
            jax.ShapeDtypeStruct((1, LANES), jnp.float32),
            jax.ShapeDtypeStruct((1,), jnp.float32),
        ],
        in_specs=[vmem] * 3,
        out_specs=[vmem, vmem, pl.BlockSpec(memory_space=pltpu.SMEM)],
        compiler_params=pltpu.CompilerParams(vmem_limit_bytes=VMEM_LIMIT),
        name="finish",
    )(received, raw, log_like)


def local(
    loglike, start_weights, self_trans, entry_trans, arc_weight, arc_src, send_ids, state_senone
):
    n_blk = lax.axis_size("blk")
    n_chip = n_blk // 2
    n_emit = lax.axis_size("emit")
    blk_dev, width = self_trans.shape[:2]
    utts = start_weights.shape[0]
    frames = loglike.shape[0]
    core = lax.axis_index("blk") % 2
    core_no = core.astype(jnp.int32).reshape(1)

    other_core = [(n, n ^ 1) for n in range(n_blk)]
    same_core = [[2 * n + c for n in range(n_chip)] for c in range(2)]

    def swap(x):
        return lax.ppermute(x, "blk", other_core)

    def exchange_chips(x):
        return lax.all_to_all(
            x, "blk", split_axis=0, concat_axis=0, tiled=True, axis_index_groups=same_core
        )

    slots = [send_ids[0, 0, :, 0]]
    other_slots = [swap(slots[0])]

    senone_tiles = state_senone.reshape(-1, LANES)

    def own_utterances(rows):
        return lax.dynamic_slice_in_dim(rows, lax.axis_index("emit") * utts, utts, 1)

    def first_rows(part):
        me = lax.axis_index("emit")
        parts = []
        for ahead in range(n_emit):
            piece = lax.dynamic_slice_in_dim(part, ((me + ahead) % n_emit) * utts, utts, 0)
            if ahead:
                piece = lax.ppermute(
                    piece, "emit", [(n, (n + ahead) % n_emit) for n in range(n_emit)]
                )
            parts.append(piece)
        order = [
            functools.reduce(
                lambda kept, ahead: jnp.where((me - n) % n_emit == ahead, parts[ahead], kept),
                range(1, n_emit),
                parts[0],
            )
            for n in range(n_emit)
        ]
        return jnp.concatenate(order, axis=1)

    codes = jnp.concatenate(
        [start_weights.astype(jnp.bfloat16), jnp.zeros((utts, width), jnp.bfloat16)], axis=1
    )
    gathered = lax.all_gather(loglike, "emit", axis=2, tiled=True)
    indices = (core_no, arc_src, arc_weight.astype(jnp.float32))
    tallies = (jnp.zeros((utts, LANES), jnp.float32),) * 2
    for frame_no in range(frames):
        outgoing = pack(
            width, n_chip, core_no, slots[frame_no], other_slots[frame_no], codes, swap(codes)
        )
        if frame_no == 0:
            outgoing, scores, ids = lax.optimization_barrier((outgoing, loglike, send_ids))
            values = own_product(codes, self_trans, outgoing)
            first = first_rows(scores[0])
            ids = ids[1:, 0, :, 0]
            other_ids = swap(ids)
            slots += [ids[n] for n in range(frames - 1)]
            other_slots += [other_ids[n] for n in range(frames - 1)]
            emission, level = emissions(first[None].astype(jnp.float32), senone_tiles)
        if frame_no == 1:
            outgoing, gathered = lax.optimization_barrier((outgoing, gathered))
            later = own_utterances(gathered[1:])
            emission, level = emissions(later.astype(jnp.float32), senone_tiles)
        received = exchange_chips(outgoing)
        values, *tallies, codes = step(
            frame_no, frame_no == frames - 1, indices, received, values, emission, level,
            max(frame_no - 1, 0), tallies, (self_trans, entry_trans),
        )

    scaled, log_like, bad = finish(exchange(codes), values, tallies[0])
    return lax.cond(
        bad[0] == 0.0,
        lambda: (scaled, log_like[0, :utts]),
        lambda: normalised_path(
            start_weights, first, later, self_trans, entry_trans, arc_weight, arc_src, send_ids,
            state_senone,
        ),
    )


def solution(mesh):
    in_specs = (
        P(None, None, "emit"),
        P("emit", "blk"),
        P("blk", None, None),
        P("blk", None, None),
        P("blk", None),
        P("blk", None),
        P(None, "blk", None, None),
        P("blk"),
    )
    out_specs = (P("emit", "blk"), P("emit"))
    return jax.shard_map(local, mesh=mesh, in_specs=in_specs, out_specs=out_specs, check_vma=False)
```

```python
import functools

import jax
import jax.numpy as jnp
from jax import lax
from jax.experimental import pallas as pl
from jax.experimental.pallas import tpu as pltpu
from jax.sharding import PartitionSpec as P

LANES = 128
TOP, BIAS, RATIO, TINY = 65535.0, 32768.0, 2.0**-22, 1e-30
META, PEAK_STEPS = 16, 256.0
MEAN_LOW, MEAN_HIGH = 2.0**-4, 4095.0
VMEM_LIMIT = 48 * 2**20


def exchange(outgoing):
    return lax.all_to_all(outgoing, "blk", split_axis=0, concat_axis=0, tiled=True)


def sum_over_blk(part):
    n_blk = lax.axis_size("blk")
    return jnp.sum(exchange(jnp.broadcast_to(part[None], (n_blk,) + part.shape)), axis=0)


def advance(values, matrices):
    return jnp.einsum("juv,jvw->juw", values, matrices, preferred_element_type=jnp.float32)


def normalised_path(
    start, first, later, self_trans, entry_trans, arc_weight, arc_src, send_ids, state_senone
):
    rows = jnp.concatenate([first[None], later], axis=0)
    slots = send_ids[:, 0, :, 0]
    utt_dev, n_blk = start.shape[0], lax.axis_size("blk")
    blk_dev, block_width = self_trans.shape[:2]
    state_count = blk_dev * block_width * n_blk
    senders = lax.broadcasted_iota(jnp.int32, (1, 1, n_blk), 2)
    arc_values = jnp.where(
        (arc_src // blk_dev)[:, :, None] == senders, arc_weight[:, :, None].astype(jnp.float32), 0.0
    )
    mixing = jnp.sum(arc_values, axis=1).astype(jnp.bfloat16)

    def blocks(values):
        return values.reshape(utt_dev, blk_dev, block_width).transpose(1, 0, 2)

    def frame(frame_no, carry):
        forward, log_like = carry
        sent = forward.astype(jnp.bfloat16)
        padded = jnp.concatenate([sent, jnp.zeros_like(sent[:1])], axis=0)
        outgoing = padded.at[slots[frame_no]].get(mode="promise_in_bounds")
        incoming = exchange(outgoing).reshape(n_blk, utt_dev * block_width)
        inflow = jnp.dot(mixing, incoming, preferred_element_type=jnp.float32)
        inflow = inflow.astype(jnp.bfloat16).reshape(blk_dev, utt_dev, block_width)
        raw_mass = advance(sent, self_trans) + advance(inflow, entry_trans)
        scores = rows[frame_no].at[:, state_senone].get(mode="promise_in_bounds")
        raw_mass = raw_mass * jnp.exp(blocks(scores).astype(jnp.float32))
        mass_sum = sum_over_blk(jnp.sum(raw_mass, axis=(0, 2)))
        forward = raw_mass * (state_count / mass_sum)[None, :, None]
        return forward, log_like + jnp.log(mass_sum / state_count)

    log_like = jnp.zeros((utt_dev,), jnp.float32)
    forward, log_like = lax.fori_loop(0, rows.shape[0], frame, (blocks(start), log_like))
    return forward.transpose(1, 0, 2).reshape(start.shape), log_like


def short(values):
    return values.astype(jnp.int32).astype(jnp.int16)


def wide(codes):
    return codes.astype(jnp.int32).astype(jnp.float32)


def encode(blocks, mean, core, out_ref):
    utts, width = blocks[0].shape
    lane = lax.broadcasted_iota(jnp.int32, (utts, LANES), 1) - core * META
    meta = jnp.zeros((utts, LANES), jnp.float32)
    bad = jnp.where((mean >= MEAN_LOW) & (mean <= MEAN_HIGH), 0.0, 1.0)
    for d, block in enumerate(blocks):
        peak = jnp.max(block, axis=1, keepdims=True)
        least = jnp.min(block, axis=1, keepdims=True)
        bad = jnp.where((least >= peak * RATIO) & (least >= TINY), bad, 1.0)
        steps = jnp.ceil(jnp.log2(peak) * PEAK_STEPS)
        share = block * jnp.exp2(steps * (-1.0 / PEAK_STEPS))
        root = jnp.exp2(jnp.log2(share) * (1.0 / 3.0))
        code = jnp.clip(jnp.round(root * TOP), 0.0, TOP) - BIAS
        out_ref[:, d * width : (d + 1) * width] = short(code)
        meta = jnp.where(lane == d, steps, meta)
    n = len(blocks)
    out_ref[:, n * width : (n + 1) * width] = short(jnp.full((utts, width), -BIAS, jnp.float32))
    rest = mean * 8.0
    for digit in range(3):
        whole = jnp.floor(rest)
        meta = jnp.where(lane == n + digit, whole, meta)
        rest = (rest - whole) * 2.0**15
    out_ref[:, (n + 1) * width :] = short(meta)
    return jnp.broadcast_to(bad, (utts, LANES))


def pack_kernel(width, core_ref, mine_ref, others_ref, own_ref, other_ref, out_ref):
    core = core_ref[0]
    mine_at = pl.multiple_of(core * width, width)
    others_at = pl.multiple_of((1 - core) * width, width)
    with_meta = out_ref.shape[2] > 2 * width
    if with_meta:
        last = slice(own_ref.shape[1] - LANES, own_ref.shape[1])
        meta = short(wide(own_ref[:, last]) + wide(other_ref[:, last]))
    for chip in range(out_ref.shape[0]):
        mine = pl.multiple_of(mine_ref[2 * chip + core] * width, width)
        others = pl.multiple_of(others_ref[2 * chip + core] * width, width)
        out_ref[chip, :, pl.ds(mine_at, width)] = own_ref[:, pl.ds(mine, width)]
        out_ref[chip, :, pl.ds(others_at, width)] = other_ref[:, pl.ds(others, width)]
        if with_meta:
            out_ref[chip, :, 2 * width :] = meta


def pack(width, n_chip, core, mine, others, own, other):
    smem = pl.BlockSpec(memory_space=pltpu.SMEM)
    vmem = pl.BlockSpec(memory_space=pltpu.VMEM)
    return pl.pallas_call(
        functools.partial(pack_kernel, width),
        out_shape=jax.ShapeDtypeStruct(
            (n_chip, own.shape[0], 2 * width + own.shape[1] % width), own.dtype
        ),
        in_specs=[smem] * 3 + [vmem] * 2,
        out_specs=vmem,
        compiler_params=pltpu.CompilerParams(vmem_limit_bytes=VMEM_LIMIT),
        name="pack",
    )(core, mine, others, own, other)


def emission_kernel(rows_ref, senone_ref, emission_ref, level_ref):
    frames, utts, senones = rows_ref.shape
    tiles = senones // LANES
    levels = []
    for frame in range(frames):
        rows = rows_ref[frame]
        top = jnp.max(rows, axis=1, keepdims=True)
        mean = jnp.sum(jnp.exp(rows - top), axis=1, keepdims=True) * (1.0 / senones)
        levels.append(top + jnp.log(mean))
        level_ref[frame] = jnp.broadcast_to(levels[-1], (utts, LANES))

    def packed(pair, n):
        at = slice(n * LANES, (n + 1) * LANES)
        low = rows_ref[2 * pair, :, at] * -16.0
        if 2 * pair + 1 < frames:
            low += rows_ref[2 * pair + 1, :, at] * -32768.0
        return low

    pairs = (frames + 1) // 2

    def group(state_group, _):
        senone = jnp.broadcast_to(senone_ref[pl.ds(state_group, 1), :], (utts, LANES))
        lane = senone & (LANES - 1)
        tile = senone >> 7
        found = [jnp.zeros((utts, LANES), jnp.float32)] * pairs
        for n in range(tiles):
            here = tile == n
            for pair in range(pairs):
                picked = jnp.take_along_axis(
                    packed(pair, n), lane, axis=1, mode="promise_in_bounds"
                )
                found[pair] = jnp.where(here, picked, found[pair])
        at = pl.multiple_of(state_group * LANES, LANES)
        for pair in range(pairs):
            high = jnp.floor(found[pair] * (1.0 / 2048.0))
            both = (found[pair] - high * 2048.0, high)
            for frame in range(2 * pair, min(2 * pair + 2, frames)):
                score = both[frame - 2 * pair] * (-1.0 / 16.0)
                emission_ref[frame, :, pl.ds(at, LANES)] = jnp.exp(score - levels[frame])
        return 0

    lax.fori_loop(0, senone_ref.shape[0], group, 0)


def emissions(rows, senone_tiles):
    frames, utts, senones = rows.shape
    groups = senone_tiles.shape[0]
    return pl.pallas_call(
        emission_kernel,
        out_shape=(
            jax.ShapeDtypeStruct((frames, utts, groups * LANES), jnp.float32),
            jax.ShapeDtypeStruct((frames, utts, LANES), jnp.float32),
        ),
        compiler_params=pltpu.CompilerParams(vmem_limit_bytes=VMEM_LIMIT),
        cost_estimate=pl.CostEstimate(
            flops=8 * frames * groups * senones * utts, bytes_accessed=2**20,
            transcendentals=frames * groups * utts * LANES,
        ),
        name="emissions",
    )(rows, senone_tiles)


def column_to_row(column):
    n = column.shape[0]
    lane = lax.broadcasted_iota(jnp.int32, (n, LANES), 1)
    place = lax.broadcasted_iota(jnp.int32, (n, LANES), 0)
    return jnp.sum(jnp.where(lane == place, column, 0.0), axis=0, keepdims=True)


def row_to_column(row, n):
    lane = lax.broadcasted_iota(jnp.int32, (n, LANES), 1)
    place = lax.broadcasted_iota(jnp.int32, (n, LANES), 0)
    return jnp.sum(jnp.where(lane == place, row, 0.0), axis=1, keepdims=True)


def step_kernel(
    first, last, streamed, slot, core_ref, arc_ref, weight_ref, recv_ref, prev_ref, emission_ref,
    level_ref, log_in_ref, bad_in_ref, self_in, entry_in, raw_ref, log_ref, bad_ref,
    end_ref, *scratch,
):
    n_chip, utts = recv_ref.shape[:2]
    blk_dev, width = self_in.shape[:2]
    arcs = arc_ref.shape[1]
    bits = blk_dev.bit_length() - 1
    lane = lax.broadcasted_iota(jnp.int32, (utts, LANES), 1)
    self_ref, entry_ref, copies = self_in, entry_in, []
    if streamed:
        self_ref, entry_ref, arrived = scratch
        for d in range(blk_dev):
            pairs = [(entry_in, entry_ref)] if first else [(self_in, self_ref), (entry_in, entry_ref)]
            copies.append(
                [
                    pltpu.make_async_copy(src.at[d], dst.at[d], arrived.at[2 * d + n])
                    for n, (src, dst) in enumerate(pairs)
                ]
            )
            for copy in copies[d]:
                copy.start()
    log_like = log_in_ref[...] + level_ref[slot]
    if first:
        scale = jnp.ones((utts, 1), jnp.float32)
    else:
        sums = wide(recv_ref[0, :, 2 * width :])
        for chip in range(1, n_chip):
            sums += wide(recv_ref[chip, :, 2 * width :])
        digit = lane % META - blk_dev
        place = jnp.where(
            digit == 0,
            2.0**-3,
            jnp.where(digit == 1, 2.0**-18, jnp.where(digit == 2, 2.0**-33, 0.0)),
        )
        scale = (2.0 * n_chip) / jnp.sum(sums * place, axis=1, keepdims=True)
        log_like = log_like - jnp.log(scale)
    log_ref[...] = log_like
    narrow = jnp.broadcast_to(scale, (utts, LANES)) * TOP**-3
    scale = jnp.broadcast_to(scale, (utts, width))

    def inflow_of(d):
        inflow = jnp.zeros((utts, width), jnp.float32)
        for a in range(arcs):
            source = arc_ref[d, a]
            chip, side, block = source >> (bits + 1), (source >> bits) & 1, source & (blk_dev - 1)
            code = recv_ref[chip, :, pl.ds(pl.multiple_of(side * width, width), width)]
            if first:
                inflow += code.astype(jnp.float32) * weight_ref[d, a]
                continue
            code = wide(code) + BIAS
            meta = wide(recv_ref[chip, :, 2 * width :])
            at = jnp.full((utts, LANES), side * META + block, jnp.int32)
            steps = jnp.take_along_axis(meta, at, axis=1, mode="promise_in_bounds")
            unit = jnp.exp2(steps * (1.0 / PEAK_STEPS)) * narrow
            unit = jnp.concatenate([unit] * (width // LANES), axis=1)
            sent = (code * unit * code * code).astype(jnp.bfloat16).astype(jnp.float32)
            inflow += sent * weight_ref[d, a]
        return inflow.astype(jnp.bfloat16)

    blocks = []
    total = jnp.zeros((utts, width), jnp.float32)
    inflow = inflow_of(0)
    for d in range(blk_dev):
        here = slice(d * width, (d + 1) * width)
        if streamed:
            for copy in copies[d]:
                copy.wait()
        if first:
            raw = prev_ref[:, here]
        else:
            own = (prev_ref[:, here] * scale).astype(jnp.bfloat16)
            raw = jnp.dot(own, self_ref[d], preferred_element_type=jnp.float32)
        after = inflow_of(d + 1) if d + 1 < blk_dev else None
        raw += jnp.dot(inflow, entry_ref[d], preferred_element_type=jnp.float32)
        raw = raw * emission_ref[slot, :, here]
        raw_ref[:, here] = raw
        total += raw
        blocks.append(raw)
        inflow = after
    mean = jnp.sum(total, axis=1, keepdims=True) * (1.0 / (blk_dev * width))
    if last:
        bad_ref[...] = bad_in_ref[...]
        row = column_to_row(mean)
        bad = jnp.max(bad_in_ref[...], axis=0, keepdims=True)
        row = jnp.where(lane[:1] == utts, bad, row)
        end_ref[...] = jnp.broadcast_to(row, end_ref.shape)
    else:
        bad_ref[...] = jnp.maximum(bad_in_ref[...], encode(blocks, mean, core_ref[0], end_ref))


def step(frame_no, last, indices, received, previous, emission, level, slot, tallies, matrices):
    blk_dev, width = matrices[0].shape[:2]
    n_chip = received.shape[0]
    utts, states = previous.shape
    streamed = frame_no < 2
    smem = pl.BlockSpec(memory_space=pltpu.SMEM)
    vmem = pl.BlockSpec(memory_space=pltpu.VMEM)
    matrix = pl.BlockSpec(memory_space=pl.ANY) if streamed else vmem
    end = (2 * n_chip, LANES) if last else (utts, states + width + LANES)
    tile = jax.ShapeDtypeStruct((utts, LANES), jnp.float32)
    scratch = []
    if streamed:
        scratch = [pltpu.VMEM(m.shape, m.dtype) for m in matrices]
        scratch.append(pltpu.SemaphoreType.DMA((2 * blk_dev,)))
    return pl.pallas_call(
        functools.partial(step_kernel, frame_no == 0, last, streamed, slot),
        out_shape=[
            jax.ShapeDtypeStruct((utts, states), jnp.float32),
            tile,
            tile,
            jax.ShapeDtypeStruct(end, jnp.float32 if last else jnp.int16),
        ],
        in_specs=[smem] * 3 + [vmem] * 6 + [matrix] * 2,
        out_specs=[vmem] * 4,
        scratch_shapes=scratch,
        compiler_params=pltpu.CompilerParams(vmem_limit_bytes=VMEM_LIMIT),
        cost_estimate=pl.CostEstimate(
            flops=4 * utts * blk_dev * width**2, bytes_accessed=4 * blk_dev * width**2,
            transcendentals=0,
        ),
        name="step",
    )(*indices, received, previous, emission, level, *tallies, *matrices)


def own_kernel(start_ref, self_in, after_ref, out_ref, self_ref, arrived):
    del after_ref
    blk_dev, width = self_ref.shape[:2]
    copies = [
        pltpu.make_async_copy(self_in.at[d], self_ref.at[d], arrived.at[d]) for d in range(blk_dev)
    ]
    for copy in copies:
        copy.start()
    for d in range(blk_dev):
        here = slice(d * width, (d + 1) * width)
        copies[d].wait()
        out_ref[:, here] = jnp.dot(
            start_ref[:, here], self_ref[d], preferred_element_type=jnp.float32
        )


def own_product(start, self_trans, after):
    blk_dev, width = self_trans.shape[:2]
    utts = start.shape[0]
    vmem = pl.BlockSpec(memory_space=pltpu.VMEM)
    anywhere = pl.BlockSpec(memory_space=pl.ANY)
    return pl.pallas_call(
        own_kernel,
        out_shape=jax.ShapeDtypeStruct((utts, blk_dev * width), jnp.float32),
        in_specs=[vmem, anywhere, anywhere],
        out_specs=vmem,
        scratch_shapes=[
            pltpu.VMEM(self_trans.shape, self_trans.dtype),
            pltpu.SemaphoreType.DMA((blk_dev,)),
        ],
        compiler_params=pltpu.CompilerParams(vmem_limit_bytes=VMEM_LIMIT),
        cost_estimate=pl.CostEstimate(
            flops=2 * utts * blk_dev * width**2, bytes_accessed=2 * blk_dev * width**2,
            transcendentals=0,
        ),
        name="own",
    )(start, self_trans, after)


def finish_kernel(recv_ref, raw_ref, log_ref, out_ref, log_row_ref, bad_ref):
    utts = raw_ref.shape[0]
    sums = jnp.sum(recv_ref[...], axis=0, keepdims=True)
    mean = row_to_column(sums, utts) * (1.0 / recv_ref.shape[0])
    out_ref[...] = raw_ref[...] * (1.0 / mean)
    log_row_ref[...] = column_to_row((log_ref[...] + jnp.log(mean))[:, :1])
    lane = lax.broadcasted_iota(jnp.int32, (1, LANES), 1)
    bad_ref[0] = jnp.sum(jnp.where(lane == utts, sums, 0.0))


def finish(received, raw, log_like):
    vmem = pl.BlockSpec(memory_space=pltpu.VMEM)
    return pl.pallas_call(
        finish_kernel,
        out_shape=[
            jax.ShapeDtypeStruct(raw.shape, jnp.float32),
            jax.ShapeDtypeStruct((1, LANES), jnp.float32),
            jax.ShapeDtypeStruct((1,), jnp.float32),
        ],
        in_specs=[vmem] * 3,
        out_specs=[vmem, vmem, pl.BlockSpec(memory_space=pltpu.SMEM)],
        compiler_params=pltpu.CompilerParams(vmem_limit_bytes=VMEM_LIMIT),
        name="finish",
    )(received, raw, log_like)


def local(
    loglike, start_weights, self_trans, entry_trans, arc_weight, arc_src, send_ids, state_senone
):
    n_blk = lax.axis_size("blk")
    n_chip = n_blk // 2
    n_emit = lax.axis_size("emit")
    blk_dev, width = self_trans.shape[:2]
    utts = start_weights.shape[0]
    frames = loglike.shape[0]
    core = lax.axis_index("blk") % 2
    core_no = core.astype(jnp.int32).reshape(1)

    other_core = [(n, n ^ 1) for n in range(n_blk)]
    same_core = [[2 * n + c for n in range(n_chip)] for c in range(2)]

    def swap(x):
        return lax.ppermute(x, "blk", other_core)

    def exchange_chips(x):
        return lax.all_to_all(
            x, "blk", split_axis=0, concat_axis=0, tiled=True, axis_index_groups=same_core
        )

    slots = [send_ids[0, 0, :, 0]]
    other_slots = [swap(slots[0])]

    senone_tiles = state_senone.reshape(-1, LANES)

    def own_utterances(rows):
        return lax.dynamic_slice_in_dim(rows, lax.axis_index("emit") * utts, utts, 1)

    def first_rows(part):
        me = lax.axis_index("emit")
        parts = []
        for ahead in range(n_emit):
            piece = lax.dynamic_slice_in_dim(part, ((me + ahead) % n_emit) * utts, utts, 0)
            if ahead:
                piece = lax.ppermute(
                    piece, "emit", [(n, (n + ahead) % n_emit) for n in range(n_emit)]
                )
            parts.append(piece)
        order = [
            functools.reduce(
                lambda kept, ahead: jnp.where((me - n) % n_emit == ahead, parts[ahead], kept),
                range(1, n_emit),
                parts[0],
            )
            for n in range(n_emit)
        ]
        return jnp.concatenate(order, axis=1)

    codes = jnp.concatenate(
        [start_weights.astype(jnp.bfloat16), jnp.zeros((utts, width), jnp.bfloat16)], axis=1
    )
    gathered = lax.all_gather(loglike, "emit", axis=2, tiled=True)
    indices = (core_no, arc_src, arc_weight.astype(jnp.float32))
    tallies = (jnp.zeros((utts, LANES), jnp.float32),) * 2
    for frame_no in range(frames):
        outgoing = pack(
            width, n_chip, core_no, slots[frame_no], other_slots[frame_no], codes, swap(codes)
        )
        if frame_no == 0:
            outgoing, scores, ids = lax.optimization_barrier((outgoing, loglike, send_ids))
            values = own_product(codes, self_trans, outgoing)
            first = first_rows(scores[0])
            ids = ids[1:, 0, :, 0]
            other_ids = swap(ids)
            slots += [ids[n] for n in range(frames - 1)]
            other_slots += [other_ids[n] for n in range(frames - 1)]
            emission, level = emissions(first[None].astype(jnp.float32), senone_tiles)
        if frame_no == 1:
            outgoing, gathered = lax.optimization_barrier((outgoing, gathered))
            later = own_utterances(gathered[1:])
            emission, level = emissions(later.astype(jnp.float32), senone_tiles)
        received = exchange_chips(outgoing)
        values, *tallies, codes = step(
            frame_no, frame_no == frames - 1, indices, received, values, emission, level,
            max(frame_no - 1, 0), tallies, (self_trans, entry_trans),
        )

    scaled, log_like, bad = finish(exchange(codes), values, tallies[0])
    return lax.cond(
        bad[0] == 0.0,
        lambda: (scaled, log_like[0, :utts]),
        lambda: normalised_path(
            start_weights, first, later, self_trans, entry_trans, arc_weight, arc_src, send_ids,
            state_senone,
        ),
    )


def solution(mesh):
    in_specs = (
        P(None, None, "emit"),
        P("emit", "blk"),
        P("blk", None, None),
        P("blk", None, None),
        P("blk", None),
        P("blk", None),
        P(None, "blk", None, None),
        P("blk"),
    )
    out_specs = (P("emit", "blk"), P("emit"))
    return jax.shard_map(local, mesh=mesh, in_specs=in_specs, out_specs=out_specs, check_vma=False)
```

```python
import functools

import jax
import jax.numpy as jnp
from jax import lax
from jax.experimental import pallas as pl
from jax.experimental.pallas import tpu as pltpu
from jax.sharding import PartitionSpec as P

LANES = 128
TOP, BIAS, RATIO, TINY = 65535.0, 32768.0, 2.0**-22, 1e-30
META, PEAK_STEPS = 16, 256.0
MEAN_LOW, MEAN_HIGH = 2.0**-4, 4095.0
VMEM_LIMIT = 48 * 2**20


def exchange(outgoing):
    return lax.all_to_all(outgoing, "blk", split_axis=0, concat_axis=0, tiled=True)


def sum_over_blk(part):
    n_blk = lax.axis_size("blk")
    return jnp.sum(exchange(jnp.broadcast_to(part[None], (n_blk,) + part.shape)), axis=0)


def advance(values, matrices):
    return jnp.einsum("juv,jvw->juw", values, matrices, preferred_element_type=jnp.float32)


def normalised_path(
    start, first, later, self_trans, entry_trans, arc_weight, arc_src, send_ids, state_senone
):
    rows = jnp.concatenate([first[None], later], axis=0)
    slots = send_ids[:, 0, :, 0]
    utt_dev, n_blk = start.shape[0], lax.axis_size("blk")
    blk_dev, block_width = self_trans.shape[:2]
    state_count = blk_dev * block_width * n_blk
    senders = lax.broadcasted_iota(jnp.int32, (1, 1, n_blk), 2)
    arc_values = jnp.where(
        (arc_src // blk_dev)[:, :, None] == senders, arc_weight[:, :, None].astype(jnp.float32), 0.0
    )
    mixing = jnp.sum(arc_values, axis=1).astype(jnp.bfloat16)

    def blocks(values):
        return values.reshape(utt_dev, blk_dev, block_width).transpose(1, 0, 2)

    def frame(frame_no, carry):
        forward, log_like = carry
        sent = forward.astype(jnp.bfloat16)
        padded = jnp.concatenate([sent, jnp.zeros_like(sent[:1])], axis=0)
        outgoing = padded.at[slots[frame_no]].get(mode="promise_in_bounds")
        incoming = exchange(outgoing).reshape(n_blk, utt_dev * block_width)
        inflow = jnp.dot(mixing, incoming, preferred_element_type=jnp.float32)
        inflow = inflow.astype(jnp.bfloat16).reshape(blk_dev, utt_dev, block_width)
        raw_mass = advance(sent, self_trans) + advance(inflow, entry_trans)
        scores = rows[frame_no].at[:, state_senone].get(mode="promise_in_bounds")
        raw_mass = raw_mass * jnp.exp(blocks(scores).astype(jnp.float32))
        mass_sum = sum_over_blk(jnp.sum(raw_mass, axis=(0, 2)))
        forward = raw_mass * (state_count / mass_sum)[None, :, None]
        return forward, log_like + jnp.log(mass_sum / state_count)

    log_like = jnp.zeros((utt_dev,), jnp.float32)
    forward, log_like = lax.fori_loop(0, rows.shape[0], frame, (blocks(start), log_like))
    return forward.transpose(1, 0, 2).reshape(start.shape), log_like


def short(values):
    return values.astype(jnp.int32).astype(jnp.int16)


def wide(codes):
    return codes.astype(jnp.int32).astype(jnp.float32)


def encode(blocks, mean, core, out_ref):
    utts, width = blocks[0].shape
    lane = lax.broadcasted_iota(jnp.int32, (utts, LANES), 1) - core * META
    meta = jnp.zeros((utts, LANES), jnp.float32)
    bad = jnp.where((mean >= MEAN_LOW) & (mean <= MEAN_HIGH), 0.0, 1.0)
    for d, block in enumerate(blocks):
        peak = jnp.max(block, axis=1, keepdims=True)
        least = jnp.min(block, axis=1, keepdims=True)
        bad = jnp.where((least >= peak * RATIO) & (least >= TINY), bad, 1.0)
        steps = jnp.ceil(jnp.log2(peak) * PEAK_STEPS)
        share = block * jnp.exp2(steps * (-1.0 / PEAK_STEPS))
        root = jnp.exp2(jnp.log2(share) * (1.0 / 3.0))
        code = jnp.clip(jnp.round(root * TOP), 0.0, TOP) - BIAS
        out_ref[:, d * width : (d + 1) * width] = short(code)
        meta = jnp.where(lane == d, steps, meta)
    n = len(blocks)
    out_ref[:, n * width : (n + 1) * width] = short(jnp.full((utts, width), -BIAS, jnp.float32))
    rest = mean * 8.0
    for digit in range(3):
        whole = jnp.floor(rest)
        meta = jnp.where(lane == n + digit, whole, meta)
        rest = (rest - whole) * 2.0**15
    out_ref[:, (n + 1) * width :] = short(meta)
    return jnp.broadcast_to(bad, (utts, LANES))


def pack_kernel(width, core_ref, mine_ref, others_ref, own_ref, other_ref, out_ref, zero_ref):
    core = core_ref[0]
    zero_ref[0] = 0
    mine_at = pl.multiple_of(core * width, width)
    others_at = pl.multiple_of((1 - core) * width, width)
    with_meta = out_ref.shape[2] > 2 * width
    if with_meta:
        last = slice(own_ref.shape[1] - LANES, own_ref.shape[1])
        meta = short(wide(own_ref[:, last]) + wide(other_ref[:, last]))
    for chip in range(out_ref.shape[0]):
        mine = pl.multiple_of(mine_ref[2 * chip + core] * width, width)
        others = pl.multiple_of(others_ref[2 * chip + core] * width, width)
        out_ref[chip, :, pl.ds(mine_at, width)] = own_ref[:, pl.ds(mine, width)]
        out_ref[chip, :, pl.ds(others_at, width)] = other_ref[:, pl.ds(others, width)]
        if with_meta:
            out_ref[chip, :, 2 * width :] = meta


def pack(width, n_chip, core, mine, others, own, other):
    smem = pl.BlockSpec(memory_space=pltpu.SMEM)
    vmem = pl.BlockSpec(memory_space=pltpu.VMEM)
    return pl.pallas_call(
        functools.partial(pack_kernel, width),
        out_shape=[
            jax.ShapeDtypeStruct(
                (n_chip, own.shape[0], 2 * width + own.shape[1] % width), own.dtype
            ),
            jax.ShapeDtypeStruct((1,), jnp.int32),
        ],
        in_specs=[smem] * 3 + [vmem] * 2,
        out_specs=[vmem, smem],
        compiler_params=pltpu.CompilerParams(vmem_limit_bytes=VMEM_LIMIT),
        name="pack",
    )(core, mine, others, own, other)


def emission_kernel(rows_ref, senone_ref, emission_ref, level_ref):
    frames, utts, senones = rows_ref.shape
    tiles = senones // LANES
    levels = []
    for frame in range(frames):
        rows = rows_ref[frame]
        top = jnp.max(rows, axis=1, keepdims=True)
        mean = jnp.sum(jnp.exp(rows - top), axis=1, keepdims=True) * (1.0 / senones)
        levels.append(top + jnp.log(mean))
        level_ref[frame] = jnp.broadcast_to(levels[-1], (utts, LANES))

    def packed(pair, n):
        at = slice(n * LANES, (n + 1) * LANES)
        low = rows_ref[2 * pair, :, at] * -16.0
        if 2 * pair + 1 < frames:
            low += rows_ref[2 * pair + 1, :, at] * -32768.0
        return low

    pairs = (frames + 1) // 2

    def group(state_group, _):
        senone = jnp.broadcast_to(senone_ref[pl.ds(state_group, 1), :], (utts, LANES))
        lane = senone & (LANES - 1)
        tile = senone >> 7
        found = [jnp.zeros((utts, LANES), jnp.float32)] * pairs
        for n in range(tiles):
            here = tile == n
            for pair in range(pairs):
                picked = jnp.take_along_axis(
                    packed(pair, n), lane, axis=1, mode="promise_in_bounds"
                )
                found[pair] = jnp.where(here, picked, found[pair])
        at = pl.multiple_of(state_group * LANES, LANES)
        for pair in range(pairs):
            high = jnp.floor(found[pair] * (1.0 / 2048.0))
            both = (found[pair] - high * 2048.0, high)
            for frame in range(2 * pair, min(2 * pair + 2, frames)):
                score = both[frame - 2 * pair] * (-1.0 / 16.0)
                emission_ref[frame, :, pl.ds(at, LANES)] = jnp.exp(score - levels[frame])
        return 0

    lax.fori_loop(0, senone_ref.shape[0], group, 0)


def emissions(rows, senone_tiles):
    frames, utts, senones = rows.shape
    groups = senone_tiles.shape[0]
    return pl.pallas_call(
        emission_kernel,
        out_shape=(
            jax.ShapeDtypeStruct((frames, utts, groups * LANES), jnp.float32),
            jax.ShapeDtypeStruct((frames, utts, LANES), jnp.float32),
        ),
        compiler_params=pltpu.CompilerParams(vmem_limit_bytes=VMEM_LIMIT),
        cost_estimate=pl.CostEstimate(
            flops=8 * frames * groups * senones * utts, bytes_accessed=2**20,
            transcendentals=frames * groups * utts * LANES,
        ),
        name="emissions",
    )(rows, senone_tiles)


def column_to_row(column):
    n = column.shape[0]
    lane = lax.broadcasted_iota(jnp.int32, (n, LANES), 1)
    place = lax.broadcasted_iota(jnp.int32, (n, LANES), 0)
    return jnp.sum(jnp.where(lane == place, column, 0.0), axis=0, keepdims=True)


def row_to_column(row, n):
    lane = lax.broadcasted_iota(jnp.int32, (n, LANES), 1)
    place = lax.broadcasted_iota(jnp.int32, (n, LANES), 0)
    return jnp.sum(jnp.where(lane == place, row, 0.0), axis=1, keepdims=True)


def step_kernel(
    first, last, streamed, slot, core_ref, arc_ref, weight_ref, recv_ref, prev_ref, emission_ref,
    level_ref, log_in_ref, bad_in_ref, self_in, entry_in, raw_ref, log_ref, bad_ref,
    end_ref, *scratch,
):
    n_chip, utts = recv_ref.shape[:2]
    blk_dev, width = self_in.shape[:2]
    arcs = arc_ref.shape[1]
    bits = blk_dev.bit_length() - 1
    lane = lax.broadcasted_iota(jnp.int32, (utts, LANES), 1)
    self_ref, entry_ref, copies = self_in, entry_in, []
    if streamed:
        self_ref, entry_ref, arrived = scratch
        for d in range(blk_dev):
            pairs = [(entry_in, entry_ref)] if first else [(self_in, self_ref), (entry_in, entry_ref)]
            copies.append(
                [
                    pltpu.make_async_copy(src.at[d], dst.at[d], arrived.at[2 * d + n])
                    for n, (src, dst) in enumerate(pairs)
                ]
            )
            for copy in copies[d]:
                copy.start()
    log_like = log_in_ref[...] + level_ref[slot]
    if first:
        scale = jnp.ones((utts, 1), jnp.float32)
    else:
        sums = wide(recv_ref[0, :, 2 * width :])
        for chip in range(1, n_chip):
            sums += wide(recv_ref[chip, :, 2 * width :])
        digit = lane % META - blk_dev
        place = jnp.where(
            digit == 0,
            2.0**-3,
            jnp.where(digit == 1, 2.0**-18, jnp.where(digit == 2, 2.0**-33, 0.0)),
        )
        scale = (2.0 * n_chip) / jnp.sum(sums * place, axis=1, keepdims=True)
        log_like = log_like - jnp.log(scale)
    log_ref[...] = log_like
    narrow = jnp.broadcast_to(scale, (utts, LANES)) * TOP**-3
    scale = jnp.broadcast_to(scale, (utts, width))

    def inflow_of(d):
        inflow = jnp.zeros((utts, width), jnp.float32)
        for a in range(arcs):
            source = arc_ref[d, a]
            chip, side, block = source >> (bits + 1), (source >> bits) & 1, source & (blk_dev - 1)
            code = recv_ref[chip, :, pl.ds(pl.multiple_of(side * width, width), width)]
            if first:
                inflow += code.astype(jnp.float32) * weight_ref[d, a]
                continue
            code = wide(code) + BIAS
            meta = wide(recv_ref[chip, :, 2 * width :])
            at = jnp.full((utts, LANES), side * META + block, jnp.int32)
            steps = jnp.take_along_axis(meta, at, axis=1, mode="promise_in_bounds")
            unit = jnp.exp2(steps * (1.0 / PEAK_STEPS)) * narrow
            unit = jnp.concatenate([unit] * (width // LANES), axis=1)
            sent = (code * unit * code * code).astype(jnp.bfloat16).astype(jnp.float32)
            inflow += sent * weight_ref[d, a]
        return inflow.astype(jnp.bfloat16)

    blocks = []
    total = jnp.zeros((utts, width), jnp.float32)
    inflow = inflow_of(0)
    for d in range(blk_dev):
        here = slice(d * width, (d + 1) * width)
        if streamed:
            for copy in copies[d]:
                copy.wait()
        if first:
            raw = prev_ref[:, here]
        else:
            own = (prev_ref[:, here] * scale).astype(jnp.bfloat16)
            raw = jnp.dot(own, self_ref[d], preferred_element_type=jnp.float32)
        after = inflow_of(d + 1) if d + 1 < blk_dev else None
        raw += jnp.dot(inflow, entry_ref[d], preferred_element_type=jnp.float32)
        raw = raw * emission_ref[slot, :, here]
        raw_ref[:, here] = raw
        total += raw
        blocks.append(raw)
        inflow = after
    mean = jnp.sum(total, axis=1, keepdims=True) * (1.0 / (blk_dev * width))
    if last:
        bad_ref[...] = bad_in_ref[...]
        row = column_to_row(mean)
        bad = jnp.max(bad_in_ref[...], axis=0, keepdims=True)
        row = jnp.where(lane[:1] == utts, bad, row)
        end_ref[...] = jnp.broadcast_to(row, end_ref.shape)
    else:
        bad_ref[...] = jnp.maximum(bad_in_ref[...], encode(blocks, mean, core_ref[0], end_ref))


def step(frame_no, last, indices, received, previous, emission, level, slot, tallies, matrices):
    blk_dev, width = matrices[0].shape[:2]
    n_chip = received.shape[0]
    utts, states = previous.shape
    streamed = frame_no < 2
    smem = pl.BlockSpec(memory_space=pltpu.SMEM)
    vmem = pl.BlockSpec(memory_space=pltpu.VMEM)
    matrix = pl.BlockSpec(memory_space=pl.ANY) if streamed else vmem
    end = (2 * n_chip, LANES) if last else (utts, states + width + LANES)
    tile = jax.ShapeDtypeStruct((utts, LANES), jnp.float32)
    scratch = []
    if streamed:
        scratch = [pltpu.VMEM(m.shape, m.dtype) for m in matrices]
        scratch.append(pltpu.SemaphoreType.DMA((2 * blk_dev,)))
    return pl.pallas_call(
        functools.partial(step_kernel, frame_no == 0, last, streamed, slot),
        out_shape=[
            jax.ShapeDtypeStruct((utts, states), jnp.float32),
            tile,
            tile,
            jax.ShapeDtypeStruct(end, jnp.float32 if last else jnp.int16),
        ],
        in_specs=[smem] * 3 + [vmem] * 6 + [matrix] * 2,
        out_specs=[vmem] * 4,
        scratch_shapes=scratch,
        compiler_params=pltpu.CompilerParams(vmem_limit_bytes=VMEM_LIMIT),
        cost_estimate=pl.CostEstimate(
            flops=4 * utts * blk_dev * width**2, bytes_accessed=4 * blk_dev * width**2,
            transcendentals=0,
        ),
        name="step",
    )(*indices, received, previous, emission, level, *tallies, *matrices)


def own_kernel(start_ref, self_in, after_ref, out_ref, self_ref, arrived):
    del after_ref
    blk_dev, width = self_ref.shape[:2]
    copies = [
        pltpu.make_async_copy(self_in.at[d], self_ref.at[d], arrived.at[d]) for d in range(blk_dev)
    ]
    for copy in copies:
        copy.start()
    for d in range(blk_dev):
        here = slice(d * width, (d + 1) * width)
        copies[d].wait()
        out_ref[:, here] = jnp.dot(
            start_ref[:, here], self_ref[d], preferred_element_type=jnp.float32
        )


def own_product(start, self_trans, after):
    blk_dev, width = self_trans.shape[:2]
    utts = start.shape[0]
    vmem = pl.BlockSpec(memory_space=pltpu.VMEM)
    anywhere = pl.BlockSpec(memory_space=pl.ANY)
    return pl.pallas_call(
        own_kernel,
        out_shape=jax.ShapeDtypeStruct((utts, blk_dev * width), jnp.float32),
        in_specs=[vmem, anywhere, anywhere],
        out_specs=vmem,
        scratch_shapes=[
            pltpu.VMEM(self_trans.shape, self_trans.dtype),
            pltpu.SemaphoreType.DMA((blk_dev,)),
        ],
        compiler_params=pltpu.CompilerParams(vmem_limit_bytes=VMEM_LIMIT),
        cost_estimate=pl.CostEstimate(
            flops=2 * utts * blk_dev * width**2, bytes_accessed=2 * blk_dev * width**2,
            transcendentals=0,
        ),
        name="own",
    )(start, self_trans, after)


def finish_kernel(recv_ref, raw_ref, log_ref, out_ref, log_row_ref, bad_ref):
    utts = raw_ref.shape[0]
    sums = jnp.sum(recv_ref[...], axis=0, keepdims=True)
    mean = row_to_column(sums, utts) * (1.0 / recv_ref.shape[0])
    out_ref[...] = raw_ref[...] * (1.0 / mean)
    log_row_ref[...] = column_to_row((log_ref[...] + jnp.log(mean))[:, :1])
    lane = lax.broadcasted_iota(jnp.int32, (1, LANES), 1)
    bad_ref[0] = jnp.sum(jnp.where(lane == utts, sums, 0.0))


def finish(received, raw, log_like):
    vmem = pl.BlockSpec(memory_space=pltpu.VMEM)
    return pl.pallas_call(
        finish_kernel,
        out_shape=[
            jax.ShapeDtypeStruct(raw.shape, jnp.float32),
            jax.ShapeDtypeStruct((1, LANES), jnp.float32),
            jax.ShapeDtypeStruct((1,), jnp.float32),
        ],
        in_specs=[vmem] * 3,
        out_specs=[vmem, vmem, pl.BlockSpec(memory_space=pltpu.SMEM)],
        compiler_params=pltpu.CompilerParams(vmem_limit_bytes=VMEM_LIMIT),
        name="finish",
    )(received, raw, log_like)


def local(
    loglike, start_weights, self_trans, entry_trans, arc_weight, arc_src, send_ids, state_senone
):
    n_blk = lax.axis_size("blk")
    n_chip = n_blk // 2
    n_emit = lax.axis_size("emit")
    blk_dev, width = self_trans.shape[:2]
    utts = start_weights.shape[0]
    frames = loglike.shape[0]
    core = lax.axis_index("blk") % 2
    core_no = core.astype(jnp.int32).reshape(1)

    other_core = [(n, n ^ 1) for n in range(n_blk)]
    same_core = [[2 * n + c for n in range(n_chip)] for c in range(2)]

    def swap(x):
        return lax.ppermute(x, "blk", other_core)

    def exchange_chips(x):
        return lax.all_to_all(
            x, "blk", split_axis=0, concat_axis=0, tiled=True, axis_index_groups=same_core
        )

    slots = [send_ids[0, 0, :, 0]]
    other_slots = [swap(slots[0])]

    senone_tiles = state_senone.reshape(-1, LANES)

    def first_rows(part):
        me = lax.axis_index("emit")
        parts = []
        for ahead in range(n_emit):
            piece = lax.dynamic_slice_in_dim(part, ((me + ahead) % n_emit) * utts, utts, 0)
            if ahead:
                piece = lax.ppermute(
                    piece, "emit", [(n, (n + ahead) % n_emit) for n in range(n_emit)]
                )
            parts.append(piece)
        order = [
            functools.reduce(
                lambda kept, ahead: jnp.where((me - n) % n_emit == ahead, parts[ahead], kept),
                range(1, n_emit),
                parts[0],
            )
            for n in range(n_emit)
        ]
        return jnp.concatenate(order, axis=1)

    codes = jnp.concatenate(
        [start_weights.astype(jnp.bfloat16), jnp.zeros((utts, width), jnp.bfloat16)], axis=1
    )
    gathered = lax.all_gather(loglike, "emit", axis=2, tiled=True)
    indices = (core_no, arc_src, arc_weight.astype(jnp.float32))
    tallies = (jnp.zeros((utts, LANES), jnp.float32),) * 2
    for frame_no in range(frames):
        outgoing, zero = pack(
            width, n_chip, core_no, slots[frame_no], other_slots[frame_no], codes, swap(codes)
        )
        if frame_no == 0:
            outgoing, scores, ids = lax.optimization_barrier((outgoing, loglike, send_ids))
            values = own_product(codes, self_trans, outgoing)
            first = first_rows(scores[0])
            ids = ids[1:, 0, :, 0]
            other_ids = swap(ids)
            slots += [ids[n] for n in range(frames - 1)]
            other_slots += [other_ids[n] for n in range(frames - 1)]
            emission, level = emissions(first[None].astype(jnp.float32), senone_tiles)
        if frame_no == 1:
            at = lax.axis_index("emit") * utts + zero[0]
            later = lax.dynamic_slice_in_dim(gathered[1:], at, utts, 1)
            emission, level = emissions(later.astype(jnp.float32), senone_tiles)
        received = exchange_chips(outgoing)
        values, *tallies, codes = step(
            frame_no, frame_no == frames - 1, indices, received, values, emission, level,
            max(frame_no - 1, 0), tallies, (self_trans, entry_trans),
        )

    scaled, log_like, bad = finish(exchange(codes), values, tallies[0])
    return lax.cond(
        bad[0] == 0.0,
        lambda: (scaled, log_like[0, :utts]),
        lambda: normalised_path(
            start_weights, first, later, self_trans, entry_trans, arc_weight, arc_src, send_ids,
            state_senone,
        ),
    )


def solution(mesh):
    in_specs = (
        P(None, None, "emit"),
        P("emit", "blk"),
        P("blk", None, None),
        P("blk", None, None),
        P("blk", None),
        P("blk", None),
        P(None, "blk", None, None),
        P("blk"),
    )
    out_specs = (P("emit", "blk"), P("emit"))
    return jax.shard_map(local, mesh=mesh, in_specs=in_specs, out_specs=out_specs, check_vma=False)
```

```python
import functools

import jax
import jax.numpy as jnp
from jax import lax
from jax.experimental import pallas as pl
from jax.experimental.pallas import tpu as pltpu
from jax.sharding import PartitionSpec as P

LANES = 128
TOP, BIAS, RATIO, TINY = 65535.0, 32768.0, 2.0**-22, 1e-30
META, PEAK_STEPS = 16, 256.0
MEAN_LOW, MEAN_HIGH = 2.0**-4, 4095.0
VMEM_LIMIT = 48 * 2**20


def exchange(outgoing):
    return lax.all_to_all(outgoing, "blk", split_axis=0, concat_axis=0, tiled=True)


def sum_over_blk(part):
    n_blk = lax.axis_size("blk")
    return jnp.sum(exchange(jnp.broadcast_to(part[None], (n_blk,) + part.shape)), axis=0)


def advance(values, matrices):
    return jnp.einsum("juv,jvw->juw", values, matrices, preferred_element_type=jnp.float32)


def normalised_path(
    start, first, later, self_trans, entry_trans, arc_weight, arc_src, send_ids, state_senone
):
    rows = jnp.concatenate([first[None], later], axis=0)
    slots = send_ids[:, 0, :, 0]
    utt_dev, n_blk = start.shape[0], lax.axis_size("blk")
    blk_dev, block_width = self_trans.shape[:2]
    state_count = blk_dev * block_width * n_blk
    senders = lax.broadcasted_iota(jnp.int32, (1, 1, n_blk), 2)
    arc_values = jnp.where(
        (arc_src // blk_dev)[:, :, None] == senders, arc_weight[:, :, None].astype(jnp.float32), 0.0
    )
    mixing = jnp.sum(arc_values, axis=1).astype(jnp.bfloat16)

    def blocks(values):
        return values.reshape(utt_dev, blk_dev, block_width).transpose(1, 0, 2)

    def frame(frame_no, carry):
        forward, log_like = carry
        sent = forward.astype(jnp.bfloat16)
        padded = jnp.concatenate([sent, jnp.zeros_like(sent[:1])], axis=0)
        outgoing = padded.at[slots[frame_no]].get(mode="promise_in_bounds")
        incoming = exchange(outgoing).reshape(n_blk, utt_dev * block_width)
        inflow = jnp.dot(mixing, incoming, preferred_element_type=jnp.float32)
        inflow = inflow.astype(jnp.bfloat16).reshape(blk_dev, utt_dev, block_width)
        raw_mass = advance(sent, self_trans) + advance(inflow, entry_trans)
        scores = rows[frame_no].at[:, state_senone].get(mode="promise_in_bounds")
        raw_mass = raw_mass * jnp.exp(blocks(scores).astype(jnp.float32))
        mass_sum = sum_over_blk(jnp.sum(raw_mass, axis=(0, 2)))
        forward = raw_mass * (state_count / mass_sum)[None, :, None]
        return forward, log_like + jnp.log(mass_sum / state_count)

    log_like = jnp.zeros((utt_dev,), jnp.float32)
    forward, log_like = lax.fori_loop(0, rows.shape[0], frame, (blocks(start), log_like))
    return forward.transpose(1, 0, 2).reshape(start.shape), log_like


def short(values):
    return values.astype(jnp.int32).astype(jnp.int16)


def wide(codes):
    return codes.astype(jnp.int32).astype(jnp.float32)


def encode(blocks, mean, core, out_ref):
    utts, width = blocks[0].shape
    lane = lax.broadcasted_iota(jnp.int32, (utts, LANES), 1) - core * META
    meta = jnp.zeros((utts, LANES), jnp.float32)
    bad = jnp.where((mean >= MEAN_LOW) & (mean <= MEAN_HIGH), 0.0, 1.0)
    for d, block in enumerate(blocks):
        peak = jnp.max(block, axis=1, keepdims=True)
        least = jnp.min(block, axis=1, keepdims=True)
        bad = jnp.where((least >= peak * RATIO) & (least >= TINY), bad, 1.0)
        steps = jnp.ceil(jnp.log2(peak) * PEAK_STEPS)
        share = block * jnp.exp2(steps * (-1.0 / PEAK_STEPS))
        root = jnp.exp2(jnp.log2(share) * (1.0 / 3.0))
        code = jnp.clip(jnp.round(root * TOP), 0.0, TOP) - BIAS
        out_ref[:, d * width : (d + 1) * width] = short(code)
        meta = jnp.where(lane == d, steps, meta)
    n = len(blocks)
    out_ref[:, n * width : (n + 1) * width] = short(jnp.full((utts, width), -BIAS, jnp.float32))
    rest = mean * 8.0
    for digit in range(3):
        whole = jnp.floor(rest)
        meta = jnp.where(lane == n + digit, whole, meta)
        rest = (rest - whole) * 2.0**15
    out_ref[:, (n + 1) * width :] = short(meta)
    return jnp.broadcast_to(bad, (utts, LANES))


def pack_kernel(width, core_ref, mine_ref, others_ref, own_ref, other_ref, out_ref, *zero_ref):
    core = core_ref[0]
    if zero_ref:
        zero_ref[0][0] = 0
    mine_at = pl.multiple_of(core * width, width)
    others_at = pl.multiple_of((1 - core) * width, width)
    with_meta = out_ref.shape[2] > 2 * width
    if with_meta:
        last = slice(own_ref.shape[1] - LANES, own_ref.shape[1])
        meta = short(wide(own_ref[:, last]) + wide(other_ref[:, last]))
    for chip in range(out_ref.shape[0]):
        mine = pl.multiple_of(mine_ref[2 * chip + core] * width, width)
        others = pl.multiple_of(others_ref[2 * chip + core] * width, width)
        out_ref[chip, :, pl.ds(mine_at, width)] = own_ref[:, pl.ds(mine, width)]
        out_ref[chip, :, pl.ds(others_at, width)] = other_ref[:, pl.ds(others, width)]
        if with_meta:
            out_ref[chip, :, 2 * width :] = meta


def pack(width, n_chip, with_zero, core, mine, others, own, other):
    smem = pl.BlockSpec(memory_space=pltpu.SMEM)
    vmem = pl.BlockSpec(memory_space=pltpu.VMEM)
    return pl.pallas_call(
        functools.partial(pack_kernel, width),
        out_shape=[
            jax.ShapeDtypeStruct(
                (n_chip, own.shape[0], 2 * width + own.shape[1] % width), own.dtype
            ),
            jax.ShapeDtypeStruct((1,), jnp.int32),
        ][: 1 + with_zero],
        in_specs=[smem] * 3 + [vmem] * 2,
        out_specs=[vmem, smem][: 1 + with_zero],
        compiler_params=pltpu.CompilerParams(vmem_limit_bytes=VMEM_LIMIT),
        name="pack",
    )(core, mine, others, own, other)


def emission_kernel(rows_ref, senone_ref, emission_ref, level_ref):
    frames, utts, senones = rows_ref.shape
    tiles = senones // LANES
    levels = []
    for frame in range(frames):
        rows = rows_ref[frame]
        top = jnp.max(rows, axis=1, keepdims=True)
        mean = jnp.sum(jnp.exp(rows - top), axis=1, keepdims=True) * (1.0 / senones)
        levels.append(top + jnp.log(mean))
        level_ref[frame] = jnp.broadcast_to(levels[-1], (utts, LANES))

    def packed(pair, n):
        at = slice(n * LANES, (n + 1) * LANES)
        low = rows_ref[2 * pair, :, at] * -16.0
        if 2 * pair + 1 < frames:
            low += rows_ref[2 * pair + 1, :, at] * -32768.0
        return low

    pairs = (frames + 1) // 2

    def group(state_group, _):
        senone = jnp.broadcast_to(senone_ref[pl.ds(state_group, 1), :], (utts, LANES))
        lane = senone & (LANES - 1)
        tile = senone >> 7
        found = [jnp.zeros((utts, LANES), jnp.float32)] * pairs
        for n in range(tiles):
            here = tile == n
            for pair in range(pairs):
                picked = jnp.take_along_axis(
                    packed(pair, n), lane, axis=1, mode="promise_in_bounds"
                )
                found[pair] = jnp.where(here, picked, found[pair])
        at = pl.multiple_of(state_group * LANES, LANES)
        for pair in range(pairs):
            high = jnp.floor(found[pair] * (1.0 / 2048.0))
            both = (found[pair] - high * 2048.0, high)
            for frame in range(2 * pair, min(2 * pair + 2, frames)):
                score = both[frame - 2 * pair] * (-1.0 / 16.0)
                emission_ref[frame, :, pl.ds(at, LANES)] = jnp.exp(score - levels[frame])
        return 0

    lax.fori_loop(0, senone_ref.shape[0], group, 0)


def emissions(rows, senone_tiles):
    frames, utts, senones = rows.shape
    groups = senone_tiles.shape[0]
    return pl.pallas_call(
        emission_kernel,
        out_shape=(
            jax.ShapeDtypeStruct((frames, utts, groups * LANES), jnp.float32),
            jax.ShapeDtypeStruct((frames, utts, LANES), jnp.float32),
        ),
        compiler_params=pltpu.CompilerParams(vmem_limit_bytes=VMEM_LIMIT),
        cost_estimate=pl.CostEstimate(
            flops=8 * frames * groups * senones * utts, bytes_accessed=2**20,
            transcendentals=frames * groups * utts * LANES,
        ),
        name="emissions",
    )(rows, senone_tiles)


def column_to_row(column):
    n = column.shape[0]
    lane = lax.broadcasted_iota(jnp.int32, (n, LANES), 1)
    place = lax.broadcasted_iota(jnp.int32, (n, LANES), 0)
    return jnp.sum(jnp.where(lane == place, column, 0.0), axis=0, keepdims=True)


def row_to_column(row, n):
    lane = lax.broadcasted_iota(jnp.int32, (n, LANES), 1)
    place = lax.broadcasted_iota(jnp.int32, (n, LANES), 0)
    return jnp.sum(jnp.where(lane == place, row, 0.0), axis=1, keepdims=True)


def step_kernel(
    first, last, streamed, slot, core_ref, arc_ref, weight_ref, recv_ref, prev_ref, emission_ref,
    level_ref, log_in_ref, bad_in_ref, self_in, entry_in, raw_ref, log_ref, bad_ref,
    end_ref, *scratch,
):
    n_chip, utts = recv_ref.shape[:2]
    blk_dev, width = self_in.shape[:2]
    arcs = arc_ref.shape[1]
    bits = blk_dev.bit_length() - 1
    lane = lax.broadcasted_iota(jnp.int32, (utts, LANES), 1)
    self_ref, entry_ref, copies = self_in, entry_in, []
    if streamed:
        self_ref, entry_ref, arrived = scratch
        for d in range(blk_dev):
            pairs = [(entry_in, entry_ref)] if first else [(self_in, self_ref), (entry_in, entry_ref)]
            copies.append(
                [
                    pltpu.make_async_copy(src.at[d], dst.at[d], arrived.at[2 * d + n])
                    for n, (src, dst) in enumerate(pairs)
                ]
            )
            for copy in copies[d]:
                copy.start()
    log_like = log_in_ref[...] + level_ref[slot]
    if first:
        scale = jnp.ones((utts, 1), jnp.float32)
    else:
        sums = wide(recv_ref[0, :, 2 * width :])
        for chip in range(1, n_chip):
            sums += wide(recv_ref[chip, :, 2 * width :])
        digit = lane % META - blk_dev
        place = jnp.where(
            digit == 0,
            2.0**-3,
            jnp.where(digit == 1, 2.0**-18, jnp.where(digit == 2, 2.0**-33, 0.0)),
        )
        scale = (2.0 * n_chip) / jnp.sum(sums * place, axis=1, keepdims=True)
        log_like = log_like - jnp.log(scale)
    log_ref[...] = log_like
    narrow = jnp.broadcast_to(scale, (utts, LANES)) * TOP**-3
    scale = jnp.broadcast_to(scale, (utts, width))

    def inflow_of(d):
        inflow = jnp.zeros((utts, width), jnp.float32)
        for a in range(arcs):
            source = arc_ref[d, a]
            chip, side, block = source >> (bits + 1), (source >> bits) & 1, source & (blk_dev - 1)
            code = recv_ref[chip, :, pl.ds(pl.multiple_of(side * width, width), width)]
            if first:
                inflow += code.astype(jnp.float32) * weight_ref[d, a]
                continue
            code = wide(code) + BIAS
            meta = wide(recv_ref[chip, :, 2 * width :])
            at = jnp.full((utts, LANES), side * META + block, jnp.int32)
            steps = jnp.take_along_axis(meta, at, axis=1, mode="promise_in_bounds")
            unit = jnp.exp2(steps * (1.0 / PEAK_STEPS)) * narrow
            unit = jnp.concatenate([unit] * (width // LANES), axis=1)
            sent = (code * unit * code * code).astype(jnp.bfloat16).astype(jnp.float32)
            inflow += sent * weight_ref[d, a]
        return inflow.astype(jnp.bfloat16)

    blocks = []
    total = jnp.zeros((utts, width), jnp.float32)
    inflow = inflow_of(0)
    for d in range(blk_dev):
        here = slice(d * width, (d + 1) * width)
        if streamed:
            for copy in copies[d]:
                copy.wait()
        if first:
            raw = prev_ref[:, here]
        else:
            own = (prev_ref[:, here] * scale).astype(jnp.bfloat16)
            raw = jnp.dot(own, self_ref[d], preferred_element_type=jnp.float32)
        after = inflow_of(d + 1) if d + 1 < blk_dev else None
        raw += jnp.dot(inflow, entry_ref[d], preferred_element_type=jnp.float32)
        raw = raw * emission_ref[slot, :, here]
        raw_ref[:, here] = raw
        total += raw
        blocks.append(raw)
        inflow = after
    mean = jnp.sum(total, axis=1, keepdims=True) * (1.0 / (blk_dev * width))
    if last:
        bad_ref[...] = bad_in_ref[...]
        row = column_to_row(mean)
        bad = jnp.max(bad_in_ref[...], axis=0, keepdims=True)
        row = jnp.where(lane[:1] == utts, bad, row)
        end_ref[...] = jnp.broadcast_to(row, end_ref.shape)
    else:
        bad_ref[...] = jnp.maximum(bad_in_ref[...], encode(blocks, mean, core_ref[0], end_ref))


def step(frame_no, last, indices, received, previous, emission, level, slot, tallies, matrices):
    blk_dev, width = matrices[0].shape[:2]
    n_chip = received.shape[0]
    utts, states = previous.shape
    streamed = frame_no < 2
    smem = pl.BlockSpec(memory_space=pltpu.SMEM)
    vmem = pl.BlockSpec(memory_space=pltpu.VMEM)
    matrix = pl.BlockSpec(memory_space=pl.ANY) if streamed else vmem
    end = (2 * n_chip, LANES) if last else (utts, states + width + LANES)
    tile = jax.ShapeDtypeStruct((utts, LANES), jnp.float32)
    scratch = []
    if streamed:
        scratch = [pltpu.VMEM(m.shape, m.dtype) for m in matrices]
        scratch.append(pltpu.SemaphoreType.DMA((2 * blk_dev,)))
    return pl.pallas_call(
        functools.partial(step_kernel, frame_no == 0, last, streamed, slot),
        out_shape=[
            jax.ShapeDtypeStruct((utts, states), jnp.float32),
            tile,
            tile,
            jax.ShapeDtypeStruct(end, jnp.float32 if last else jnp.int16),
        ],
        in_specs=[smem] * 3 + [vmem] * 6 + [matrix] * 2,
        out_specs=[vmem] * 4,
        scratch_shapes=scratch,
        compiler_params=pltpu.CompilerParams(vmem_limit_bytes=VMEM_LIMIT),
        cost_estimate=pl.CostEstimate(
            flops=4 * utts * blk_dev * width**2, bytes_accessed=4 * blk_dev * width**2,
            transcendentals=0,
        ),
        name="step",
    )(*indices, received, previous, emission, level, *tallies, *matrices)


def own_kernel(start_ref, self_in, after_ref, out_ref, self_ref, arrived):
    del after_ref
    blk_dev, width = self_ref.shape[:2]
    copies = [
        pltpu.make_async_copy(self_in.at[d], self_ref.at[d], arrived.at[d]) for d in range(blk_dev)
    ]
    for copy in copies:
        copy.start()
    for d in range(blk_dev):
        here = slice(d * width, (d + 1) * width)
        copies[d].wait()
        out_ref[:, here] = jnp.dot(
            start_ref[:, here], self_ref[d], preferred_element_type=jnp.float32
        )


def own_product(start, self_trans, after):
    blk_dev, width = self_trans.shape[:2]
    utts = start.shape[0]
    vmem = pl.BlockSpec(memory_space=pltpu.VMEM)
    anywhere = pl.BlockSpec(memory_space=pl.ANY)
    return pl.pallas_call(
        own_kernel,
        out_shape=jax.ShapeDtypeStruct((utts, blk_dev * width), jnp.float32),
        in_specs=[vmem, anywhere, anywhere],
        out_specs=vmem,
        scratch_shapes=[
            pltpu.VMEM(self_trans.shape, self_trans.dtype),
            pltpu.SemaphoreType.DMA((blk_dev,)),
        ],
        compiler_params=pltpu.CompilerParams(vmem_limit_bytes=VMEM_LIMIT),
        cost_estimate=pl.CostEstimate(
            flops=2 * utts * blk_dev * width**2, bytes_accessed=2 * blk_dev * width**2,
            transcendentals=0,
        ),
        name="own",
    )(start, self_trans, after)


def finish_kernel(recv_ref, raw_ref, log_ref, out_ref, log_row_ref, bad_ref):
    utts = raw_ref.shape[0]
    sums = jnp.sum(recv_ref[...], axis=0, keepdims=True)
    mean = row_to_column(sums, utts) * (1.0 / recv_ref.shape[0])
    out_ref[...] = raw_ref[...] * (1.0 / mean)
    log_row_ref[...] = column_to_row((log_ref[...] + jnp.log(mean))[:, :1])
    lane = lax.broadcasted_iota(jnp.int32, (1, LANES), 1)
    bad_ref[0] = jnp.sum(jnp.where(lane == utts, sums, 0.0))


def finish(received, raw, log_like):
    vmem = pl.BlockSpec(memory_space=pltpu.VMEM)
    return pl.pallas_call(
        finish_kernel,
        out_shape=[
            jax.ShapeDtypeStruct(raw.shape, jnp.float32),
            jax.ShapeDtypeStruct((1, LANES), jnp.float32),
            jax.ShapeDtypeStruct((1,), jnp.float32),
        ],
        in_specs=[vmem] * 3,
        out_specs=[vmem, vmem, pl.BlockSpec(memory_space=pltpu.SMEM)],
        compiler_params=pltpu.CompilerParams(vmem_limit_bytes=VMEM_LIMIT),
        name="finish",
    )(received, raw, log_like)


def local(
    loglike, start_weights, self_trans, entry_trans, arc_weight, arc_src, send_ids, state_senone
):
    n_blk = lax.axis_size("blk")
    n_chip = n_blk // 2
    n_emit = lax.axis_size("emit")
    blk_dev, width = self_trans.shape[:2]
    utts = start_weights.shape[0]
    frames = loglike.shape[0]
    core = lax.axis_index("blk") % 2
    core_no = core.astype(jnp.int32).reshape(1)

    other_core = [(n, n ^ 1) for n in range(n_blk)]
    same_core = [[2 * n + c for n in range(n_chip)] for c in range(2)]

    def swap(x):
        return lax.ppermute(x, "blk", other_core)

    def exchange_chips(x):
        return lax.all_to_all(
            x, "blk", split_axis=0, concat_axis=0, tiled=True, axis_index_groups=same_core
        )

    slots = [send_ids[0, 0, :, 0]]
    other_slots = [swap(slots[0])]

    senone_tiles = state_senone.reshape(-1, LANES)

    def first_rows(part):
        me = lax.axis_index("emit")
        parts = []
        for ahead in range(n_emit):
            piece = lax.dynamic_slice_in_dim(part, ((me + ahead) % n_emit) * utts, utts, 0)
            if ahead:
                piece = lax.ppermute(
                    piece, "emit", [(n, (n + ahead) % n_emit) for n in range(n_emit)]
                )
            parts.append(piece)
        order = [
            functools.reduce(
                lambda kept, ahead: jnp.where((me - n) % n_emit == ahead, parts[ahead], kept),
                range(1, n_emit),
                parts[0],
            )
            for n in range(n_emit)
        ]
        return jnp.concatenate(order, axis=1)

    codes = jnp.concatenate(
        [start_weights.astype(jnp.bfloat16), jnp.zeros((utts, width), jnp.bfloat16)], axis=1
    )
    gathered = lax.all_gather(loglike, "emit", axis=2, tiled=True)
    indices = (core_no, arc_src, arc_weight.astype(jnp.float32))
    tallies = (jnp.zeros((utts, LANES), jnp.float32),) * 2
    for frame_no in range(frames):
        outgoing, *zero = pack(
            width, n_chip, frame_no == 1, core_no, slots[frame_no], other_slots[frame_no], codes, swap(codes)
        )
        if frame_no == 0:
            outgoing, scores, ids = lax.optimization_barrier((outgoing, loglike, send_ids))
            values = own_product(codes, self_trans, outgoing)
            first = first_rows(scores[0])
            ids = ids[1:, 0, :, 0]
            other_ids = swap(ids)
            slots += [ids[n] for n in range(frames - 1)]
            other_slots += [other_ids[n] for n in range(frames - 1)]
            emission, level = emissions(first[None].astype(jnp.float32), senone_tiles)
        if frame_no == 1:
            at = lax.axis_index("emit") * utts + zero[0][0]
            later = lax.dynamic_slice_in_dim(gathered[1:], at, utts, 1)
            emission, level = emissions(later.astype(jnp.float32), senone_tiles)
        received = exchange_chips(outgoing)
        values, *tallies, codes = step(
            frame_no, frame_no == frames - 1, indices, received, values, emission, level,
            max(frame_no - 1, 0), tallies, (self_trans, entry_trans),
        )

    scaled, log_like, bad = finish(exchange(codes), values, tallies[0])
    return lax.cond(
        bad[0] == 0.0,
        lambda: (scaled, log_like[0, :utts]),
        lambda: normalised_path(
            start_weights, first, later, self_trans, entry_trans, arc_weight, arc_src, send_ids,
            state_senone,
        ),
    )


def solution(mesh):
    in_specs = (
        P(None, None, "emit"),
        P("emit", "blk"),
        P("blk", None, None),
        P("blk", None, None),
        P("blk", None),
        P("blk", None),
        P(None, "blk", None, None),
        P("blk"),
    )
    out_specs = (P("emit", "blk"), P("emit"))
    return jax.shard_map(local, mesh=mesh, in_specs=in_specs, out_specs=out_specs, check_vma=False)
```
